32 devices in a mesh: fsdp: 8 (over y, x, core), tp: 4 (over z).
Axes of the slice: x: 2, y: 2, z: 4, core: 2. Of those that a mesh axis runs over, the one named last changes fastest.
Arguments:
- tokens: bfloat16 [8192, 2048], P(('fsdp', 'tp')), may hold values from -6 to 6
- segment_ids: int32 [8, 1024], P('fsdp'), may hold values from 0 to 3, never falling along the last dimension, each value on 1 to 800 neighbouring positions
- attn_gain: float32 [2, 2048], replicated, may hold values from 0.25 to 1.75
- query_gain: float32 [2, 128], replicated, may hold values from 0.25 to 1.75
- key_gain: float32 [2, 128], replicated, may hold values from 0.25 to 1.75
- query_weight: bfloat16 [2, 2048, 2048], P(None, 'fsdp', 'tp'), may hold values from -0.125 to 0.125
- key_matrix: bfloat16 [2, 2048, 1024], P(None, 'fsdp', 'tp'), may hold values from -0.125 to 0.125
- value_matrix: bfloat16 [2, 2048, 1024], P(None, 'fsdp', 'tp'), may hold values from -0.125 to 0.125
- out_weight: bfloat16 [2, 2048, 2048], P(None, 'tp', 'fsdp'), may hold values from -1 to 1
- mlp_gain: float32 [2, 2048], replicated, may hold values from 0.25 to 1.75
- gate_weight: bfloat16 [2, 2048, 6144], P(None, 'fsdp', 'tp'), may hold values from -0.125 to 0.125
- up_weight: bfloat16 [2, 2048, 6144], P(None, 'fsdp', 'tp'), may hold values from -0.125 to 0.125
- down_weight: bfloat16 [2, 6144, 2048], P(None, 'tp', 'fsdp'), may hold values from -0.078125 to 0.078125
- cotangent: bfloat16 [8192, 2048], P(('fsdp', 'tp')), may hold values from -6 to 6
Outputs:
- result: bfloat16 [8192, 2048], P(('fsdp', 'tp'))
- grad_tokens: float32 [8192, 2048], P(('fsdp', 'tp'))
- grad_attn_gain: float32 [2, 2048], replicated
- grad_query_gain: float32 [2, 128], replicated
- grad_key_gain: float32 [2, 128], replicated
- grad_query_weight: float32 [2, 2048, 2048], P(None, 'fsdp', 'tp')
- grad_key_weight: float32 [2, 2048, 1024], P(None, 'fsdp', 'tp')
- grad_value_weight: float32 [2, 2048, 1024], P(None, 'fsdp', 'tp')
- grad_out_weight: float32 [2, 2048, 2048], P(None, 'tp', 'fsdp')
- grad_mlp_gain: float32 [2, 2048], replicated
- grad_gate_weight: float32 [2, 2048, 6144], P(None, 'fsdp', 'tp')
- grad_up_weight: float32 [2, 2048, 6144], P(None, 'fsdp', 'tp')
- grad_down_weight: float32 [2, 6144, 2048], P(None, 'tp', 'fsdp')
The draws below stay inside these ranges and needn't reach their ends.
Inputs may be any that keep to these rules, and one draw needn't show every extreme that they name: `segment_ids`: along each sequence the ids never fall; a document (a run of equal ids) has at most 800 tokens, and in each sequence one document has exactly 800.
All inputs are finite; a program needn't handle non-finite values.
Results may differ from the reference program's by a relative error of at most 0.03.
Values may be sent and summed in bfloat16 or wider, within the bound.
No kernel may reach another device: no remote copies, remote signals or barrier semaphores. Data moves between devices by JAX's collectives and lax.ppermute only.
A program may use at most 320 MiB of HBM per device.

```python
import math
import jax
import jax.numpy as jnp
import numpy as np
from jax import lax

MODEL_WIDTH = 2048
HEAD_WIDTH = 128
QUERY_HEADS = 16
KEY_VALUE_HEADS = 8
FF = 6144
SEQ = 1024
DECODER_LAYERS = 2
SEQS = 8
TOKENS = 8192
DOCS = 4
DOC_MOST = 800


def steps_of(key, shape, split, least, largest):
    factor_of, own = 1.0, jax.random.fold_in(key, 6)
    for position, shards_of in split:
        heights = jnp.exp(jax.random.uniform(jax.random.fold_in(own, position), (shards_of,), jnp.float32, least / len(split), largest / len(split)))
        factor_of = factor_of * jnp.repeat(heights, shape[position] // shards_of).reshape([-1 if axis == position else 1 for axis in range(len(shape))])
    return factor_of


def profile(count, total, reach, slope):
    portions = [(1 << 20) // math.isqrt(rank ** slope) + 1 for rank in range(2, count + 1)]
    surplus, holding = total - reach - (count - 1), [1] * (count - 1)
    while surplus > 0:
        movable = [i for i in range(count - 1) if holding[i] < reach]
        pool, budget = sum([portions[i] for i in movable]), surplus
        for i in movable:
            extra = min(reach - holding[i], max(1, budget * portions[i] // pool), surplus)
            holding[i] = holding[i] + extra
            surplus = surplus - extra
    return np.array([reach] + holding)


def uneven(rng, count, total, limit, slope):
    if count == 2:
        one = jax.random.randint(rng, (), max(1, total - limit), min(limit, total - 1) + 1)
        return jnp.stack([one, total - one])
    lengths = jnp.asarray(profile(count, total, limit, slope), jnp.int32)
    twos = (count - 1) // 2
    source_of, sink = lengths[1:1 + 2 * twos:2], lengths[2:2 + 2 * twos:2]
    margin = jnp.minimum(source_of - 1, limit - sink)
    shifted = jax.random.randint(jax.random.fold_in(rng, 1), (twos,), 0, 1 << 20) % (margin + 1)
    lengths = lengths.at[1:1 + 2 * twos:2].set(source_of - shifted).at[2:2 + 2 * twos:2].set(sink + shifted)
    return lengths[jax.random.permutation(jax.random.fold_in(rng, 2), count)]


def gaussian(rng, extent, width, reach, pieces=(), kind=jnp.bfloat16):
    factor_of = steps_of(rng, extent, pieces, -0.22, 0.18) if pieces else 1.0
    entries = jax.random.normal(rng, extent, jnp.float32) * width * factor_of
    return jnp.minimum(jnp.maximum(entries, -reach), reach).astype(kind)


def setup_inputs(seed: int = 0) -> dict:
    arg_keys = jax.random.split(jax.random.key(seed), 15)
    return {
        "tokens": gaussian(arg_keys[0], (TOKENS, MODEL_WIDTH), 1.0, 6.0, ((0, 32),)),
        "segment_ids": jax.vmap(lambda own: jnp.searchsorted(jnp.cumsum(uneven(own, DOCS, SEQ, DOC_MOST, 2)), jnp.arange(SEQ), side="right"))(jax.random.split(arg_keys[1], SEQS)).reshape((SEQS, SEQ)).astype(jnp.int32),
        "attn_gain": jnp.clip(1.0 + 0.15 * jax.random.normal(arg_keys[2], (DECODER_LAYERS, MODEL_WIDTH), jnp.float32), 0.25, 1.75),
        "query_gain": jnp.clip(1.0 + 0.15 * jax.random.normal(arg_keys[3], (DECODER_LAYERS, HEAD_WIDTH), jnp.float32), 0.25, 1.75),
        "key_gain": jnp.clip(1.0 + 0.15 * jax.random.normal(arg_keys[4], (DECODER_LAYERS, HEAD_WIDTH), jnp.float32), 0.25, 1.75),
        "query_weight": gaussian(arg_keys[5], (DECODER_LAYERS, MODEL_WIDTH, QUERY_HEADS * HEAD_WIDTH), MODEL_WIDTH ** -0.5, 0.125, ((1, 8), (2, 4))),
        "key_matrix": gaussian(arg_keys[6], (DECODER_LAYERS, MODEL_WIDTH, KEY_VALUE_HEADS * HEAD_WIDTH), MODEL_WIDTH ** -0.5, 0.125, ((1, 8), (2, 4))),
        "value_matrix": gaussian(arg_keys[7], (DECODER_LAYERS, MODEL_WIDTH, KEY_VALUE_HEADS * HEAD_WIDTH), MODEL_WIDTH ** -0.5, 0.125, ((1, 8), (2, 4))),
        "out_weight": gaussian(arg_keys[8], (DECODER_LAYERS, QUERY_HEADS * HEAD_WIDTH, MODEL_WIDTH), (QUERY_HEADS * HEAD_WIDTH // 64) ** -0.5, 1.0, ((1, 4), (2, 8))),
        "mlp_gain": jnp.clip(1.0 + 0.15 * jax.random.normal(arg_keys[9], (DECODER_LAYERS, MODEL_WIDTH), jnp.float32), 0.25, 1.75),
        "gate_weight": gaussian(arg_keys[10], (DECODER_LAYERS, MODEL_WIDTH, FF), MODEL_WIDTH ** -0.5, 0.125, ((1, 8), (2, 4))),
        "up_weight": gaussian(arg_keys[11], (DECODER_LAYERS, MODEL_WIDTH, FF), MODEL_WIDTH ** -0.5, 0.125, ((1, 8), (2, 4))),
        "down_weight": gaussian(arg_keys[12], (DECODER_LAYERS, FF, MODEL_WIDTH), FF ** -0.5, 0.078125, ((1, 4), (2, 8))),
        "cotangent": gaussian(arg_keys[13], (TOKENS, MODEL_WIDTH), 1.0, 6.0, ((0, 32),)),
    }


EPSILON = 1e-06
ROPE_BASE = 1000000.0
HIGHEST = lax.Precision.HIGHEST

@jax.custom_vjp
def reduced_precision(v):
    return lax.optimization_barrier(v.astype(jnp.bfloat16)).astype(jnp.float32)

@jax.custom_vjp
def reduced_precision_backward(v):
    return v

def low_keep(v):
    return (reduced_precision(v), None)

def low_pass(kept, grad):
    return (grad,)

def back_keep(v):
    return (v, None)

def back_low(kept, grad):
    return (reduced_precision(grad),)
reduced_precision.defvjp(low_keep, low_pass)
reduced_precision_backward.defvjp(back_keep, back_low)

def matrix_multiply(left_side, right_side):
    return jnp.dot(left_side, right_side, precision=HIGHEST, preferred_element_type=jnp.float32)

def rms_scale(values, gain_row):
    return values * lax.rsqrt(lax.optimization_barrier(jnp.mean(values * values, axis=-1, keepdims=True)) + EPSILON) * gain_row

def positions_of(segment_row):
    sequence_length = segment_row.shape[0]
    position_index = jnp.arange(sequence_length, dtype=jnp.int32)
    starts = jnp.concatenate([jnp.ones((1,), dtype=jnp.bool_), segment_row[1:] != segment_row[:-1]])
    first_index = lax.cummax(jnp.where(starts, position_index, jnp.zeros_like(position_index)), axis=0)
    return position_index - first_index

def rope_tables(positions, head_size):
    half_size = head_size // 2
    steps_float = jnp.arange(half_size, dtype=jnp.float32)
    inverse = jnp.exp(steps_float * (-2.0 * math.log(ROPE_BASE) / head_size))
    angles = positions.astype(jnp.float32)[:, None] * inverse[None, :]
    angles = jnp.concatenate([angles, angles], axis=-1)
    return (jnp.cos(angles), jnp.sin(angles))

def rotate(values, cosine_table, sine_table):
    half_size = values.shape[-1] // 2
    turned = jnp.concatenate([-values[..., half_size:], values[..., :half_size]], axis=-1)
    return values * cosine_table[:, None, :] + turned * sine_table[:, None, :]

def attention(heads_of_query, heads_of_key, heads_of_value, segment_row):
    sequence_length = heads_of_query.shape[0]
    rows_per_block = min(512, sequence_length)
    number_blocks = sequence_length // rows_per_block
    group_width = QUERY_HEADS // KEY_VALUE_HEADS
    score_scale = HEAD_WIDTH ** (-0.5)
    position_index = jnp.arange(sequence_length, dtype=jnp.int32)
    blocks_of_query = heads_of_query.reshape(number_blocks, rows_per_block, KEY_VALUE_HEADS, group_width, HEAD_WIDTH)
    row_index = position_index.reshape(number_blocks, rows_per_block)
    row_segment = segment_row.reshape(number_blocks, rows_per_block)

    def one_block(inputs):
        query_block, block_index, block_segment = inputs
        raw_dots = jnp.einsum('qngd,knd->ngqk', query_block, heads_of_key, precision=HIGHEST)
        scores = reduced_precision_backward(raw_dots * score_scale)
        allowed = (position_index[None, :] <= block_index[:, None]) & (segment_row[None, :] == block_segment[:, None])
        scores = jnp.where(allowed[None, None], scores, -1e+30)
        top_score = lax.optimization_barrier(jnp.max(scores, axis=-1, keepdims=True))
        weights = jnp.exp(scores - top_score)
        prob_block = weights / lax.optimization_barrier(jnp.sum(weights, axis=-1, keepdims=True))
        return jnp.einsum('ngqk,knd->qngd', reduced_precision(prob_block), heads_of_value, precision=HIGHEST)
    outputs = lax.map(jax.checkpoint(one_block), (blocks_of_query, row_index, row_segment))
    return outputs.reshape(sequence_length, QUERY_HEADS * HEAD_WIDTH)

def apply_layer(residual, weights, cosine_table, sine_table, segment_row):
    attn_gain, query_gain, key_gain, query_weight, key_matrix, value_matrix, out_weight, mlp_gain, gate_weight, up_weight, down_weight = weights
    sequence_length = residual.shape[0]
    normalized_rows = reduced_precision(rms_scale(residual, attn_gain))
    heads_of_query = reduced_precision_backward(matrix_multiply(normalized_rows, query_weight)).reshape(sequence_length, QUERY_HEADS, HEAD_WIDTH)
    heads_of_key = reduced_precision_backward(matrix_multiply(normalized_rows, key_matrix)).reshape(sequence_length, KEY_VALUE_HEADS, HEAD_WIDTH)
    heads_of_value = reduced_precision(reduced_precision_backward(matrix_multiply(normalized_rows, value_matrix))).reshape(sequence_length, KEY_VALUE_HEADS, HEAD_WIDTH)
    heads_of_query = reduced_precision(rotate(rms_scale(heads_of_query, query_gain), cosine_table, sine_table))
    heads_of_key = reduced_precision(rotate(rms_scale(heads_of_key, key_gain), cosine_table, sine_table))
    attn_mixed = reduced_precision(reduced_precision_backward(attention(heads_of_query, heads_of_key, heads_of_value, segment_row)))
    residual = residual + reduced_precision_backward(matrix_multiply(attn_mixed, out_weight))
    normalized_rows = reduced_precision(rms_scale(residual, mlp_gain))
    gate_proj = reduced_precision_backward(matrix_multiply(normalized_rows, gate_weight))
    upward = reduced_precision_backward(matrix_multiply(normalized_rows, up_weight))
    hidden = reduced_precision(jax.nn.silu(gate_proj) * upward)
    return residual + reduced_precision_backward(matrix_multiply(hidden, down_weight))

def forward(residual, segment_row, weights):
    cosine_table, sine_table = rope_tables(positions_of(segment_row), HEAD_WIDTH)
    for layer_index in range(DECODER_LAYERS):
        residual = apply_layer(residual, [weight_item[layer_index] for weight_item in weights], cosine_table, sine_table, segment_row)
    return residual

def reference(tokens, segment_ids, attn_gain, query_gain, key_gain, query_weight, key_matrix, value_matrix, out_weight, mlp_gain, gate_weight, up_weight, down_weight, cotangent):
    weights = tuple((weight_item.astype(jnp.float32) for weight_item in (attn_gain, query_gain, key_gain, query_weight, key_matrix, value_matrix, out_weight, mlp_gain, gate_weight, up_weight, down_weight)))
    token_rows = tokens.astype(jnp.float32).reshape(SEQS, SEQ, MODEL_WIDTH)
    cotangent_rows = cotangent.astype(jnp.float32).reshape(SEQS, SEQ, MODEL_WIDTH)

    def one_sequence(totals, inputs):
        sequence_rows, segment_row, sequence_grad = inputs

        def apply_all(rows_in, *params):
            return forward(rows_in, segment_row, params)
        outputs, back_fn = jax.vjp(apply_all, sequence_rows, *weights)
        grad_list = back_fn(sequence_grad)
        totals = tuple((total_item + grad_item for total_item, grad_item in zip(totals, grad_list[1:])))
        return (totals, (outputs.astype(jnp.bfloat16), grad_list[0]))
    zero_totals = tuple((jnp.zeros_like(weight_item) for weight_item in weights))
    totals, (outputs, input_grads) = lax.scan(one_sequence, zero_totals, (token_rows, segment_ids, cotangent_rows))
    return (outputs.reshape(TOKENS, MODEL_WIDTH), input_grads.reshape(TOKENS, MODEL_WIDTH), totals[0], totals[1], totals[2], totals[3], totals[4], totals[5], totals[6], totals[7], totals[8], totals[9], totals[10])
```

```python
import functools
import math

import jax
import jax.numpy as jnp
from jax import lax
from jax.experimental import pallas as pl
from jax.experimental.pallas import tpu as pltpu
from jax.sharding import PartitionSpec as P

EPSILON = 1e-06
ROPE_BASE = 1000000.0


def rms_scale(values, gain_row):
    return (
        values * lax.rsqrt(jnp.mean(values * values, axis=-1, keepdims=True) + EPSILON) * gain_row
    )


def positions_of(segment_row):
    sequence_length = segment_row.shape[0]
    position_index = jnp.arange(sequence_length, dtype=jnp.int32)
    starts = jnp.concatenate([jnp.ones((1,), dtype=jnp.bool_), segment_row[1:] != segment_row[:-1]])
    first_index = lax.cummax(
        jnp.where(starts, position_index, jnp.zeros_like(position_index)), axis=0
    )
    return position_index - first_index


def rope_tables(positions, head_size):
    half_size = head_size // 2
    steps_float = jnp.arange(half_size, dtype=jnp.float32)
    inverse = jnp.exp(steps_float * (-2.0 * math.log(ROPE_BASE) / head_size))
    angles = positions.astype(jnp.float32)[:, None] * inverse[None, :]
    angles = jnp.concatenate([angles, angles], axis=-1)
    return (jnp.cos(angles), jnp.sin(angles))


def rotate(values, cosine_table, sine_table):
    half_size = values.shape[-1] // 2
    turned = jnp.concatenate([-values[..., half_size:], values[..., :half_size]], axis=-1)
    return values * cosine_table[:, None, :] + turned * sine_table[:, None, :]


def head_norm(raw_rows, gain_row, cosine_table, sine_table):
    head_size = gain_row.shape[-1]
    shaped = raw_rows.reshape(raw_rows.shape[0], raw_rows.shape[1] // head_size, head_size)
    return rotate(rms_scale(shaped, gain_row), cosine_table, sine_table)


def swiglu(gate_proj, upward):
    return jax.nn.silu(gate_proj) * upward


def contract_rows(left_side, right_side):
    return lax.dot_general(
        left_side, right_side, (((0,), (0,)), ((), ())), preferred_element_type=jnp.float32
    )


def contract_cols(left_side, right_side):
    return lax.dot_general(
        left_side, right_side, (((1,), (1,)), ((), ())), preferred_element_type=jnp.float32
    )


def spread_rows(rows_low):
    return lax.all_gather(rows_low, "tp", axis=0, tiled=True)


def spread_grads(grad_low):
    return lax.all_gather(grad_low, "tp", axis=0, tiled=True)


def collect_rows(left_side, right_side):
    return lax.psum_scatter(
        jnp.dot(left_side, right_side, preferred_element_type=jnp.float32).astype(jnp.bfloat16),
        "tp",
        scatter_dimension=0,
        tiled=True,
    ).astype(jnp.float32)


def collect_grads(pairs_list):
    running = None
    for left_side, right_side in pairs_list:
        product = contract_cols(left_side, right_side)
        running = product if running is None else running + product
    return lax.psum_scatter(
        running.astype(jnp.bfloat16), "tp", scatter_dimension=0, tiled=True
    ).astype(jnp.float32)


def gather_layer(weight_set, layer_index):
    query_weight, key_matrix, value_matrix, out_weight, gate_weight, up_weight, down_weight = (
        weight_set
    )
    return (
        lax.all_gather(query_weight[layer_index], "fsdp", axis=0, tiled=True),
        lax.all_gather(key_matrix[layer_index], "fsdp", axis=0, tiled=True),
        lax.all_gather(value_matrix[layer_index], "fsdp", axis=0, tiled=True),
        lax.all_gather(out_weight[layer_index], "fsdp", axis=1, tiled=True),
        lax.all_gather(gate_weight[layer_index], "fsdp", axis=0, tiled=True),
        lax.all_gather(up_weight[layer_index], "fsdp", axis=0, tiled=True),
        lax.all_gather(down_weight[layer_index], "fsdp", axis=1, tiled=True),
    )


def score_block(
    query_block, heads_of_key, block_index, block_segment, position_index, segment_row, score_scale
):
    raw_dots = jnp.einsum(
        "qngd,knd->ngqk", query_block, heads_of_key, preferred_element_type=jnp.float32
    )
    allowed = (position_index[None, :] <= block_index[:, None]) & (
        segment_row[None, :] == block_segment[:, None]
    )
    return jnp.where(allowed[None, None], raw_dots * score_scale, -1e30)


def block_layout(heads_of_query, segment_row):
    sequence_length, kv_local, group_width, head_size = heads_of_query.shape
    rows_per_block = min(512, sequence_length)
    number_blocks = sequence_length // rows_per_block
    position_index = jnp.arange(sequence_length, dtype=jnp.int32)
    row_index = position_index.reshape(number_blocks, rows_per_block)
    row_segment = segment_row.reshape(number_blocks, rows_per_block)
    return (number_blocks, rows_per_block, position_index, row_index, row_segment)


def attend(heads_of_query, heads_of_key, heads_of_value, segment_row):
    sequence_length, kv_local, group_width, head_size = heads_of_query.shape
    score_scale = head_size ** (-0.5)
    number_blocks, rows_per_block, position_index, row_index, row_segment = block_layout(
        heads_of_query, segment_row
    )
    blocks_of_query = heads_of_query.reshape(
        number_blocks, rows_per_block, kv_local, group_width, head_size
    )

    def forward_block(inputs):
        query_block, block_index, block_segment = inputs
        scores = score_block(
            query_block,
            heads_of_key,
            block_index,
            block_segment,
            position_index,
            segment_row,
            score_scale,
        )
        top_score = jnp.max(scores, axis=-1, keepdims=True)
        weights = jnp.exp(scores - top_score)
        total_weight = jnp.sum(weights, axis=-1, keepdims=True)
        prob_low = (weights / total_weight).astype(jnp.bfloat16)
        block_out = jnp.einsum(
            "ngqk,knd->qngd", prob_low, heads_of_value, preferred_element_type=jnp.float32
        )
        return (block_out.astype(jnp.bfloat16), (top_score + jnp.log(total_weight))[..., 0])

    outputs, log_totals = lax.map(forward_block, (blocks_of_query, row_index, row_segment))
    return (outputs.reshape(sequence_length, kv_local * group_width * head_size), log_totals)


def attend_back(heads_of_query, heads_of_key, heads_of_value, segment_row, out_grad, log_totals):
    sequence_length, kv_local, group_width, head_size = heads_of_query.shape
    score_scale = head_size ** (-0.5)
    number_blocks, rows_per_block, position_index, row_index, row_segment = block_layout(
        heads_of_query, segment_row
    )
    blocks_of_query = heads_of_query.reshape(
        number_blocks, rows_per_block, kv_local, group_width, head_size
    )
    grad_blocks = out_grad.reshape(number_blocks, rows_per_block, kv_local, group_width, head_size)

    def backward_block(running_grads, inputs):
        key_grad, value_grad = running_grads
        query_block, grad_block, block_total, block_index, block_segment = inputs
        scores = score_block(
            query_block,
            heads_of_key,
            block_index,
            block_segment,
            position_index,
            segment_row,
            score_scale,
        )
        prob_block = jnp.exp(scores - block_total[..., None])
        prob_grad = jnp.einsum(
            "qngd,knd->ngqk", grad_block, heads_of_value, preferred_element_type=jnp.float32
        )
        inner_sum = jnp.sum(prob_block * prob_grad, axis=-1, keepdims=True)
        score_grad = (prob_block * (prob_grad - inner_sum)).astype(jnp.bfloat16)
        query_grad = (
            jnp.einsum(
                "ngqk,knd->qngd", score_grad, heads_of_key, preferred_element_type=jnp.float32
            )
            * score_scale
        )
        key_grad = (
            key_grad
            + jnp.einsum(
                "ngqk,qngd->knd", score_grad, query_block, preferred_element_type=jnp.float32
            )
            * score_scale
        )
        value_grad = value_grad + jnp.einsum(
            "ngqk,qngd->knd",
            prob_block.astype(jnp.bfloat16),
            grad_block,
            preferred_element_type=jnp.float32,
        )
        return ((key_grad, value_grad), query_grad)

    zero_keys = jnp.zeros(heads_of_key.shape, jnp.float32)
    (key_grad, value_grad), query_grad = lax.scan(
        backward_block,
        (zero_keys, zero_keys),
        (blocks_of_query, grad_blocks, log_totals, row_index, row_segment),
    )
    return (
        query_grad.reshape(sequence_length, kv_local * group_width, head_size),
        key_grad,
        value_grad,
    )


def general_plan(
    tokens,
    segment_ids,
    attn_gain,
    query_gain,
    key_gain,
    query_weight,
    key_matrix,
    value_matrix,
    out_weight,
    mlp_gain,
    gate_weight,
    up_weight,
    down_weight,
    cotangent,
):
    layer_count = attn_gain.shape[0]
    head_size = query_gain.shape[-1]
    segment_row = segment_ids[0]
    cosine_table, sine_table = rope_tables(positions_of(segment_row), head_size)
    weight_set = (
        query_weight,
        key_matrix,
        value_matrix,
        out_weight,
        gate_weight,
        up_weight,
        down_weight,
    )

    def turn_heads(raw_rows, gain_row):
        return head_norm(raw_rows, gain_row, cosine_table, sine_table)

    residual = tokens.astype(jnp.float32)
    saved_layers = []
    for layer_index in range(layer_count):
        gathered = gather_layer(weight_set, layer_index)
        wide_query, wide_key, wide_value, wide_out, wide_gate, wide_up, wide_down = gathered
        attn_normed, attn_back = jax.vjp(rms_scale, residual, attn_gain[layer_index])
        seq_rows = spread_rows(attn_normed.astype(jnp.bfloat16))
        sequence_length = seq_rows.shape[0]
        query_raw = jnp.dot(seq_rows, wide_query, preferred_element_type=jnp.float32)
        key_raw = jnp.dot(seq_rows, wide_key, preferred_element_type=jnp.float32)
        value_raw = jnp.dot(seq_rows, wide_value, preferred_element_type=jnp.float32)
        query_turned, query_back = jax.vjp(turn_heads, query_raw, query_gain[layer_index])
        key_turned, key_back = jax.vjp(turn_heads, key_raw, key_gain[layer_index])
        kv_local = key_raw.shape[1] // head_size
        heads_of_query = query_turned.astype(jnp.bfloat16).reshape(
            sequence_length, kv_local, -1, head_size
        )
        heads_of_key = key_turned.astype(jnp.bfloat16)
        heads_of_value = value_raw.astype(jnp.bfloat16).reshape(
            sequence_length, kv_local, head_size
        )
        attn_rows, log_totals = attend(heads_of_query, heads_of_key, heads_of_value, segment_row)
        residual_mid = residual + collect_rows(attn_rows, wide_out)
        mlp_normed, mlp_back = jax.vjp(rms_scale, residual_mid, mlp_gain[layer_index])
        mlp_rows = spread_rows(mlp_normed.astype(jnp.bfloat16))
        gate_proj = jnp.dot(mlp_rows, wide_gate, preferred_element_type=jnp.float32)
        upward = jnp.dot(mlp_rows, wide_up, preferred_element_type=jnp.float32)
        hidden_float, swiglu_back = jax.vjp(swiglu, gate_proj, upward)
        hidden = hidden_float.astype(jnp.bfloat16)
        residual = residual_mid + collect_rows(hidden, wide_down)
        saved_layers.append(
            (
                gathered,
                attn_back,
                seq_rows,
                query_back,
                key_back,
                heads_of_query,
                heads_of_key,
                heads_of_value,
                attn_rows,
                log_totals,
                mlp_back,
                mlp_rows,
                swiglu_back,
                hidden,
            )
        )
    result = residual.astype(jnp.bfloat16)
    residual_grad = cotangent.astype(jnp.float32)
    grad_weights = [None] * layer_count
    gain_grads = [None] * layer_count
    for layer_index in reversed(range(layer_count)):
        (
            gathered,
            attn_back,
            seq_rows,
            query_back,
            key_back,
            heads_of_query,
            heads_of_key,
            heads_of_value,
            attn_rows,
            log_totals,
            mlp_back,
            mlp_rows,
            swiglu_back,
            hidden,
        ) = saved_layers[layer_index]
        gathered = gather_layer(weight_set, layer_index)
        wide_query, wide_key, wide_value, wide_out, wide_gate, wide_up, wide_down = gathered
        grad_rows = spread_grads(residual_grad.astype(jnp.bfloat16))
        down_grad = contract_rows(hidden, grad_rows)
        hidden_grad = contract_cols(grad_rows, wide_down)
        gate_grad, upward_grad = swiglu_back(hidden_grad)
        gate_low = gate_grad.astype(jnp.bfloat16)
        upward_low = upward_grad.astype(jnp.bfloat16)
        gate_wgrad = contract_rows(mlp_rows, gate_low)
        upward_wgrad = contract_rows(mlp_rows, upward_low)
        normed_grad = collect_grads(((gate_low, wide_gate), (upward_low, wide_up)))
        residual_part, mlp_gain_grad = mlp_back(normed_grad)
        residual_grad = residual_grad + residual_part
        grad_rows = spread_grads(residual_grad.astype(jnp.bfloat16))
        sequence_length = grad_rows.shape[0]
        out_wgrad = contract_rows(attn_rows, grad_rows)
        mixed_grad = contract_cols(grad_rows, wide_out).astype(jnp.bfloat16)
        query_grad, key_grad, value_grad = attend_back(
            heads_of_query,
            heads_of_key,
            heads_of_value,
            segment_row,
            mixed_grad.reshape(heads_of_query.shape),
            log_totals,
        )
        query_raw_grad, query_gain_grad = query_back(query_grad)
        key_raw_grad, key_gain_grad = key_back(key_grad)
        query_low = query_raw_grad.astype(jnp.bfloat16)
        key_low = key_raw_grad.astype(jnp.bfloat16)
        value_low = value_grad.reshape(sequence_length, -1).astype(jnp.bfloat16)
        query_wgrad = contract_rows(seq_rows, query_low)
        key_wgrad = contract_rows(seq_rows, key_low)
        value_wgrad = contract_rows(seq_rows, value_low)
        normed_grad = collect_grads(
            ((query_low, wide_query), (key_low, wide_key), (value_low, wide_value))
        )
        residual_part, attn_gain_grad = attn_back(normed_grad)
        residual_grad = residual_grad + residual_part
        grad_weights[layer_index] = (
            lax.psum_scatter(
                query_wgrad.astype(jnp.bfloat16), "fsdp", scatter_dimension=0, tiled=True
            ).astype(jnp.float32),
            lax.psum_scatter(
                key_wgrad.astype(jnp.bfloat16), "fsdp", scatter_dimension=0, tiled=True
            ).astype(jnp.float32),
            lax.psum_scatter(
                value_wgrad.astype(jnp.bfloat16), "fsdp", scatter_dimension=0, tiled=True
            ).astype(jnp.float32),
            lax.psum_scatter(
                out_wgrad.astype(jnp.bfloat16), "fsdp", scatter_dimension=1, tiled=True
            ).astype(jnp.float32),
            lax.psum_scatter(
                gate_wgrad.astype(jnp.bfloat16), "fsdp", scatter_dimension=0, tiled=True
            ).astype(jnp.float32),
            lax.psum_scatter(
                upward_wgrad.astype(jnp.bfloat16), "fsdp", scatter_dimension=0, tiled=True
            ).astype(jnp.float32),
            lax.psum_scatter(
                down_grad.astype(jnp.bfloat16), "fsdp", scatter_dimension=1, tiled=True
            ).astype(jnp.float32),
        )
        gain_grads[layer_index] = (attn_gain_grad, query_gain_grad, key_gain_grad, mlp_gain_grad)
    local_stacks = tuple(
        (
            jnp.stack([grad_weights[layer_index][member] for layer_index in range(layer_count)])
            for member in range(7)
        )
    )
    gain_stacks = tuple(
        (
            jnp.stack([gain_grads[layer_index][member] for layer_index in range(layer_count)])
            for member in range(4)
        )
    )
    summed = lax.psum(
        (gain_stacks[0], gain_stacks[1], gain_stacks[2], gain_stacks[3]), ("fsdp", "tp")
    )
    return (
        result,
        residual_grad,
        summed[0],
        summed[1],
        summed[2],
        local_stacks[0],
        local_stacks[1],
        local_stacks[2],
        local_stacks[3],
        summed[3],
        local_stacks[4],
        local_stacks[5],
        local_stacks[6],
    )


def plane_send(values, distance):
    size = lax.axis_size("fsdp")
    return lax.ppermute(values, "fsdp", [(i, i ^ distance) for i in range(size)])


def plane_place():
    return lax.axis_index("fsdp").astype(jnp.int32).reshape(1)


def low(values):
    return values.astype(jnp.bfloat16)


def wide(values):
    return values.astype(jnp.float32)


def add_low(left, right):
    return low(wide(left) + wide(right))


def gather_plane(own):
    half = own.shape[0] // 2
    core = plane_send(own, 1)
    across_x = plane_send(own, 2)
    across_y = plane_send(own, 4)
    diagonal = jnp.concatenate(
        [plane_send(across_y[:half], 2), plane_send(across_x[half:], 4)]
    )
    return [
        own,
        core,
        across_x,
        plane_send(across_x, 1),
        across_y,
        plane_send(across_y, 1),
        diagonal,
        plane_send(diagonal, 1),
    ]


def reduce_plane(part):
    received = {d: plane_send(low(part(d)), 1) for d in (7, 5, 3, 1)}
    far, by_y, by_x, here = (
        low(part(d) + wide(received[d + 1])) if d else part(d) + wide(received[d + 1])
        for d in (6, 4, 2, 0)
    )
    half = far.shape[0] // 2
    top = plane_send(far[:half], 2)
    bottom = plane_send(far[half:], 4)
    by_y = jnp.concatenate([add_low(by_y[:half], top), by_y[half:]])
    by_x = jnp.concatenate([by_x[:half], add_low(by_x[half:], bottom)])
    from_x = plane_send(by_x, 2)
    from_y = plane_send(by_y, 4)
    return here + wide(from_x) + wide(from_y), far, by_x


def reduce_all(values):
    for distance in (1, 2, 4):
        values = values + plane_send(values, distance)
    size = lax.axis_size("tp")
    if size & (size - 1):
        return lax.psum(values, "tp")
    distance = 1
    while distance < size:
        pairs = [(i, i ^ distance) for i in range(size)]
        values = values + lax.ppermute(values, "tp", pairs)
        distance *= 2
    return values


def after(token, *values):
    if token is None:
        return values
    return lax.optimization_barrier((token, *values))[1:]


def line_gather(own, axis=0):
    return lax.all_gather(own, "tp", axis=axis, tiled=True)


def line_reduce(terms, axis=0):
    return lax.psum_scatter(terms, "tp", scatter_dimension=axis, tiled=True)


def assemble(pieces, axis, places):
    size = len(pieces)
    block = pieces[0].shape[axis]
    shape = list(pieces[0].shape)
    shape[axis] = size * block

    def kernel(place_ref, *refs):
        out = refs[size]
        for d in range(size):
            start = pl.multiple_of(place_ref[d] * block, block)
            where = tuple([slice(None)] * axis + [pl.ds(start, block)])
            out[where] = refs[d][...]

    return pl.pallas_call(
        kernel,
        out_shape=jax.ShapeDtypeStruct(tuple(shape), pieces[0].dtype),
        in_specs=[pl.BlockSpec(memory_space=pltpu.SMEM)]
        + [pl.BlockSpec(memory_space=pltpu.VMEM)] * size,
        out_specs=pl.BlockSpec(memory_space=pltpu.VMEM),
        compiler_params=pltpu.CompilerParams(vmem_limit_bytes=32 * 1024 * 1024),
        name="assemble",
    )(places, *pieces)


def block_at(array, index, block, axis):
    return lax.dynamic_slice_in_dim(array, index * block, block, axis)


def swap(array, axis, into, start=None, done=None):
    size = lax.axis_size("fsdp")
    places = lax.axis_index("fsdp").astype(jnp.int32) ^ jnp.arange(size, dtype=jnp.int32)
    block = array.shape[axis] // size
    (array,) = after(start, array)
    pieces = [block_at(array, places[d], block, axis) for d in range(size)]
    order = (6, 7, 4, 5, 2, 3, 1)
    moved = {d: plane_send(pieces[d], d) for d in order}
    moved = after(done, *(moved[d] for d in range(1, size)))
    return assemble([pieces[0], *moved], into, places)


def line_swap(array, start=None, done=None):
    size = lax.axis_size("tp")
    place = lax.axis_index("tp").astype(jnp.int32)
    block = array.shape[0] // size
    sources = (place - jnp.arange(size, dtype=jnp.int32)) % size
    (array,) = after(start, array)
    moved = []
    for step in range(1, size):
        piece = block_at(array, (place + step) % size, block, 0)
        pairs = [(i, (i + step) % size) for i in range(size)]
        moved.append(lax.ppermute(piece, "tp", pairs))
    moved = after(done, *moved)
    return assemble([block_at(array, place, block, 0), *moved], 0, sources)


def line_rows(rows, start=None, done=None):
    size, line = lax.axis_size("fsdp"), lax.axis_size("tp")
    count, width = rows.shape
    blocks = line_swap(rows, start, done).reshape(line, size // line, count // size, width)
    return blocks.transpose(1, 0, 2, 3).reshape(count, width)


def line_rows_back(rows, start=None, done=None):
    size, line = lax.axis_size("fsdp"), lax.axis_size("tp")
    count, width = rows.shape
    blocks = rows.reshape(size // line, line, count // size, width).transpose(1, 0, 2, 3)
    return line_swap(blocks.reshape(count, width), start, done)


def plane_segments(segment_ids):
    size, line = lax.axis_size("fsdp"), lax.axis_size("tp")
    rows = segment_ids
    for distance in (1, 2, 4):
        rows = jnp.concatenate([rows, plane_send(rows, distance)])
    local = size // line
    wanted = lax.axis_index("tp") * local + jnp.arange(local)
    return rows[wanted ^ lax.axis_index("fsdp")]


def attention_weights(query_shard, key_shard, value_shard, out_shard):
    size, line = lax.axis_size("fsdp"), lax.axis_size("tp")
    per, depth = size // line, query_shard.shape[0]
    pack = jnp.concatenate(
        [
            query_shard.T.reshape(per, -1, depth),
            key_shard.T.reshape(per, -1, depth),
            value_shard.T.reshape(per, -1, depth),
            out_shard.reshape(per, -1, depth),
        ],
        axis=1,
    )
    gathered = line_gather(pack)
    return swap(gathered, 0, 2)[0], gathered


def turn(values, cosine, sine):
    return values * cosine + pltpu.roll(values, values.shape[1] // 2, 1) * sine


def turn_back(values, cosine, sine):
    return values * cosine - pltpu.roll(values, values.shape[1] // 2, 1) * sine


def inverse_rms(values):
    return lax.rsqrt(jnp.mean(values * values, axis=-1, keepdims=True) + EPSILON)


def rows_in_order(place, groups, target, pick):
    for d in range(2 * len(groups)):
        ref = groups[d // 2]
        blocks, block = ref.shape[2], ref.shape[3]
        for i in range(blocks):
            start = pl.multiple_of((i * 2 * len(groups) + (place ^ d)) * block, block)
            target[pl.ds(start, block), :] = pick(ref[d % 2, 0, i])


def rows_from_order(place, source, groups):
    for d in range(2 * len(groups)):
        ref = groups[d // 2]
        blocks, block = ref.shape[2], ref.shape[3]
        for i in range(blocks):
            start = pl.multiple_of((i * 2 * len(groups) + (place ^ d)) * block, block)
            ref[d % 2, 0, i] = source[pl.ds(start, block), :].astype(ref.dtype)


def head_columns(index, head):
    return slice(index * head, (index + 1) * head)


def heads_from_raw(nat, cos_ref, sin_ref, gains, heads, low_ref, rows):
    head = cos_ref.shape[-1]
    for start in range(0, nat.shape[0], rows):
        here = slice(start, start + rows)
        cosine, sine = cos_ref[0, here, :], sin_ref[0, here, :]
        for h in range(heads + 2):
            raw = nat[here, head_columns(h, head)]
            if h <= heads:
                gain = gains[0] if h < heads else gains[1]
                raw = turn(raw * inverse_rms(raw) * gain[...], cosine, sine)
            low_ref[here, head_columns(h, head)] = raw.astype(low_ref.dtype)


def block_operands(low_ref, start, rows, heads, head):
    query = jnp.concatenate(
        [low_ref[start : start + rows, head_columns(h, head)] for h in range(heads)], axis=0
    )
    key = low_ref[: start + rows, head_columns(heads, head)]
    value = low_ref[: start + rows, head_columns(heads + 1, head)]
    return query, key, value


def masked_scores(key, query, first_ref, start, rows, heads, scale):
    scores = lax.dot_general(
        key, query, (((1,), (1,)), ((), ())), preferred_element_type=jnp.float32
    )
    shape = (key.shape[0], rows)
    index = lax.broadcasted_iota(jnp.int32, shape, 0)
    mine = lax.broadcasted_iota(jnp.int32, shape, 1) + start
    first = first_ref[0, :, start : start + rows]
    allowed = (index <= mine) & (index >= first)
    allowed = jnp.concatenate([allowed] * heads, axis=1)
    return jnp.where(allowed, scores * scale, -1e30)


def attend_kernel(groups, heads, rows, *refs):
    place = refs[0][0]
    raw_refs = refs[1 : 1 + groups]
    cos_ref, sin_ref, first_ref, query_gain, key_gain = refs[1 + groups : 6 + groups]
    out_refs = refs[6 + groups : 6 + 2 * groups]
    total_ref, nat, low_ref, mixed = refs[6 + 2 * groups :]
    head = cos_ref.shape[-1]
    rows_in_order(place, raw_refs, nat, lambda v: v)
    heads_from_raw(nat, cos_ref, sin_ref, (query_gain, key_gain), heads, low_ref, rows)
    for i in range(nat.shape[0] // rows):
        start = i * rows
        query, key, value = block_operands(low_ref, start, rows, heads, head)
        scores = masked_scores(key, query, first_ref, start, rows, heads, head ** (-0.5))
        top = jnp.max(scores, axis=0, keepdims=True)
        weights = jnp.exp(scores - top)
        total = jnp.sum(weights, axis=0, keepdims=True)
        total_ref[0, i : i + 1, :] = top + jnp.log(total)
        prob = (weights * (1.0 / total)).astype(jnp.bfloat16)
        out = lax.dot_general(
            prob, value, (((0,), (0,)), ((), ())), preferred_element_type=jnp.float32
        ).astype(jnp.bfloat16)
        for h in range(heads):
            mixed[start : start + rows, head_columns(h, head)] = out[h * rows : (h + 1) * rows]
    rows_from_order(place, mixed, out_refs)


def attend_back_kernel(groups, heads, rows, *refs):
    place = refs[0][0]
    raw_refs = refs[1 : 1 + groups]
    grad_refs = refs[1 + groups : 1 + 2 * groups]
    rest = refs[1 + 2 * groups :]
    total_ref, cos_ref, sin_ref, first_ref, query_gain, key_gain = rest[:6]
    out_refs = rest[6 : 6 + groups]
    gain_ref, nat, low_ref, mixed, grads, key_sum, value_sum, done = rest[6 + groups :]
    head = cos_ref.shape[-1]
    scale = head ** (-0.5)
    rows_in_order(place, raw_refs, nat, lambda v: v)
    rows_in_order(place, grad_refs, mixed, lambda v: v)
    heads_from_raw(nat, cos_ref, sin_ref, (query_gain, key_gain), heads, low_ref, rows)
    key_sum[...] = jnp.zeros_like(key_sum)
    value_sum[...] = jnp.zeros_like(value_sum)
    for i in range(nat.shape[0] // rows):
        start = i * rows
        stop = start + rows
        query, key, value = block_operands(low_ref, start, rows, heads, head)
        out_grad = jnp.concatenate(
            [mixed[start:stop, head_columns(h, head)] for h in range(heads)], axis=0
        )
        scores = masked_scores(key, query, first_ref, start, rows, heads, scale)
        prob = jnp.exp(scores - total_ref[0, i : i + 1, :])
        prob_grad = lax.dot_general(
            value, out_grad, (((1,), (1,)), ((), ())), preferred_element_type=jnp.float32
        )
        inner = jnp.sum(prob * prob_grad, axis=0, keepdims=True)
        score_grad = (prob * (prob_grad - inner)).astype(jnp.bfloat16)
        value_sum[:stop, :] += jnp.dot(
            prob.astype(jnp.bfloat16), out_grad, preferred_element_type=jnp.float32
        )
        key_sum[:stop, :] += jnp.dot(score_grad, query, preferred_element_type=jnp.float32)
        query_grad = lax.dot_general(
            score_grad, key, (((0,), (0,)), ((), ())), preferred_element_type=jnp.float32
        )
        for h in range(heads):
            grads[start:stop, head_columns(h, head)] = query_grad[h * rows : (h + 1) * rows] * scale
    sums = [jnp.zeros((1, head), jnp.float32)] * 2
    for start in range(0, nat.shape[0], rows):
        here = slice(start, start + rows)
        cosine, sine = cos_ref[0, here, :], sin_ref[0, here, :]
        for h in range(heads + 1):
            kind = 0 if h < heads else 1
            gain = (query_gain, key_gain)[kind][...]
            grad = grads[here, head_columns(h, head)] if h < heads else key_sum[here, :] * scale
            raw = nat[here, head_columns(h, head)]
            inverse = inverse_rms(raw)
            grad = turn_back(grad, cosine, sine)
            sums[kind] += jnp.sum(grad * raw * inverse, axis=0, keepdims=True)
            grad = grad * gain
            middle = jnp.mean(grad * raw, axis=-1, keepdims=True)
            done[here, head_columns(h, head)] = (
                inverse * grad - raw * (inverse * inverse * inverse) * middle
            ).astype(done.dtype)
        done[here, head_columns(heads + 1, head)] = value_sum[here, :].astype(done.dtype)
    gain_ref[0] = jnp.concatenate(sums, axis=0)
    rows_from_order(place, done, out_refs)


def attend_specs(raw, tables, first, length, head):
    local = tables[0].shape[0]
    group = pl.BlockSpec((2, 1) + raw[0].shape[2:], lambda s: (0, s, 0, 0, 0))
    table = pl.BlockSpec((1, length, head), lambda s: (s, 0, 0))
    line = pl.BlockSpec((1, 1, length), lambda s: (s, 0, 0))
    gain = pl.BlockSpec((1, head), lambda s: (0, 0))
    return local, group, table, line, gain


def grouped(rows, local, blocks):
    count, width = rows.shape
    return rows.reshape(2, local, blocks, count // (2 * local * blocks), width)


def plane_attend(raw, tables, first, gains, rows=256):
    head = tables[0].shape[-1]
    length = tables[0].shape[1]
    local, group, table, line, gain = attend_specs(raw, tables, first, length, head)
    width = raw[0].shape[-1]
    heads = width // head - 2
    groups = len(raw)
    out_shape = raw[0].shape[:-1] + (heads * head,)
    out_group = pl.BlockSpec((2, 1) + out_shape[2:], lambda s: (0, s, 0, 0, 0))
    totals = jax.ShapeDtypeStruct((local, length // rows, heads * rows), jnp.float32)
    out = pl.pallas_call(
        functools.partial(attend_kernel, groups, heads, rows),
        grid=(local,),
        out_shape=[jax.ShapeDtypeStruct(out_shape, jnp.bfloat16)] * groups + [totals],
        in_specs=[pl.BlockSpec(memory_space=pltpu.SMEM)]
        + [group] * groups
        + [table, table, line, gain, gain],
        out_specs=[out_group] * groups
        + [pl.BlockSpec((1,) + totals.shape[1:], lambda s: (s, 0, 0))],
        scratch_shapes=[
            pltpu.VMEM((length, width), jnp.float32),
            pltpu.VMEM((length, width), jnp.bfloat16),
            pltpu.VMEM((length, heads * head), jnp.bfloat16),
        ],
        compiler_params=pltpu.CompilerParams(vmem_limit_bytes=48 * 1024 * 1024),
        cost_estimate=pl.CostEstimate(
            flops=local * heads * length * length * head * 5 // 2,
            bytes_accessed=local * length * width * 6,
            transcendentals=local * heads * length * length * 5 // 8,
        ),
        name="attend",
    )(plane_place(), *raw, *tables, first, *gains)
    return out[:groups], out[groups]


def plane_attend_back(raw, out_grad, totals, tables, first, gains, rows=256):
    head = tables[0].shape[-1]
    length = tables[0].shape[1]
    local, group, table, line, gain = attend_specs(raw, tables, first, length, head)
    width = raw[0].shape[-1]
    heads = width // head - 2
    groups = len(raw)
    grad_group = pl.BlockSpec((2, 1) + out_grad[0].shape[2:], lambda s: (0, s, 0, 0, 0))
    out = pl.pallas_call(
        functools.partial(attend_back_kernel, groups, heads, rows),
        grid=(local,),
        out_shape=[jax.ShapeDtypeStruct(raw[0].shape, jnp.bfloat16)] * groups
        + [jax.ShapeDtypeStruct((local, 2, head), jnp.float32)],
        in_specs=[pl.BlockSpec(memory_space=pltpu.SMEM)]
        + [group] * groups
        + [grad_group] * groups
        + [pl.BlockSpec((1,) + totals.shape[1:], lambda s: (s, 0, 0))]
        + [table, table, line, gain, gain],
        out_specs=[group] * groups + [pl.BlockSpec((1, 2, head), lambda s: (s, 0, 0))],
        scratch_shapes=[
            pltpu.VMEM((length, width), jnp.float32),
            pltpu.VMEM((length, width), jnp.bfloat16),
            pltpu.VMEM((length, heads * head), jnp.bfloat16),
            pltpu.VMEM((length, heads * head), jnp.float32),
            pltpu.VMEM((length, head), jnp.float32),
            pltpu.VMEM((length, head), jnp.float32),
            pltpu.VMEM((length, width), jnp.bfloat16),
        ],
        compiler_params=pltpu.CompilerParams(vmem_limit_bytes=56 * 1024 * 1024),
        cost_estimate=pl.CostEstimate(
            flops=local * heads * length * length * head * 25 // 4,
            bytes_accessed=local * length * width * 8,
            transcendentals=local * heads * length * length * 5 // 8,
        ),
        name="attend_back",
    )(plane_place(), *raw, *out_grad, totals, *tables, first, *gains)
    return out[:groups], jnp.sum(out[groups], axis=0)


def plane_plan(
    tokens,
    segment_ids,
    attn_gain,
    query_gain,
    key_gain,
    query_weight,
    key_matrix,
    value_matrix,
    out_weight,
    mlp_gain,
    gate_weight,
    up_weight,
    down_weight,
    cotangent,
):
    layers = attn_gain.shape[0]
    head = query_gain.shape[-1]
    size, line = lax.axis_size("fsdp"), lax.axis_size("tp")
    local = size // line
    segments = plane_segments(segment_ids)
    length = segments.shape[1]
    positions = jax.vmap(positions_of)(segments)
    first = (jnp.arange(length, dtype=jnp.int32)[None] - positions).reshape(local, 1, length)
    cosine_table, sine_table = rope_tables(positions.reshape(-1), head)
    turned_sign = jnp.where(jnp.arange(head) < head // 2, -1.0, 1.0)
    tables = (
        cosine_table.reshape(local, length, head),
        (sine_table * turned_sign).reshape(local, length, head),
    )
    query_count = query_weight.shape[2] * line // size
    key_count = key_matrix.shape[2] * line // size
    split = query_count + 2 * key_count

    def pairs_of(pieces):
        return [jnp.concatenate(pieces[d : d + 2]) for d in range(0, size, 2)]

    def piece(pairs, d):
        half = pairs[d // 2].shape[0] // 2
        return pairs[d // 2][half * (d % 2) : half * (d % 2 + 1)]

    def dot(left, right):
        return jnp.dot(left, right, preferred_element_type=jnp.float32)

    attn_sets, attn_gathered, hidden_sets = ([None] * layers for _ in range(3))

    def fetch_attn(index, token):
        shards = (query_weight[index], key_matrix[index], value_matrix[index], out_weight[index])
        attn_sets[index], attn_gathered[index] = attention_weights(*after(token, *shards))

    def shard_hidden(index, start, done):
        shards = jnp.stack([gate_weight[index].T, up_weight[index].T, down_weight[index]])
        return swap(shards, 1, 2, start, done)

    fetch_attn(0, segment_ids)
    first_rows = swap(tokens, 0, 0)
    residual = line_rows(first_rows)
    residual = wide(residual)
    grad = None
    saved = []
    for index in range(layers):
        pack = attn_sets[index]
        gains = (query_gain[index][None], key_gain[index][None])
        normed, attn_back = jax.vjp(rms_scale, residual, attn_gain[index])
        pieces = gather_plane(low(normed))
        if index == 0:
            shards = shard_hidden(0, first_rows, pieces[1])
            hidden_sets[0] = line_gather(after(attn_gathered[0], shards)[0], 1)
            pieces[6:] = after(shards, *pieces[6:])
        rows = pairs_of(pieces)
        raw = [grouped(contract_cols(v, pack[:split]), local, line) for v in rows]
        if index + 1 < layers:
            fetch_attn(index + 1, raw[0])
        mixed, totals = plane_attend(raw, tables, first, gains)
        mixed = [v.reshape(-1, query_count) for v in mixed]
        if index == 0:
            grad = swap(cotangent, 0, 0, raw[0])
            mixed = after(grad, *mixed)
        total, *_ = reduce_plane(lambda d: dot(piece(mixed, d), pack[split:]))
        middle = residual + total
        if index == 0:
            grad = line_rows(grad, mixed[0])
            middle, grad = lax.optimization_barrier((middle, grad))
            grad = wide(grad)
        gate_rows, up_rows, down_rows = hidden_sets[index]
        normed, mlp_back = jax.vjp(rms_scale, middle, mlp_gain[index])
        mlp_rows = pairs_of(gather_plane(low(normed)))
        hidden, swiglu_backs = [], []
        for v in mlp_rows:
            gate, upward = contract_cols(v, gate_rows), contract_cols(v, up_rows)
            units, swiglu_back = jax.vjp(swiglu, gate, upward)
            hidden.append(low(units))
            swiglu_backs.append(swiglu_back)
        if index + 1 < layers:
            shards = shard_hidden(index + 1, mlp_rows[-1], None)
            hidden_sets[index + 1] = line_gather(shards, 1)
            hidden = list(after(shards, *hidden))
        total, *_ = reduce_plane(lambda d: dot(piece(hidden, d), down_rows))
        residual = middle + total
        saved.append(
            (attn_back, rows, raw, mixed, totals, mlp_back, mlp_rows, swiglu_backs, hidden)
        )
    result = residual
    pack_grads, pack_sums, gain_grads, hidden_sums, hidden_grads = (
        [None] * layers for _ in range(5)
    )
    for index in reversed(range(layers)):
        pack = attn_sets[index]
        gains = (query_gain[index][None], key_gain[index][None])
        gate_rows, up_rows, down_rows = hidden_sets[index]
        attn_back, rows, raw, mixed, totals, mlp_back, mlp_rows, swiglu_backs, hidden = saved[index]
        if index + 1 == layers:
            (grad,) = after(tuple(mlp_rows), grad)
        grad_rows = pairs_of(gather_plane(low(grad)))
        gate_grads, up_grads = [], []
        for v, swiglu_back in zip(grad_rows, swiglu_backs):
            gate_grad, up_grad = swiglu_back(contract_cols(v, down_rows))
            gate_grads.append(low(gate_grad))
            up_grads.append(low(up_grad))
        if index + 1 == layers:
            gate_grads = after(result, *gate_grads)
        normed_grad, token, token_next = reduce_plane(
            lambda d: dot(piece(gate_grads, d), gate_rows) + dot(piece(up_grads, d), up_rows)
        )
        hidden, grad_rows = (after(token, *v) for v in (hidden, grad_rows))
        gate_grads, up_grads, mlp_rows = (
            after(token_next, *v) for v in (gate_grads, up_grads, mlp_rows)
        )
        all_grads, all_rows = jnp.concatenate(grad_rows), jnp.concatenate(mlp_rows)
        terms = [
            low(contract_rows(jnp.concatenate(gate_grads), all_rows)),
            low(contract_rows(jnp.concatenate(up_grads), all_rows)),
            low(contract_rows(jnp.concatenate(hidden), all_grads)),
        ]
        normed_grad, *terms = lax.optimization_barrier((normed_grad, *terms))
        if index + 1 < layers:
            done = hidden_sums[index + 1]
            above = swap(pack_grads[index + 1][None], 2, 0, grad_rows[-1])
            result = swap(result, 0, 0, grad_rows[-1])
            normed_grad, above, result = lax.optimization_barrier((normed_grad, above, result))
            pack_sums[index + 1] = line_reduce(after(done, above)[0])
            terms = after(done, *terms)
        hidden_sums[index] = line_reduce(jnp.stack(terms), 1)
        grad_part, mlp_gain_grad = mlp_back(normed_grad)
        grad = grad + grad_part
        grad_rows = pairs_of(gather_plane(low(grad)))
        mixed_grad = [
            grouped(low(contract_cols(v, pack[split:])), local, line) for v in grad_rows
        ]
        raw_grad, head_gain_grads = plane_attend_back(raw, mixed_grad, totals, tables, first, gains)
        if index + 1 < layers:
            hidden_grads[index + 1] = swap(hidden_sums[index + 1], 2, 1, mixed_grad[-1])
            raw_grad = after(hidden_grads[index + 1], *raw_grad)
        raw_grad = [v.reshape(-1, split) for v in raw_grad]
        normed_grad, token, token_next = reduce_plane(lambda d: dot(piece(raw_grad, d), pack[:split]))
        mixed, grad_rows = (after(token, *v) for v in (mixed, grad_rows))
        raw_grad, rows = (after(token_next, *v) for v in (raw_grad, rows))
        pack_grad = jnp.concatenate(
            [
                low(contract_rows(jnp.concatenate(raw_grad), jnp.concatenate(rows))),
                low(contract_rows(jnp.concatenate(mixed), jnp.concatenate(grad_rows))),
            ]
        )
        normed_grad, pack_grad = lax.optimization_barrier((normed_grad, pack_grad))
        pack_grads[index] = pack_grad
        if index + 1 == layers:
            result = line_rows_back(low(result), raw_grad[0])
            normed_grad, result = lax.optimization_barrier((normed_grad, result))
        grad_part, attn_gain_grad = attn_back(normed_grad)
        grad = grad + grad_part
        gain_grads[index] = jnp.concatenate(
            [attn_gain_grad, mlp_gain_grad, head_gain_grads[0], head_gain_grads[1]]
        )
    token_grad = wide(swap(line_rows_back(low(grad)), 0, 0))
    below = swap(pack_grads[0][None], 2, 0)
    pack_sums[0] = line_reduce(after((hidden_sums[0], pack_sums[1:]), below)[0])
    hidden_grads[0] = swap(hidden_sums[0], 2, 1)
    kinds = wide(jnp.stack(hidden_grads, 1))
    hidden_stacks = (kinds[0].swapaxes(1, 2), kinds[1].swapaxes(1, 2), kinds[2])
    marks = (0, query_count, query_count + key_count, split, pack_sums[0].shape[1])
    kinds = [
        jnp.stack(
            [wide(v[:, low_mark:high_mark]).reshape(-1, v.shape[-1]) for v in pack_sums]
        )
        for low_mark, high_mark in zip(marks, marks[1:])
    ]
    weight_stacks = [v.swapaxes(1, 2) for v in kinds[:3]] + kinds[3:]
    width = attn_gain.shape[1]
    gain_stack = reduce_all(jnp.stack(gain_grads).reshape(-1, head)).reshape(layers, -1)
    attn_sum, mlp_sum, query_sum, key_sum = (
        gain_stack[:, :width],
        gain_stack[:, width : 2 * width],
        gain_stack[:, 2 * width : 2 * width + head],
        gain_stack[:, 2 * width + head :],
    )
    return (
        result,
        token_grad,
        attn_sum,
        query_sum,
        key_sum,
        *weight_stacks,
        mlp_sum,
        *hidden_stacks,
    )


def plane_fits(mesh, shapes):
    size, line = mesh.shape["fsdp"], mesh.shape["tp"]
    heads = shapes[6].shape[2] // shapes[4].shape[1]
    return size == 8 and heads == size and size % line == 0 and shapes[1].shape[0] == size


def solution(mesh):
    placed = (
        P(("fsdp", "tp"), None),
        P("fsdp", None),
        P(),
        P(),
        P(),
        P(None, "fsdp", "tp"),
        P(None, "fsdp", "tp"),
        P(None, "fsdp", "tp"),
        P(None, "tp", "fsdp"),
        P(),
        P(None, "fsdp", "tp"),
        P(None, "fsdp", "tp"),
        P(None, "tp", "fsdp"),
        P(("fsdp", "tp"), None),
    )
    def mapped(plan):
      return jax.shard_map(
        plan,
        mesh=mesh,
        in_specs=placed,
        out_specs=(
            P(("fsdp", "tp"), None),
            P(("fsdp", "tp"), None),
            P(),
            P(),
            P(),
            P(None, "fsdp", "tp"),
            P(None, "fsdp", "tp"),
            P(None, "fsdp", "tp"),
            P(None, "tp", "fsdp"),
            P(),
            P(None, "fsdp", "tp"),
            P(None, "fsdp", "tp"),
            P(None, "tp", "fsdp"),
        ),
        check_vma=False,
    )

    def whole(*args):
        return mapped(plane_plan if plane_fits(mesh, args) else general_plan)(*args)

    return whole
```

```python
import functools
import math

import jax
import jax.numpy as jnp
from jax import lax
from jax.experimental import pallas as pl
from jax.experimental.pallas import tpu as pltpu
from jax.sharding import PartitionSpec as P

EPSILON = 1e-06
ROPE_BASE = 1000000.0


def rms_scale(values, gain_row):
    return (
        values * lax.rsqrt(jnp.mean(values * values, axis=-1, keepdims=True) + EPSILON) * gain_row
    )


def positions_of(segment_row):
    sequence_length = segment_row.shape[0]
    position_index = jnp.arange(sequence_length, dtype=jnp.int32)
    starts = jnp.concatenate([jnp.ones((1,), dtype=jnp.bool_), segment_row[1:] != segment_row[:-1]])
    first_index = lax.cummax(
        jnp.where(starts, position_index, jnp.zeros_like(position_index)), axis=0
    )
    return position_index - first_index


def rope_tables(positions, head_size):
    half_size = head_size // 2
    steps_float = jnp.arange(half_size, dtype=jnp.float32)
    inverse = jnp.exp(steps_float * (-2.0 * math.log(ROPE_BASE) / head_size))
    angles = positions.astype(jnp.float32)[:, None] * inverse[None, :]
    angles = jnp.concatenate([angles, angles], axis=-1)
    return (jnp.cos(angles), jnp.sin(angles))


def rotate(values, cosine_table, sine_table):
    half_size = values.shape[-1] // 2
    turned = jnp.concatenate([-values[..., half_size:], values[..., :half_size]], axis=-1)
    return values * cosine_table[:, None, :] + turned * sine_table[:, None, :]


def head_norm(raw_rows, gain_row, cosine_table, sine_table):
    head_size = gain_row.shape[-1]
    shaped = raw_rows.reshape(raw_rows.shape[0], raw_rows.shape[1] // head_size, head_size)
    return rotate(rms_scale(shaped, gain_row), cosine_table, sine_table)


def swiglu(gate_proj, upward):
    return jax.nn.silu(gate_proj) * upward


def contract_rows(left_side, right_side):
    return lax.dot_general(
        left_side, right_side, (((0,), (0,)), ((), ())), preferred_element_type=jnp.float32
    )


def contract_cols(left_side, right_side):
    return lax.dot_general(
        left_side, right_side, (((1,), (1,)), ((), ())), preferred_element_type=jnp.float32
    )


def spread_rows(rows_low):
    return lax.all_gather(rows_low, "tp", axis=0, tiled=True)


def spread_grads(grad_low):
    return lax.all_gather(grad_low, "tp", axis=0, tiled=True)


def collect_rows(left_side, right_side):
    return lax.psum_scatter(
        jnp.dot(left_side, right_side, preferred_element_type=jnp.float32).astype(jnp.bfloat16),
        "tp",
        scatter_dimension=0,
        tiled=True,
    ).astype(jnp.float32)


def collect_grads(pairs_list):
    running = None
    for left_side, right_side in pairs_list:
        product = contract_cols(left_side, right_side)
        running = product if running is None else running + product
    return lax.psum_scatter(
        running.astype(jnp.bfloat16), "tp", scatter_dimension=0, tiled=True
    ).astype(jnp.float32)


def gather_layer(weight_set, layer_index):
    query_weight, key_matrix, value_matrix, out_weight, gate_weight, up_weight, down_weight = (
        weight_set
    )
    return (
        lax.all_gather(query_weight[layer_index], "fsdp", axis=0, tiled=True),
        lax.all_gather(key_matrix[layer_index], "fsdp", axis=0, tiled=True),
        lax.all_gather(value_matrix[layer_index], "fsdp", axis=0, tiled=True),
        lax.all_gather(out_weight[layer_index], "fsdp", axis=1, tiled=True),
        lax.all_gather(gate_weight[layer_index], "fsdp", axis=0, tiled=True),
        lax.all_gather(up_weight[layer_index], "fsdp", axis=0, tiled=True),
        lax.all_gather(down_weight[layer_index], "fsdp", axis=1, tiled=True),
    )


def score_block(
    query_block, heads_of_key, block_index, block_segment, position_index, segment_row, score_scale
):
    raw_dots = jnp.einsum(
        "qngd,knd->ngqk", query_block, heads_of_key, preferred_element_type=jnp.float32
    )
    allowed = (position_index[None, :] <= block_index[:, None]) & (
        segment_row[None, :] == block_segment[:, None]
    )
    return jnp.where(allowed[None, None], raw_dots * score_scale, -1e30)


def block_layout(heads_of_query, segment_row):
    sequence_length, kv_local, group_width, head_size = heads_of_query.shape
    rows_per_block = min(512, sequence_length)
    number_blocks = sequence_length // rows_per_block
    position_index = jnp.arange(sequence_length, dtype=jnp.int32)
    row_index = position_index.reshape(number_blocks, rows_per_block)
    row_segment = segment_row.reshape(number_blocks, rows_per_block)
    return (number_blocks, rows_per_block, position_index, row_index, row_segment)


def attend(heads_of_query, heads_of_key, heads_of_value, segment_row):
    sequence_length, kv_local, group_width, head_size = heads_of_query.shape
    score_scale = head_size ** (-0.5)
    number_blocks, rows_per_block, position_index, row_index, row_segment = block_layout(
        heads_of_query, segment_row
    )
    blocks_of_query = heads_of_query.reshape(
        number_blocks, rows_per_block, kv_local, group_width, head_size
    )

    def forward_block(inputs):
        query_block, block_index, block_segment = inputs
        scores = score_block(
            query_block,
            heads_of_key,
            block_index,
            block_segment,
            position_index,
            segment_row,
            score_scale,
        )
        top_score = jnp.max(scores, axis=-1, keepdims=True)
        weights = jnp.exp(scores - top_score)
        total_weight = jnp.sum(weights, axis=-1, keepdims=True)
        prob_low = (weights / total_weight).astype(jnp.bfloat16)
        block_out = jnp.einsum(
            "ngqk,knd->qngd", prob_low, heads_of_value, preferred_element_type=jnp.float32
        )
        return (block_out.astype(jnp.bfloat16), (top_score + jnp.log(total_weight))[..., 0])

    outputs, log_totals = lax.map(forward_block, (blocks_of_query, row_index, row_segment))
    return (outputs.reshape(sequence_length, kv_local * group_width * head_size), log_totals)


def attend_back(heads_of_query, heads_of_key, heads_of_value, segment_row, out_grad, log_totals):
    sequence_length, kv_local, group_width, head_size = heads_of_query.shape
    score_scale = head_size ** (-0.5)
    number_blocks, rows_per_block, position_index, row_index, row_segment = block_layout(
        heads_of_query, segment_row
    )
    blocks_of_query = heads_of_query.reshape(
        number_blocks, rows_per_block, kv_local, group_width, head_size
    )
    grad_blocks = out_grad.reshape(number_blocks, rows_per_block, kv_local, group_width, head_size)

    def backward_block(running_grads, inputs):
        key_grad, value_grad = running_grads
        query_block, grad_block, block_total, block_index, block_segment = inputs
        scores = score_block(
            query_block,
            heads_of_key,
            block_index,
            block_segment,
            position_index,
            segment_row,
            score_scale,
        )
        prob_block = jnp.exp(scores - block_total[..., None])
        prob_grad = jnp.einsum(
            "qngd,knd->ngqk", grad_block, heads_of_value, preferred_element_type=jnp.float32
        )
        inner_sum = jnp.sum(prob_block * prob_grad, axis=-1, keepdims=True)
        score_grad = (prob_block * (prob_grad - inner_sum)).astype(jnp.bfloat16)
        query_grad = (
            jnp.einsum(
                "ngqk,knd->qngd", score_grad, heads_of_key, preferred_element_type=jnp.float32
            )
            * score_scale
        )
        key_grad = (
            key_grad
            + jnp.einsum(
                "ngqk,qngd->knd", score_grad, query_block, preferred_element_type=jnp.float32
            )
            * score_scale
        )
        value_grad = value_grad + jnp.einsum(
            "ngqk,qngd->knd",
            prob_block.astype(jnp.bfloat16),
            grad_block,
            preferred_element_type=jnp.float32,
        )
        return ((key_grad, value_grad), query_grad)

    zero_keys = jnp.zeros(heads_of_key.shape, jnp.float32)
    (key_grad, value_grad), query_grad = lax.scan(
        backward_block,
        (zero_keys, zero_keys),
        (blocks_of_query, grad_blocks, log_totals, row_index, row_segment),
    )
    return (
        query_grad.reshape(sequence_length, kv_local * group_width, head_size),
        key_grad,
        value_grad,
    )


def general_plan(
    tokens,
    segment_ids,
    attn_gain,
    query_gain,
    key_gain,
    query_weight,
    key_matrix,
    value_matrix,
    out_weight,
    mlp_gain,
    gate_weight,
    up_weight,
    down_weight,
    cotangent,
):
    layer_count = attn_gain.shape[0]
    head_size = query_gain.shape[-1]
    segment_row = segment_ids[0]
    cosine_table, sine_table = rope_tables(positions_of(segment_row), head_size)
    weight_set = (
        query_weight,
        key_matrix,
        value_matrix,
        out_weight,
        gate_weight,
        up_weight,
        down_weight,
    )

    def turn_heads(raw_rows, gain_row):
        return head_norm(raw_rows, gain_row, cosine_table, sine_table)

    residual = tokens.astype(jnp.float32)
    saved_layers = []
    for layer_index in range(layer_count):
        gathered = gather_layer(weight_set, layer_index)
        wide_query, wide_key, wide_value, wide_out, wide_gate, wide_up, wide_down = gathered
        attn_normed, attn_back = jax.vjp(rms_scale, residual, attn_gain[layer_index])
        seq_rows = spread_rows(attn_normed.astype(jnp.bfloat16))
        sequence_length = seq_rows.shape[0]
        query_raw = jnp.dot(seq_rows, wide_query, preferred_element_type=jnp.float32)
        key_raw = jnp.dot(seq_rows, wide_key, preferred_element_type=jnp.float32)
        value_raw = jnp.dot(seq_rows, wide_value, preferred_element_type=jnp.float32)
        query_turned, query_back = jax.vjp(turn_heads, query_raw, query_gain[layer_index])
        key_turned, key_back = jax.vjp(turn_heads, key_raw, key_gain[layer_index])
        kv_local = key_raw.shape[1] // head_size
        heads_of_query = query_turned.astype(jnp.bfloat16).reshape(
            sequence_length, kv_local, -1, head_size
        )
        heads_of_key = key_turned.astype(jnp.bfloat16)
        heads_of_value = value_raw.astype(jnp.bfloat16).reshape(
            sequence_length, kv_local, head_size
        )
        attn_rows, log_totals = attend(heads_of_query, heads_of_key, heads_of_value, segment_row)
        residual_mid = residual + collect_rows(attn_rows, wide_out)
        mlp_normed, mlp_back = jax.vjp(rms_scale, residual_mid, mlp_gain[layer_index])
        mlp_rows = spread_rows(mlp_normed.astype(jnp.bfloat16))
        gate_proj = jnp.dot(mlp_rows, wide_gate, preferred_element_type=jnp.float32)
        upward = jnp.dot(mlp_rows, wide_up, preferred_element_type=jnp.float32)
        hidden_float, swiglu_back = jax.vjp(swiglu, gate_proj, upward)
        hidden = hidden_float.astype(jnp.bfloat16)
        residual = residual_mid + collect_rows(hidden, wide_down)
        saved_layers.append(
            (
                gathered,
                attn_back,
                seq_rows,
                query_back,
                key_back,
                heads_of_query,
                heads_of_key,
                heads_of_value,
                attn_rows,
                log_totals,
                mlp_back,
                mlp_rows,
                swiglu_back,
                hidden,
            )
        )
    result = residual.astype(jnp.bfloat16)
    residual_grad = cotangent.astype(jnp.float32)
    grad_weights = [None] * layer_count
    gain_grads = [None] * layer_count
    for layer_index in reversed(range(layer_count)):
        (
            gathered,
            attn_back,
            seq_rows,
            query_back,
            key_back,
            heads_of_query,
            heads_of_key,
            heads_of_value,
            attn_rows,
            log_totals,
            mlp_back,
            mlp_rows,
            swiglu_back,
            hidden,
        ) = saved_layers[layer_index]
        gathered = gather_layer(weight_set, layer_index)
        wide_query, wide_key, wide_value, wide_out, wide_gate, wide_up, wide_down = gathered
        grad_rows = spread_grads(residual_grad.astype(jnp.bfloat16))
        down_grad = contract_rows(hidden, grad_rows)
        hidden_grad = contract_cols(grad_rows, wide_down)
        gate_grad, upward_grad = swiglu_back(hidden_grad)
        gate_low = gate_grad.astype(jnp.bfloat16)
        upward_low = upward_grad.astype(jnp.bfloat16)
        gate_wgrad = contract_rows(mlp_rows, gate_low)
        upward_wgrad = contract_rows(mlp_rows, upward_low)
        normed_grad = collect_grads(((gate_low, wide_gate), (upward_low, wide_up)))
        residual_part, mlp_gain_grad = mlp_back(normed_grad)
        residual_grad = residual_grad + residual_part
        grad_rows = spread_grads(residual_grad.astype(jnp.bfloat16))
        sequence_length = grad_rows.shape[0]
        out_wgrad = contract_rows(attn_rows, grad_rows)
        mixed_grad = contract_cols(grad_rows, wide_out).astype(jnp.bfloat16)
        query_grad, key_grad, value_grad = attend_back(
            heads_of_query,
            heads_of_key,
            heads_of_value,
            segment_row,
            mixed_grad.reshape(heads_of_query.shape),
            log_totals,
        )
        query_raw_grad, query_gain_grad = query_back(query_grad)
        key_raw_grad, key_gain_grad = key_back(key_grad)
        query_low = query_raw_grad.astype(jnp.bfloat16)
        key_low = key_raw_grad.astype(jnp.bfloat16)
        value_low = value_grad.reshape(sequence_length, -1).astype(jnp.bfloat16)
        query_wgrad = contract_rows(seq_rows, query_low)
        key_wgrad = contract_rows(seq_rows, key_low)
        value_wgrad = contract_rows(seq_rows, value_low)
        normed_grad = collect_grads(
            ((query_low, wide_query), (key_low, wide_key), (value_low, wide_value))
        )
        residual_part, attn_gain_grad = attn_back(normed_grad)
        residual_grad = residual_grad + residual_part
        grad_weights[layer_index] = (
            lax.psum_scatter(
                query_wgrad.astype(jnp.bfloat16), "fsdp", scatter_dimension=0, tiled=True
            ).astype(jnp.float32),
            lax.psum_scatter(
                key_wgrad.astype(jnp.bfloat16), "fsdp", scatter_dimension=0, tiled=True
            ).astype(jnp.float32),
            lax.psum_scatter(
                value_wgrad.astype(jnp.bfloat16), "fsdp", scatter_dimension=0, tiled=True
            ).astype(jnp.float32),
            lax.psum_scatter(
                out_wgrad.astype(jnp.bfloat16), "fsdp", scatter_dimension=1, tiled=True
            ).astype(jnp.float32),
            lax.psum_scatter(
                gate_wgrad.astype(jnp.bfloat16), "fsdp", scatter_dimension=0, tiled=True
            ).astype(jnp.float32),
            lax.psum_scatter(
                upward_wgrad.astype(jnp.bfloat16), "fsdp", scatter_dimension=0, tiled=True
            ).astype(jnp.float32),
            lax.psum_scatter(
                down_grad.astype(jnp.bfloat16), "fsdp", scatter_dimension=1, tiled=True
            ).astype(jnp.float32),
        )
        gain_grads[layer_index] = (attn_gain_grad, query_gain_grad, key_gain_grad, mlp_gain_grad)
    local_stacks = tuple(
        (
            jnp.stack([grad_weights[layer_index][member] for layer_index in range(layer_count)])
            for member in range(7)
        )
    )
    gain_stacks = tuple(
        (
            jnp.stack([gain_grads[layer_index][member] for layer_index in range(layer_count)])
            for member in range(4)
        )
    )
    summed = lax.psum(
        (gain_stacks[0], gain_stacks[1], gain_stacks[2], gain_stacks[3]), ("fsdp", "tp")
    )
    return (
        result,
        residual_grad,
        summed[0],
        summed[1],
        summed[2],
        local_stacks[0],
        local_stacks[1],
        local_stacks[2],
        local_stacks[3],
        summed[3],
        local_stacks[4],
        local_stacks[5],
        local_stacks[6],
    )


def plane_send(values, distance):
    size = lax.axis_size("fsdp")
    return lax.ppermute(values, "fsdp", [(i, i ^ distance) for i in range(size)])


def plane_place():
    return lax.axis_index("fsdp").astype(jnp.int32).reshape(1)


def low(values):
    return values.astype(jnp.bfloat16)


def wide(values):
    return values.astype(jnp.float32)


def add_low(left, right):
    return low(wide(left) + wide(right))


def gather_plane(own, use=None):
    half = own.shape[0] // 2
    near = [own, plane_send(own, 1)]
    made = [use(near, 0)] if use else []
    across_x, across_y, made = lax.optimization_barrier(
        (plane_send(own, 2), plane_send(own, 4), made)
    )
    far = plane_send(across_y[:half], 2), plane_send(across_x[half:], 4)
    across = [across_x, plane_send(across_x, 1), across_y, plane_send(across_y, 1)]
    if use:
        made = made + [use(across, 1)]
    top, bottom, made = lax.optimization_barrier((*far, made))
    last = [top, bottom, plane_send(top, 1), plane_send(bottom, 1)]
    if use:
        return [near, across, last], made + [use(last, 2)]
    return [near, across, last]


def shard_of(sets, d):
    return (sets[0], d) if d < 2 else (sets[1], d - 2) if d < 6 else (sets[2], d - 6)


def reduce_plane(part):
    odd = part((7, 5, 3, 1), None)
    received = [plane_send(v, 1) for v in odd]
    (far,) = part((6,), received[:1])
    half = far.shape[0] // 2
    top, bottom = lax.optimization_barrier(
        (plane_send(far[:half], 2), plane_send(far[half:], 4))
    )
    by_y, by_x, here = part((4, 2, 0), received[1:])
    by_y = jnp.concatenate([add_low(by_y[:half], top), by_y[half:]])
    by_x = jnp.concatenate([by_x[:half], add_low(by_x[half:], bottom)])
    by_x, by_y = lax.optimization_barrier((by_x, by_y))
    from_x = plane_send(by_x, 2)
    from_y = plane_send(by_y, 4)
    return wide(here) + wide(from_x) + wide(from_y), far, by_x


def sum_line(values):
    size = lax.axis_size("tp")
    if size & (size - 1):
        return lax.psum(values, "tp")
    distance = 1
    while distance < size:
        pairs = [(i, i ^ distance) for i in range(size)]
        values = values + lax.ppermute(values, "tp", pairs)
        distance *= 2
    return values


def sum_plane(values):
    for distance in (1, 2, 4):
        values = values + plane_send(values, distance)
    return values


def after(token, *values):
    if token is None:
        return values
    return lax.optimization_barrier((token, *values))[1:]


def line_gather(own, axis=0):
    return lax.all_gather(own, "tp", axis=axis, tiled=True)


def line_reduce(terms, axis=0):
    return lax.psum_scatter(terms, "tp", scatter_dimension=axis, tiled=True)


def assemble(sets, block_shape, axis, places):
    size = sum(len(held) for _, held in sets)
    block = block_shape[axis]
    shape = list(block_shape)
    shape[axis] = size * block

    def kernel(place_ref, *refs):
        out, d = refs[len(sets)], 0
        for (_, held), ref in zip(sets, refs):
            for i in held:
                start = pl.multiple_of(place_ref[d] * block, block)
                where = tuple([slice(None)] * axis + [pl.ds(start, block)])
                out[where] = ref[...] if i is None else ref[i]
                d += 1

    return pl.pallas_call(
        kernel,
        out_shape=jax.ShapeDtypeStruct(tuple(shape), sets[0][0].dtype),
        in_specs=[pl.BlockSpec(memory_space=pltpu.SMEM)]
        + [pl.BlockSpec(memory_space=pltpu.VMEM)] * len(sets),
        out_specs=pl.BlockSpec(memory_space=pltpu.VMEM),
        compiler_params=kernel_params(12),
        cost_estimate=kernel_cost(),
        name="assemble",
    )(places, *(array for array, _ in sets))


def block_at(array, index, block, axis):
    return lax.dynamic_slice_in_dim(array, index * block, block, axis)


def swap(array, axis, into, start=None, done=None, first=None):
    size = lax.axis_size("fsdp")
    places = lax.axis_index("fsdp").astype(jnp.int32) ^ jnp.arange(size, dtype=jnp.int32)
    block = array.shape[axis] // size
    (array,) = after(start, array)
    pieces = [block_at(array, places[d], block, axis) for d in range(size)]
    other = plane_send(jnp.stack(pieces[1::2]), 1)
    if first is not None:
        first.append(other)
    chips = [plane_send(jnp.stack([pieces[d], other[d // 2]]), d) for d in (6, 4, 2)]
    other, *chips = after(done, other[0], *chips)
    sets = [(pieces[0], (None,)), (other, (None,))] + [(v, (0, 1)) for v in reversed(chips)]
    return assemble(sets, pieces[0].shape, into, places)


def line_swap(array, start=None, done=None):
    size = lax.axis_size("tp")
    place = lax.axis_index("tp").astype(jnp.int32)
    block = array.shape[0] // size
    sources = (place - jnp.arange(size, dtype=jnp.int32)) % size
    (array,) = after(start, array)
    moved = []
    for step in range(1, size):
        piece = block_at(array, (place + step) % size, block, 0)
        pairs = [(i, (i + step) % size) for i in range(size)]
        moved.append(lax.ppermute(piece, "tp", pairs))
    moved = after(done, *moved)
    own = block_at(array, place, block, 0)
    return assemble([(v, (None,)) for v in (own, *moved)], own.shape, 0, sources)


def line_rows(rows, start=None, done=None):
    size, line = lax.axis_size("fsdp"), lax.axis_size("tp")
    count, width = rows.shape
    blocks = line_swap(rows, start, done).reshape(line, size // line, count // size, width)
    return blocks.transpose(1, 0, 2, 3).reshape(count, width)


def line_rows_back(rows, start=None, done=None):
    size, line = lax.axis_size("fsdp"), lax.axis_size("tp")
    count, width = rows.shape
    blocks = rows.reshape(size // line, line, count // size, width).transpose(1, 0, 2, 3)
    return line_swap(blocks.reshape(count, width), start, done)


def plane_segments(segment_ids):
    size, line = lax.axis_size("fsdp"), lax.axis_size("tp")
    rows = segment_ids
    for distance in (1, 2, 4):
        rows = jnp.concatenate([rows, plane_send(rows, distance)])
    local = size // line
    wanted = lax.axis_index("tp") * local + jnp.arange(local)
    return rows[wanted ^ lax.axis_index("fsdp")]


def attention_weights(query_shard, key_shard, value_shard, out_shard):
    size, line = lax.axis_size("fsdp"), lax.axis_size("tp")
    per, depth = size // line, query_shard.shape[0]
    pack = jnp.concatenate(
        [
            query_shard.T.reshape(per, -1, depth),
            key_shard.T.reshape(per, -1, depth),
            value_shard.T.reshape(per, -1, depth),
            out_shard.reshape(per, -1, depth),
        ],
        axis=1,
    )
    gathered = line_gather(pack)
    return swap(gathered, 0, 2)[0], gathered


def turn(values, cosine, sine):
    return values * cosine + pltpu.roll(values, values.shape[1] // 2, 1) * sine


def turn_back(values, cosine, sine):
    return values * cosine - pltpu.roll(values, values.shape[1] // 2, 1) * sine


def inverse_rms(values):
    return lax.rsqrt(jnp.mean(values * values, axis=-1, keepdims=True) + EPSILON)


def rows_in_order(place, groups, target, pick):
    shards = [(ref, e) for ref in groups for e in range(ref.shape[0])]
    for d, (ref, e) in enumerate(shards):
        blocks, block = ref.shape[2], ref.shape[3]
        for i in range(blocks):
            start = pl.multiple_of((i * len(shards) + (place ^ d)) * block, block)
            target[pl.ds(start, block), :] = pick(ref[e, 0, i])


def rows_from_order(place, source, groups):
    shards = [(ref, e) for ref in groups for e in range(ref.shape[0])]
    for d, (ref, e) in enumerate(shards):
        blocks, block = ref.shape[2], ref.shape[3]
        for i in range(blocks):
            start = pl.multiple_of((i * len(shards) + (place ^ d)) * block, block)
            ref[e, 0, i] = source[pl.ds(start, block), :].astype(ref.dtype)


def head_columns(index, head):
    return slice(index * head, (index + 1) * head)


def heads_from_raw(nat, cos_ref, sin_ref, gains, heads, low_ref, rows):
    head = cos_ref.shape[-1]
    for start in range(0, nat.shape[0], rows):
        here = slice(start, start + rows)
        cosine, sine = cos_ref[0, here, :], sin_ref[0, here, :]
        for h in range(heads + 2):
            raw = nat[here, head_columns(h, head)]
            if h <= heads:
                gain = gains[0] if h < heads else gains[1]
                raw = turn(raw * inverse_rms(raw) * gain[...], cosine, sine)
            low_ref[here, head_columns(h, head)] = raw.astype(low_ref.dtype)


def block_operands(low_ref, start, rows, heads, head):
    query = jnp.concatenate(
        [low_ref[start : start + rows, head_columns(h, head)] for h in range(heads)], axis=0
    )
    key = low_ref[: start + rows, head_columns(heads, head)]
    value = low_ref[: start + rows, head_columns(heads + 1, head)]
    return query, key, value


def masked_scores(key, query, first_ref, start, rows, heads, scale):
    scores = lax.dot_general(
        key, query, (((1,), (1,)), ((), ())), preferred_element_type=jnp.float32
    )
    shape = (key.shape[0], rows)
    index = lax.broadcasted_iota(jnp.int32, shape, 0)
    mine = lax.broadcasted_iota(jnp.int32, shape, 1) + start
    first = first_ref[0, :, start : start + rows]
    allowed = (index <= mine) & (index >= first)
    allowed = jnp.concatenate([allowed] * heads, axis=1)
    return jnp.where(allowed, scores * scale, -1e30)


def attend_kernel(groups, heads, rows, *refs):
    place = refs[0][0]
    raw_refs = refs[1 : 1 + groups]
    cos_ref, sin_ref, first_ref, query_gain, key_gain = refs[1 + groups : 6 + groups]
    out_refs = refs[6 + groups : 6 + 2 * groups]
    total_ref, nat, low_ref, mixed = refs[6 + 2 * groups :]
    head = cos_ref.shape[-1]
    rows_in_order(place, raw_refs, nat, lambda v: v)
    heads_from_raw(nat, cos_ref, sin_ref, (query_gain, key_gain), heads, low_ref, rows)
    for i in range(nat.shape[0] // rows):
        start = i * rows
        query, key, value = block_operands(low_ref, start, rows, heads, head)
        scores = masked_scores(key, query, first_ref, start, rows, heads, head ** (-0.5))
        top = jnp.max(scores, axis=0, keepdims=True)
        weights = jnp.exp(scores - top)
        total = jnp.sum(weights, axis=0, keepdims=True)
        total_ref[0, i : i + 1, :] = top + jnp.log(total)
        prob = (weights * (1.0 / total)).astype(jnp.bfloat16)
        out = lax.dot_general(
            prob, value, (((0,), (0,)), ((), ())), preferred_element_type=jnp.float32
        ).astype(jnp.bfloat16)
        for h in range(heads):
            mixed[start : start + rows, head_columns(h, head)] = out[h * rows : (h + 1) * rows]
    rows_from_order(place, mixed, out_refs)


def attend_back_kernel(groups, heads, rows, *refs):
    place = refs[0][0]
    raw_refs = refs[1 : 1 + groups]
    grad_refs = refs[1 + groups : 1 + 2 * groups]
    rest = refs[1 + 2 * groups :]
    total_ref, cos_ref, sin_ref, first_ref, query_gain, key_gain = rest[:6]
    out_refs = rest[6 : 6 + groups]
    gain_ref, nat, low_ref, mixed, grads, key_sum, value_sum, done = rest[6 + groups :]
    head = cos_ref.shape[-1]
    scale = head ** (-0.5)
    rows_in_order(place, raw_refs, nat, lambda v: v)
    rows_in_order(place, grad_refs, mixed, lambda v: v)
    heads_from_raw(nat, cos_ref, sin_ref, (query_gain, key_gain), heads, low_ref, rows)
    key_sum[...] = jnp.zeros_like(key_sum)
    value_sum[...] = jnp.zeros_like(value_sum)
    for i in range(nat.shape[0] // rows):
        start = i * rows
        stop = start + rows
        query, key, value = block_operands(low_ref, start, rows, heads, head)
        out_grad = jnp.concatenate(
            [mixed[start:stop, head_columns(h, head)] for h in range(heads)], axis=0
        )
        scores = masked_scores(key, query, first_ref, start, rows, heads, scale)
        prob = jnp.exp(scores - total_ref[0, i : i + 1, :])
        prob_grad = lax.dot_general(
            value, out_grad, (((1,), (1,)), ((), ())), preferred_element_type=jnp.float32
        )
        inner = jnp.sum(prob * prob_grad, axis=0, keepdims=True)
        score_grad = (prob * (prob_grad - inner)).astype(jnp.bfloat16)
        value_sum[:stop, :] += jnp.dot(
            prob.astype(jnp.bfloat16), out_grad, preferred_element_type=jnp.float32
        )
        key_sum[:stop, :] += jnp.dot(score_grad, query, preferred_element_type=jnp.float32)
        query_grad = lax.dot_general(
            score_grad, key, (((0,), (0,)), ((), ())), preferred_element_type=jnp.float32
        )
        for h in range(heads):
            grads[start:stop, head_columns(h, head)] = query_grad[h * rows : (h + 1) * rows] * scale
    sums = [jnp.zeros((1, head), jnp.float32)] * 2
    for start in range(0, nat.shape[0], rows):
        here = slice(start, start + rows)
        cosine, sine = cos_ref[0, here, :], sin_ref[0, here, :]
        for h in range(heads + 1):
            kind = 0 if h < heads else 1
            gain = (query_gain, key_gain)[kind][...]
            grad = grads[here, head_columns(h, head)] if h < heads else key_sum[here, :] * scale
            raw = nat[here, head_columns(h, head)]
            inverse = inverse_rms(raw)
            grad = turn_back(grad, cosine, sine)
            sums[kind] += jnp.sum(grad * raw * inverse, axis=0, keepdims=True)
            grad = grad * gain
            middle = jnp.mean(grad * raw, axis=-1, keepdims=True)
            done[here, head_columns(h, head)] = (
                inverse * grad - raw * (inverse * inverse * inverse) * middle
            ).astype(done.dtype)
        done[here, head_columns(heads + 1, head)] = value_sum[here, :].astype(done.dtype)
    gain_ref[0] = jnp.concatenate(sums, axis=0)
    rows_from_order(place, done, out_refs)


def kernel_cost(flops=1024):
    return pl.CostEstimate(flops=flops // 2, bytes_accessed=1024, transcendentals=0)


def kernel_params(mib=48):
    return pltpu.CompilerParams(vmem_limit_bytes=mib * 1024 * 1024)


def group_specs(arrays):
    def spec(array):
        return pl.BlockSpec((array.shape[0], 1) + array.shape[2:], lambda s: (0, s, 0, 0, 0))

    return [spec(array) for array in arrays]


def table_specs(length, head):
    table = pl.BlockSpec((1, length, head), lambda s: (s, 0, 0))
    gain = pl.BlockSpec((1, head), lambda s: (0, 0))
    return [table, table, pl.BlockSpec((1, 1, length), lambda s: (s, 0, 0)), gain, gain]


def grouped(rows, shards, local, blocks):
    count, width = rows.shape
    return rows.reshape(shards, local, blocks, count // (shards * local * blocks), width)


def plane_attend(raw, tables, first, gains, rows=256):
    local, length, head = tables[0].shape
    width = raw[0].shape[-1]
    heads = width // head - 2
    groups = len(raw)
    outs = [jax.ShapeDtypeStruct(v.shape[:-1] + (heads * head,), jnp.bfloat16) for v in raw]
    totals = jax.ShapeDtypeStruct((local, length // rows, heads * rows), jnp.float32)
    out = pl.pallas_call(
        functools.partial(attend_kernel, groups, heads, rows),
        grid=(local,),
        out_shape=outs + [totals],
        in_specs=[pl.BlockSpec(memory_space=pltpu.SMEM)]
        + group_specs(raw)
        + table_specs(length, head),
        out_specs=group_specs(outs)
        + [pl.BlockSpec((1,) + totals.shape[1:], lambda s: (s, 0, 0))],
        scratch_shapes=[
            pltpu.VMEM((length, width), jnp.float32),
            pltpu.VMEM((length, width), jnp.bfloat16),
            pltpu.VMEM((length, heads * head), jnp.bfloat16),
        ],
        compiler_params=kernel_params(24),
        cost_estimate=kernel_cost(local * heads * length * length * head * 8),
        name="attend",
    )(plane_place(), *raw, *tables, first, *gains)
    return out[:groups], out[groups]


def plane_attend_back(raw, out_grad, totals, tables, first, gains, rows=256):
    local, length, head = tables[0].shape
    width = raw[0].shape[-1]
    heads = width // head - 2
    groups = len(raw)
    out = pl.pallas_call(
        functools.partial(attend_back_kernel, groups, heads, rows),
        grid=(local,),
        out_shape=[jax.ShapeDtypeStruct(v.shape, jnp.bfloat16) for v in raw]
        + [jax.ShapeDtypeStruct((local, 2, head), jnp.float32)],
        in_specs=[pl.BlockSpec(memory_space=pltpu.SMEM)]
        + group_specs(raw)
        + group_specs(out_grad)
        + [pl.BlockSpec((1,) + totals.shape[1:], lambda s: (s, 0, 0))]
        + table_specs(length, head),
        out_specs=group_specs(raw) + [pl.BlockSpec((1, 2, head), lambda s: (s, 0, 0))],
        scratch_shapes=[
            pltpu.VMEM((length, width), jnp.float32),
            pltpu.VMEM((length, width), jnp.bfloat16),
            pltpu.VMEM((length, heads * head), jnp.bfloat16),
            pltpu.VMEM((length, heads * head), jnp.float32),
            pltpu.VMEM((length, head), jnp.float32),
            pltpu.VMEM((length, head), jnp.float32),
            pltpu.VMEM((length, width), jnp.bfloat16),
        ],
        compiler_params=kernel_params(32),
        cost_estimate=kernel_cost(local * heads * length * length * head * 16),
        name="attend_back",
    )(plane_place(), *raw, *out_grad, totals, *tables, first, *gains)
    return out[:groups], jnp.sum(out[groups], axis=0)


def whole_spec(array):
    return pl.BlockSpec(
        array.shape, lambda n: (0,) * array.ndim, pipeline_mode=pl.Buffered(buffer_count=1)
    )


def dot_cols(left, right):
    return lax.dot_general(
        left, right, (((1,), (1,)), ((), ())), preferred_element_type=jnp.float32
    )


def joined(refs, rows_ref):
    @pl.when(pl.program_id(0) == 0)
    def _():
        start = 0
        for ref in refs:
            rows_ref[start : start + ref.shape[0], :] = ref[...]
            start += ref.shape[0]

    return rows_ref[...]


def joined_scratch(pieces):
    count = sum(v.shape[0] for v in pieces)
    return [pltpu.VMEM((count, pieces[0].shape[1]), pieces[0].dtype)]


def project_kernel(count, *refs):
    weight, out, rows_ref = refs[count:]
    out[...] = dot_cols(joined(refs[:count], rows_ref), weight[...]).astype(out.dtype)


def project(pieces, weight, first, width, dtype, tile=256):
    count = sum(v.shape[0] for v in pieces)
    return pl.pallas_call(
        functools.partial(project_kernel, len(pieces)),
        grid=(width // tile,),
        out_shape=jax.ShapeDtypeStruct((count, width), dtype),
        in_specs=[whole_spec(v) for v in pieces]
        + [pl.BlockSpec((tile, weight.shape[1]), lambda n: (first // tile + n, 0))],
        out_specs=pl.BlockSpec((count, tile), lambda n: (0, n)),
        scratch_shapes=joined_scratch(pieces),
        compiler_params=kernel_params(16),
        cost_estimate=kernel_cost(2 * count * width * weight.shape[1]),
        name="project",
    )(*pieces, weight)


def units_kernel(count, *refs):
    gate_rows, up_rows, hidden_ref, gate_ref, up_ref, rows_ref = refs[count:]
    rows = joined(refs[:count], rows_ref)
    gate = dot_cols(rows, gate_rows[0])
    up = dot_cols(rows, up_rows[0])
    hidden_ref[...] = (gate * up / (1.0 + jnp.exp(-gate))).astype(hidden_ref.dtype)
    gate_ref[...] = gate.astype(gate_ref.dtype)
    up_ref[...] = up.astype(up_ref.dtype)


def unit_spec(weights, kind, tile):
    return pl.BlockSpec((1, tile, weights.shape[2]), lambda n: (kind, n, 0))


def hidden_units(pieces, weights, tile=256):
    count = sum(v.shape[0] for v in pieces)
    shape = jax.ShapeDtypeStruct((count, weights.shape[1]), jnp.bfloat16)
    return pl.pallas_call(
        functools.partial(units_kernel, len(pieces)),
        grid=(weights.shape[1] // tile,),
        out_shape=[shape] * 3,
        in_specs=[whole_spec(v) for v in pieces]
        + [unit_spec(weights, kind, tile) for kind in (0, 1)],
        out_specs=[pl.BlockSpec((count, tile), lambda n: (0, n))] * 3,
        scratch_shapes=joined_scratch(pieces),
        compiler_params=kernel_params(20),
        cost_estimate=kernel_cost(4 * count * weights.shape[1] * weights.shape[2]),
        name="hidden_units",
    )(*pieces, weights, weights)


def units_back_kernel(count, *refs):
    down_rows, gate_ref, up_ref, gate_grad, up_grad, rows_ref = refs[count:]
    grad = dot_cols(joined(refs[:count], rows_ref), down_rows[0])
    gate, up = wide(gate_ref[...]), wide(up_ref[...])
    sigmoid = 1.0 / (1.0 + jnp.exp(-gate))
    gate_grad[...] = (grad * up * sigmoid * (1.0 + gate * (1.0 - sigmoid))).astype(gate_grad.dtype)
    up_grad[...] = (grad * gate * sigmoid).astype(up_grad.dtype)


def hidden_units_back(pieces, weights, gate, up, tile=256):
    count = gate.shape[0]
    side = pl.BlockSpec((count, tile), lambda n: (0, n))
    return pl.pallas_call(
        functools.partial(units_back_kernel, len(pieces)),
        grid=(weights.shape[1] // tile,),
        out_shape=[jax.ShapeDtypeStruct(gate.shape, jnp.bfloat16)] * 2,
        in_specs=[whole_spec(v) for v in pieces] + [unit_spec(weights, 2, tile), side, side],
        out_specs=[side, side],
        scratch_shapes=joined_scratch(pieces),
        compiler_params=kernel_params(20),
        cost_estimate=kernel_cost(2 * count * weights.shape[1] * weights.shape[2]),
        name="hidden_units_back",
    )(*pieces, weights, gate, up)


def parts_kernel(shards, terms, adding, *refs):
    lefts, weights = refs[: shards * terms], refs[shards * terms : (shards + 1) * terms]
    adds = refs[(shards + 1) * terms : -shards]
    outs = refs[-shards:]
    total = None
    for t in range(terms):
        weight = weights[t][...]
        left = jnp.concatenate([lefts[i * terms + t][...] for i in range(shards)], axis=0)
        term = jnp.dot(
            left, weight.reshape(weight.shape[-2:]), preferred_element_type=jnp.float32
        )
        total = term if total is None else total + term
    rows = outs[0].shape[0]
    for i in range(shards):
        mine = total[i * rows : (i + 1) * rows]
        if adding:
            mine = mine + wide(adds[i][...])
        outs[i][...] = mine.astype(outs[i].dtype)


def parts_of(terms, ds, adds, tile=512):
    lefts, specs = [], []
    for d in ds:
        for sets, _, _ in terms:
            array, place = shard_of(sets, d)
            rows = sets[0].shape[0] // 2
            lefts.append(array)
            specs.append(
                pl.BlockSpec(
                    (rows, array.shape[1]),
                    lambda n, p=place: (p, 0),
                    pipeline_mode=pl.Buffered(buffer_count=1),
                )
            )
    width = terms[0][1].shape[-1]
    side = pl.BlockSpec((rows, tile), lambda n: (0, n))
    return pl.pallas_call(
        functools.partial(parts_kernel, len(ds), len(terms), adds is not None),
        grid=(width // tile,),
        out_shape=[jax.ShapeDtypeStruct((rows, width), jnp.bfloat16)] * len(ds),
        in_specs=specs + [spec for _, _, spec in terms] + [side] * len(adds or ()),
        out_specs=[side] * len(ds),
        compiler_params=kernel_params(16),
        cost_estimate=kernel_cost(2 * len(ds) * rows * width * sum(v.shape[-1] for v in lefts[: len(terms)])),
        name="parts",
    )(*lefts, *(weights for _, weights, _ in terms), *(adds or ()))


def rows_spec(kind, weights, tile=512):
    return pl.BlockSpec((1, weights.shape[1], tile), lambda n: (kind, 0, n))


def pack_spec(block, height, tile=512):
    return pl.BlockSpec((height, tile), lambda n: (block, n))


def outer_kernel(plan, *refs):
    for lefts, rights, place in plan:
        total = None
        for left, pieces in zip(lefts, rights):
            right = jnp.concatenate([refs[p][...] for p in pieces], axis=0)
            term = lax.dot_general(
                refs[left][...], right, (((0,), (0,)), ((), ())), preferred_element_type=jnp.float32
            )
            total = term if total is None else total + term
        refs[-1][place] = total.astype(refs[-1].dtype)


def outer(products, shape, tile=512):
    operands, specs, plan, seen = [], [], [], {}

    def operand(array, split):
        if id(array) not in seen:
            seen[id(array)] = len(operands)
            operands.append(array)
            specs.append(
                pl.BlockSpec((array.shape[0], tile), lambda n: (0, n))
                if split
                else pl.BlockSpec(
                    array.shape, lambda n: (0, 0), pipeline_mode=pl.Buffered(buffer_count=1)
                )
            )
        return seen[id(array)]

    for lefts, rights, place in products:
        plan.append(
            (
                [operand(v, False) for v in lefts],
                [[operand(v, True) for v in pieces] for pieces in rights],
                place,
            )
        )
    block = shape[:-1] + (tile,)
    return pl.pallas_call(
        functools.partial(outer_kernel, plan),
        grid=(shape[-1] // tile,),
        out_shape=jax.ShapeDtypeStruct(shape, jnp.bfloat16),
        in_specs=specs,
        out_specs=pl.BlockSpec(block, lambda n: (0,) * (len(shape) - 1) + (n,)),
        compiler_params=kernel_params(56),
        cost_estimate=kernel_cost(2 * shape[-1] * sum(v.size for lefts, _, _ in products for v in lefts)),
        name="outer",
    )(*operands)


def plane_plan(
    tokens,
    segment_ids,
    attn_gain,
    query_gain,
    key_gain,
    query_weight,
    key_matrix,
    value_matrix,
    out_weight,
    mlp_gain,
    gate_weight,
    up_weight,
    down_weight,
    cotangent,
):
    layers = attn_gain.shape[0]
    head = query_gain.shape[-1]
    size, line = lax.axis_size("fsdp"), lax.axis_size("tp")
    local = size // line
    segments = plane_segments(segment_ids)
    length = segments.shape[1]
    positions = jax.vmap(positions_of)(segments)
    first = (jnp.arange(length, dtype=jnp.int32)[None] - positions).reshape(local, 1, length)
    cosine_table, sine_table = rope_tables(positions.reshape(-1), head)
    turned_sign = jnp.where(jnp.arange(head) < head // 2, -1.0, 1.0)
    tables = (
        cosine_table.reshape(local, length, head),
        (sine_table * turned_sign).reshape(local, length, head),
    )
    query_count = query_weight.shape[2] * line // size
    key_count = key_matrix.shape[2] * line // size
    split = query_count + 2 * key_count

    def group(sets):
        counts = [v.shape[0] * size // sum(u.shape[0] for u in sets) for v in sets]
        return [grouped(v, count, local, line) for v, count in zip(sets, counts)]

    def flat(sets):
        return [v.reshape(-1, v.shape[-1]) for v in sets]

    def hold(token, sets):
        return [list(after(token, *v)) for v in sets]

    def reduce_down(hidden, weights):
        term = (hidden, weights, rows_spec(2, weights))
        return reduce_plane(lambda ds, adds: parts_of([term], ds, adds))[0]

    attn_sets, attn_gathered, hidden_sets = ([None] * layers for _ in range(3))

    def fetch_attn(index, token):
        shards = (query_weight[index], key_matrix[index], value_matrix[index], out_weight[index])
        attn_sets[index], attn_gathered[index] = attention_weights(*after(token, *shards))

    fetch_attn(0, None)
    exchanged = []
    both = jnp.concatenate([tokens, cotangent], axis=1)
    both = swap(both, 0, 0, None, None, exchanged)
    hidden_shards = jnp.stack(
        [gate_weight.swapaxes(1, 2), up_weight.swapaxes(1, 2), down_weight], axis=1
    ).reshape(-1, *down_weight.shape[1:])
    both = line_rows(both)
    hidden_shards, first = lax.optimization_barrier((hidden_shards, first))
    hidden_shards = swap(hidden_shards, 1, 2, exchanged[0], both)
    hidden_shards = hidden_shards.reshape(layers, -1, *hidden_shards.shape[1:])
    residual, grad = wide(both[:, : tokens.shape[1]]), wide(both[:, tokens.shape[1] :])
    saved = []
    for index in range(layers):
        pack = attn_sets[index]
        gains = (query_gain[index][None], key_gain[index][None])
        normed, attn_back = jax.vjp(rms_scale, residual, attn_gain[index])
        rows = gather_plane(low(normed))
        if index == 0:
            hidden_sets[0] = line_gather(after(attn_gathered[0], hidden_shards[0])[0], 1)
        raw = group([project(v, pack, 0, split, jnp.float32) for v in rows])
        if index + 1 < layers:
            fetch_attn(index + 1, raw[0])
        mixed, totals = plane_attend(raw, tables, first, gains)
        mixed = flat(mixed)
        out_term = (mixed, pack, pack_spec(split // query_count, query_count))
        total, *_ = reduce_plane(lambda ds, adds: parts_of([out_term], ds, adds))
        middle = residual + total
        weights = hidden_sets[index]
        normed, mlp_back = jax.vjp(rms_scale, middle, mlp_gain[index])
        mlp_rows = gather_plane(low(normed))
        hidden, gates, ups = zip(*(hidden_units(v, weights) for v in mlp_rows))
        if index + 1 < layers:
            hidden_sets[index + 1] = line_gather(
                after(mlp_rows[2][0], hidden_shards[index + 1])[0], 1
            )
        if index + 1 < layers:
            residual = middle + reduce_down(hidden, weights)
        else:
            residual = middle
        saved.append(
            (attn_back, rows, raw, mixed, totals, mlp_back, mlp_rows, gates, ups, hidden)
        )
    pack_grads, pack_sums, gain_grads, hidden_sums, hidden_grads = (
        [None] * layers for _ in range(5)
    )
    for index in reversed(range(layers)):
        pack = attn_sets[index]
        gains = (query_gain[index][None], key_gain[index][None])
        weights = hidden_sets[index]
        attn_back, rows, raw, mixed, totals = saved[index][:5]
        mlp_back, mlp_rows, gates, ups, hidden = saved[index][5:]
        if index + 1 == layers:
            (grad,) = after(tuple(mlp_rows[2]), grad)
        grad_rows, unit_grads = gather_plane(
            low(grad), lambda v, i: hidden_units_back(v, weights, gates[i], ups[i])
        )
        gate_grads, up_grads = zip(*unit_grads)
        unit_terms = [
            (gate_grads, weights, rows_spec(0, weights)),
            (up_grads, weights, rows_spec(1, weights)),
        ]
        normed_grad, token, *_ = reduce_plane(
            lambda ds, adds: parts_of(unit_terms, ds, adds)
        )
        (held,) = after(token, gate_grads[0])
        terms = outer(
            [
                ((held, *gate_grads[1:]), mlp_rows, 0),
                (up_grads, mlp_rows, 1),
                (hidden, grad_rows, 2),
            ],
            weights.shape,
        )
        normed_grad, terms = lax.optimization_barrier((normed_grad, terms))
        if index + 1 < layers:
            done = hidden_sums[index + 1]
            above = swap(pack_grads[index + 1][None], 2, 0, gate_grads[1])
            pack_sums[index + 1] = line_reduce(after(done, above)[0])
            (terms,) = after(pack_sums[index + 1], terms)
        hidden_sums[index] = line_reduce(terms, 1)
        grad_part, mlp_gain_grad = mlp_back(normed_grad)
        grad = grad + grad_part
        grad_rows, mixed_grad = gather_plane(
            low(grad), lambda v, i: project(v, pack, split, query_count, jnp.bfloat16)
        )
        mixed_grad = group(mixed_grad)
        raw_grad, head_gain_grads = plane_attend_back(raw, mixed_grad, totals, tables, first, gains)
        raw_grad = flat(raw_grad)
        if index + 1 == layers:
            result = residual + reduce_down(after(normed_grad, *hidden), weights)
            result, *raw_grad = lax.optimization_barrier((result, *raw_grad))
        if index + 1 < layers:
            hidden_grads[index + 1] = swap(hidden_sums[index + 1], 2, 1, mixed_grad[2])
            hidden_grads[index + 1], *raw_grad = lax.optimization_barrier(
                (hidden_grads[index + 1], *raw_grad)
            )
        raw_term = (raw_grad, pack, pack_spec(0, split))
        normed_grad, token, *_ = reduce_plane(
            lambda ds, adds: parts_of([raw_term], ds, adds)
        )
        (held,) = after(token, mixed[0])
        pack_grad = outer(
            [
                (raw_grad, rows, slice(0, split)),
                ((held, *mixed[1:]), grad_rows, slice(split, split + query_count)),
            ],
            pack.shape,
        )
        normed_grad, pack_grad = lax.optimization_barrier((normed_grad, pack_grad))
        pack_grads[index] = pack_grad
        grad_part, attn_gain_grad = attn_back(normed_grad)
        grad = grad + grad_part
        gain_grads[index] = jnp.concatenate(
            [attn_gain_grad, mlp_gain_grad, head_gain_grads[0], head_gain_grads[1]]
        )
    below = swap(pack_grads[0][None], 2, 0)
    pack_sums[0] = line_reduce(after((hidden_sums[0], pack_sums[1:]), below)[0])
    both = jnp.concatenate([low(result), low(grad)], axis=1)
    gain_stack = sum_line(jnp.stack(gain_grads).reshape(-1, head))
    both, gain_stack = lax.optimization_barrier((both, gain_stack))
    both = line_rows_back(both, below)
    gain_stack = sum_plane(gain_stack)
    hidden_grads[0] = swap(hidden_sums[0], 2, 1, below)
    both = swap(both, 0, 0)
    result, token_grad = both[:, : tokens.shape[1]], wide(both[:, tokens.shape[1] :])
    kinds = wide(jnp.stack(hidden_grads, 1))
    hidden_stacks = (kinds[0].swapaxes(1, 2), kinds[1].swapaxes(1, 2), kinds[2])
    marks = (0, query_count, query_count + key_count, split, pack_sums[0].shape[1])
    kinds = [
        jnp.stack(
            [wide(v[:, low_mark:high_mark]).reshape(-1, v.shape[-1]) for v in pack_sums]
        )
        for low_mark, high_mark in zip(marks, marks[1:])
    ]
    weight_stacks = [v.swapaxes(1, 2) for v in kinds[:3]] + kinds[3:]
    width = attn_gain.shape[1]
    gain_stack = gain_stack.reshape(layers, -1)
    attn_sum, mlp_sum, query_sum, key_sum = (
        gain_stack[:, :width],
        gain_stack[:, width : 2 * width],
        gain_stack[:, 2 * width : 2 * width + head],
        gain_stack[:, 2 * width + head :],
    )
    return (
        result,
        token_grad,
        attn_sum,
        query_sum,
        key_sum,
        *weight_stacks,
        mlp_sum,
        *hidden_stacks,
    )


def plane_fits(mesh, shapes):
    size, line = mesh.shape["fsdp"], mesh.shape["tp"]
    heads = shapes[6].shape[2] // shapes[4].shape[1]
    return size == 8 and heads == size and size % line == 0 and shapes[1].shape[0] == size


def solution(mesh):
    placed = (
        P(("fsdp", "tp"), None),
        P("fsdp", None),
        P(),
        P(),
        P(),
        P(None, "fsdp", "tp"),
        P(None, "fsdp", "tp"),
        P(None, "fsdp", "tp"),
        P(None, "tp", "fsdp"),
        P(),
        P(None, "fsdp", "tp"),
        P(None, "fsdp", "tp"),
        P(None, "tp", "fsdp"),
        P(("fsdp", "tp"), None),
    )
    def mapped(plan):
      return jax.shard_map(
        plan,
        mesh=mesh,
        in_specs=placed,
        out_specs=(
            P(("fsdp", "tp"), None),
            P(("fsdp", "tp"), None),
            P(),
            P(),
            P(),
            P(None, "fsdp", "tp"),
            P(None, "fsdp", "tp"),
            P(None, "fsdp", "tp"),
            P(None, "tp", "fsdp"),
            P(),
            P(None, "fsdp", "tp"),
            P(None, "fsdp", "tp"),
            P(None, "tp", "fsdp"),
        ),
        check_vma=False,
    )

    def whole(*args):
        return mapped(plane_plan if plane_fits(mesh, args) else general_plan)(*args)

    return whole
```

```python
import functools
import math

import jax
import jax.numpy as jnp
from jax import lax
from jax.experimental import pallas as pl
from jax.experimental.pallas import tpu as pltpu
from jax.sharding import PartitionSpec as P

EPSILON = 1e-06
ROPE_BASE = 1000000.0


def rms_scale(values, gain_row):
    return (
        values * lax.rsqrt(jnp.mean(values * values, axis=-1, keepdims=True) + EPSILON) * gain_row
    )


def positions_of(segment_row):
    sequence_length = segment_row.shape[0]
    position_index = jnp.arange(sequence_length, dtype=jnp.int32)
    starts = jnp.concatenate([jnp.ones((1,), dtype=jnp.bool_), segment_row[1:] != segment_row[:-1]])
    first_index = lax.cummax(
        jnp.where(starts, position_index, jnp.zeros_like(position_index)), axis=0
    )
    return position_index - first_index


def rope_tables(positions, head_size):
    half_size = head_size // 2
    steps_float = jnp.arange(half_size, dtype=jnp.float32)
    inverse = jnp.exp(steps_float * (-2.0 * math.log(ROPE_BASE) / head_size))
    angles = positions.astype(jnp.float32)[:, None] * inverse[None, :]
    angles = jnp.concatenate([angles, angles], axis=-1)
    return (jnp.cos(angles), jnp.sin(angles))


def rotate(values, cosine_table, sine_table):
    half_size = values.shape[-1] // 2
    turned = jnp.concatenate([-values[..., half_size:], values[..., :half_size]], axis=-1)
    return values * cosine_table[:, None, :] + turned * sine_table[:, None, :]


def head_norm(raw_rows, gain_row, cosine_table, sine_table):
    head_size = gain_row.shape[-1]
    shaped = raw_rows.reshape(raw_rows.shape[0], raw_rows.shape[1] // head_size, head_size)
    return rotate(rms_scale(shaped, gain_row), cosine_table, sine_table)


def swiglu(gate_proj, upward):
    return jax.nn.silu(gate_proj) * upward


def contract_rows(left_side, right_side):
    return lax.dot_general(
        left_side, right_side, (((0,), (0,)), ((), ())), preferred_element_type=jnp.float32
    )


def contract_cols(left_side, right_side):
    return lax.dot_general(
        left_side, right_side, (((1,), (1,)), ((), ())), preferred_element_type=jnp.float32
    )


def spread_rows(rows_low):
    return lax.all_gather(rows_low, "tp", axis=0, tiled=True)


def spread_grads(grad_low):
    return lax.all_gather(grad_low, "tp", axis=0, tiled=True)


def collect_rows(left_side, right_side):
    return lax.psum_scatter(
        jnp.dot(left_side, right_side, preferred_element_type=jnp.float32).astype(jnp.bfloat16),
        "tp",
        scatter_dimension=0,
        tiled=True,
    ).astype(jnp.float32)


def collect_grads(pairs_list):
    running = None
    for left_side, right_side in pairs_list:
        product = contract_cols(left_side, right_side)
        running = product if running is None else running + product
    return lax.psum_scatter(
        running.astype(jnp.bfloat16), "tp", scatter_dimension=0, tiled=True
    ).astype(jnp.float32)


def gather_layer(weight_set, layer_index):
    query_weight, key_matrix, value_matrix, out_weight, gate_weight, up_weight, down_weight = (
        weight_set
    )
    return (
        lax.all_gather(query_weight[layer_index], "fsdp", axis=0, tiled=True),
        lax.all_gather(key_matrix[layer_index], "fsdp", axis=0, tiled=True),
        lax.all_gather(value_matrix[layer_index], "fsdp", axis=0, tiled=True),
        lax.all_gather(out_weight[layer_index], "fsdp", axis=1, tiled=True),
        lax.all_gather(gate_weight[layer_index], "fsdp", axis=0, tiled=True),
        lax.all_gather(up_weight[layer_index], "fsdp", axis=0, tiled=True),
        lax.all_gather(down_weight[layer_index], "fsdp", axis=1, tiled=True),
    )


def score_block(
    query_block, heads_of_key, block_index, block_segment, position_index, segment_row, score_scale
):
    raw_dots = jnp.einsum(
        "qngd,knd->ngqk", query_block, heads_of_key, preferred_element_type=jnp.float32
    )
    allowed = (position_index[None, :] <= block_index[:, None]) & (
        segment_row[None, :] == block_segment[:, None]
    )
    return jnp.where(allowed[None, None], raw_dots * score_scale, -1e30)


def block_layout(heads_of_query, segment_row):
    sequence_length, kv_local, group_width, head_size = heads_of_query.shape
    rows_per_block = min(512, sequence_length)
    number_blocks = sequence_length // rows_per_block
    position_index = jnp.arange(sequence_length, dtype=jnp.int32)
    row_index = position_index.reshape(number_blocks, rows_per_block)
    row_segment = segment_row.reshape(number_blocks, rows_per_block)
    return (number_blocks, rows_per_block, position_index, row_index, row_segment)


def attend(heads_of_query, heads_of_key, heads_of_value, segment_row):
    sequence_length, kv_local, group_width, head_size = heads_of_query.shape
    score_scale = head_size ** (-0.5)
    number_blocks, rows_per_block, position_index, row_index, row_segment = block_layout(
        heads_of_query, segment_row
    )
    blocks_of_query = heads_of_query.reshape(
        number_blocks, rows_per_block, kv_local, group_width, head_size
    )

    def forward_block(inputs):
        query_block, block_index, block_segment = inputs
        scores = score_block(
            query_block,
            heads_of_key,
            block_index,
            block_segment,
            position_index,
            segment_row,
            score_scale,
        )
        top_score = jnp.max(scores, axis=-1, keepdims=True)
        weights = jnp.exp(scores - top_score)
        total_weight = jnp.sum(weights, axis=-1, keepdims=True)
        prob_low = (weights / total_weight).astype(jnp.bfloat16)
        block_out = jnp.einsum(
            "ngqk,knd->qngd", prob_low, heads_of_value, preferred_element_type=jnp.float32
        )
        return (block_out.astype(jnp.bfloat16), (top_score + jnp.log(total_weight))[..., 0])

    outputs, log_totals = lax.map(forward_block, (blocks_of_query, row_index, row_segment))
    return (outputs.reshape(sequence_length, kv_local * group_width * head_size), log_totals)


def attend_back(heads_of_query, heads_of_key, heads_of_value, segment_row, out_grad, log_totals):
    sequence_length, kv_local, group_width, head_size = heads_of_query.shape
    score_scale = head_size ** (-0.5)
    number_blocks, rows_per_block, position_index, row_index, row_segment = block_layout(
        heads_of_query, segment_row
    )
    blocks_of_query = heads_of_query.reshape(
        number_blocks, rows_per_block, kv_local, group_width, head_size
    )
    grad_blocks = out_grad.reshape(number_blocks, rows_per_block, kv_local, group_width, head_size)

    def backward_block(running_grads, inputs):
        key_grad, value_grad = running_grads
        query_block, grad_block, block_total, block_index, block_segment = inputs
        scores = score_block(
            query_block,
            heads_of_key,
            block_index,
            block_segment,
            position_index,
            segment_row,
            score_scale,
        )
        prob_block = jnp.exp(scores - block_total[..., None])
        prob_grad = jnp.einsum(
            "qngd,knd->ngqk", grad_block, heads_of_value, preferred_element_type=jnp.float32
        )
        inner_sum = jnp.sum(prob_block * prob_grad, axis=-1, keepdims=True)
        score_grad = (prob_block * (prob_grad - inner_sum)).astype(jnp.bfloat16)
        query_grad = (
            jnp.einsum(
                "ngqk,knd->qngd", score_grad, heads_of_key, preferred_element_type=jnp.float32
            )
            * score_scale
        )
        key_grad = (
            key_grad
            + jnp.einsum(
                "ngqk,qngd->knd", score_grad, query_block, preferred_element_type=jnp.float32
            )
            * score_scale
        )
        value_grad = value_grad + jnp.einsum(
            "ngqk,qngd->knd",
            prob_block.astype(jnp.bfloat16),
            grad_block,
            preferred_element_type=jnp.float32,
        )
        return ((key_grad, value_grad), query_grad)

    zero_keys = jnp.zeros(heads_of_key.shape, jnp.float32)
    (key_grad, value_grad), query_grad = lax.scan(
        backward_block,
        (zero_keys, zero_keys),
        (blocks_of_query, grad_blocks, log_totals, row_index, row_segment),
    )
    return (
        query_grad.reshape(sequence_length, kv_local * group_width, head_size),
        key_grad,
        value_grad,
    )


def general_plan(
    tokens,
    segment_ids,
    attn_gain,
    query_gain,
    key_gain,
    query_weight,
    key_matrix,
    value_matrix,
    out_weight,
    mlp_gain,
    gate_weight,
    up_weight,
    down_weight,
    cotangent,
):
    layer_count = attn_gain.shape[0]
    head_size = query_gain.shape[-1]
    segment_row = segment_ids[0]
    cosine_table, sine_table = rope_tables(positions_of(segment_row), head_size)
    weight_set = (
        query_weight,
        key_matrix,
        value_matrix,
        out_weight,
        gate_weight,
        up_weight,
        down_weight,
    )

    def turn_heads(raw_rows, gain_row):
        return head_norm(raw_rows, gain_row, cosine_table, sine_table)

    residual = tokens.astype(jnp.float32)
    saved_layers = []
    for layer_index in range(layer_count):
        gathered = gather_layer(weight_set, layer_index)
        wide_query, wide_key, wide_value, wide_out, wide_gate, wide_up, wide_down = gathered
        attn_normed, attn_back = jax.vjp(rms_scale, residual, attn_gain[layer_index])
        seq_rows = spread_rows(attn_normed.astype(jnp.bfloat16))
        sequence_length = seq_rows.shape[0]
        query_raw = jnp.dot(seq_rows, wide_query, preferred_element_type=jnp.float32)
        key_raw = jnp.dot(seq_rows, wide_key, preferred_element_type=jnp.float32)
        value_raw = jnp.dot(seq_rows, wide_value, preferred_element_type=jnp.float32)
        query_turned, query_back = jax.vjp(turn_heads, query_raw, query_gain[layer_index])
        key_turned, key_back = jax.vjp(turn_heads, key_raw, key_gain[layer_index])
        kv_local = key_raw.shape[1] // head_size
        heads_of_query = query_turned.astype(jnp.bfloat16).reshape(
            sequence_length, kv_local, -1, head_size
        )
        heads_of_key = key_turned.astype(jnp.bfloat16)
        heads_of_value = value_raw.astype(jnp.bfloat16).reshape(
            sequence_length, kv_local, head_size
        )
        attn_rows, log_totals = attend(heads_of_query, heads_of_key, heads_of_value, segment_row)
        residual_mid = residual + collect_rows(attn_rows, wide_out)
        mlp_normed, mlp_back = jax.vjp(rms_scale, residual_mid, mlp_gain[layer_index])
        mlp_rows = spread_rows(mlp_normed.astype(jnp.bfloat16))
        gate_proj = jnp.dot(mlp_rows, wide_gate, preferred_element_type=jnp.float32)
        upward = jnp.dot(mlp_rows, wide_up, preferred_element_type=jnp.float32)
        hidden_float, swiglu_back = jax.vjp(swiglu, gate_proj, upward)
        hidden = hidden_float.astype(jnp.bfloat16)
        residual = residual_mid + collect_rows(hidden, wide_down)
        saved_layers.append(
            (
                gathered,
                attn_back,
                seq_rows,
                query_back,
                key_back,
                heads_of_query,
                heads_of_key,
                heads_of_value,
                attn_rows,
                log_totals,
                mlp_back,
                mlp_rows,
                swiglu_back,
                hidden,
            )
        )
    result = residual.astype(jnp.bfloat16)
    residual_grad = cotangent.astype(jnp.float32)
    grad_weights = [None] * layer_count
    gain_grads = [None] * layer_count
    for layer_index in reversed(range(layer_count)):
        (
            gathered,
            attn_back,
            seq_rows,
            query_back,
            key_back,
            heads_of_query,
            heads_of_key,
            heads_of_value,
            attn_rows,
            log_totals,
            mlp_back,
            mlp_rows,
            swiglu_back,
            hidden,
        ) = saved_layers[layer_index]
        gathered = gather_layer(weight_set, layer_index)
        wide_query, wide_key, wide_value, wide_out, wide_gate, wide_up, wide_down = gathered
        grad_rows = spread_grads(residual_grad.astype(jnp.bfloat16))
        down_grad = contract_rows(hidden, grad_rows)
        hidden_grad = contract_cols(grad_rows, wide_down)
        gate_grad, upward_grad = swiglu_back(hidden_grad)
        gate_low = gate_grad.astype(jnp.bfloat16)
        upward_low = upward_grad.astype(jnp.bfloat16)
        gate_wgrad = contract_rows(mlp_rows, gate_low)
        upward_wgrad = contract_rows(mlp_rows, upward_low)
        normed_grad = collect_grads(((gate_low, wide_gate), (upward_low, wide_up)))
        residual_part, mlp_gain_grad = mlp_back(normed_grad)
        residual_grad = residual_grad + residual_part
        grad_rows = spread_grads(residual_grad.astype(jnp.bfloat16))
        sequence_length = grad_rows.shape[0]
        out_wgrad = contract_rows(attn_rows, grad_rows)
        mixed_grad = contract_cols(grad_rows, wide_out).astype(jnp.bfloat16)
        query_grad, key_grad, value_grad = attend_back(
            heads_of_query,
            heads_of_key,
            heads_of_value,
            segment_row,
            mixed_grad.reshape(heads_of_query.shape),
            log_totals,
        )
        query_raw_grad, query_gain_grad = query_back(query_grad)
        key_raw_grad, key_gain_grad = key_back(key_grad)
        query_low = query_raw_grad.astype(jnp.bfloat16)
        key_low = key_raw_grad.astype(jnp.bfloat16)
        value_low = value_grad.reshape(sequence_length, -1).astype(jnp.bfloat16)
        query_wgrad = contract_rows(seq_rows, query_low)
        key_wgrad = contract_rows(seq_rows, key_low)
        value_wgrad = contract_rows(seq_rows, value_low)
        normed_grad = collect_grads(
            ((query_low, wide_query), (key_low, wide_key), (value_low, wide_value))
        )
        residual_part, attn_gain_grad = attn_back(normed_grad)
        residual_grad = residual_grad + residual_part
        grad_weights[layer_index] = (
            lax.psum_scatter(
                query_wgrad.astype(jnp.bfloat16), "fsdp", scatter_dimension=0, tiled=True
            ).astype(jnp.float32),
            lax.psum_scatter(
                key_wgrad.astype(jnp.bfloat16), "fsdp", scatter_dimension=0, tiled=True
            ).astype(jnp.float32),
            lax.psum_scatter(
                value_wgrad.astype(jnp.bfloat16), "fsdp", scatter_dimension=0, tiled=True
            ).astype(jnp.float32),
            lax.psum_scatter(
                out_wgrad.astype(jnp.bfloat16), "fsdp", scatter_dimension=1, tiled=True
            ).astype(jnp.float32),
            lax.psum_scatter(
                gate_wgrad.astype(jnp.bfloat16), "fsdp", scatter_dimension=0, tiled=True
            ).astype(jnp.float32),
            lax.psum_scatter(
                upward_wgrad.astype(jnp.bfloat16), "fsdp", scatter_dimension=0, tiled=True
            ).astype(jnp.float32),
            lax.psum_scatter(
                down_grad.astype(jnp.bfloat16), "fsdp", scatter_dimension=1, tiled=True
            ).astype(jnp.float32),
        )
        gain_grads[layer_index] = (attn_gain_grad, query_gain_grad, key_gain_grad, mlp_gain_grad)
    local_stacks = tuple(
        (
            jnp.stack([grad_weights[layer_index][member] for layer_index in range(layer_count)])
            for member in range(7)
        )
    )
    gain_stacks = tuple(
        (
            jnp.stack([gain_grads[layer_index][member] for layer_index in range(layer_count)])
            for member in range(4)
        )
    )
    summed = lax.psum(
        (gain_stacks[0], gain_stacks[1], gain_stacks[2], gain_stacks[3]), ("fsdp", "tp")
    )
    return (
        result,
        residual_grad,
        summed[0],
        summed[1],
        summed[2],
        local_stacks[0],
        local_stacks[1],
        local_stacks[2],
        local_stacks[3],
        summed[3],
        local_stacks[4],
        local_stacks[5],
        local_stacks[6],
    )


def plane_send(values, distance):
    size = lax.axis_size("fsdp")
    return lax.ppermute(values, "fsdp", [(i, i ^ distance) for i in range(size)])


def plane_place():
    return lax.axis_index("fsdp").astype(jnp.int32).reshape(1)


def low(values):
    return values.astype(jnp.bfloat16)


def wide(values):
    return values.astype(jnp.float32)


def add_low(left, right):
    return low(wide(left) + wide(right))


def gather_plane(own, use=None):
    half = own.shape[0] // 2
    near = [own, plane_send(own, 1)]
    made = [use(near, 0)] if use else []
    across_x, across_y, made = lax.optimization_barrier(
        (plane_send(own, 2), plane_send(own, 4), made)
    )
    far = plane_send(across_y[:half], 2), plane_send(across_x[half:], 4)
    across = [across_x, plane_send(across_x, 1), across_y, plane_send(across_y, 1)]
    if use:
        made = made + [use(across, 1)]
    top, bottom, made = lax.optimization_barrier((*far, made))
    last = [top, bottom, plane_send(top, 1), plane_send(bottom, 1)]
    if use:
        return [near, across, last], made + [use(last, 2)]
    return [near, across, last]


def shard_of(sets, d):
    return (sets[0], d) if d < 2 else (sets[1], d - 2) if d < 6 else (sets[2], d - 6)


def reduce_plane(part, join=()):
    odd = part((7, 5, 3, 1), None)
    received = [plane_send(v, 1) for v in odd]
    (far,) = part((6,), received[:1])
    half = far.shape[0] // 2
    top, bottom = lax.optimization_barrier(
        (plane_send(far[:half], 2), plane_send(far[half:], 4))
    )
    by_y, by_x, here = part((4, 2, 0), received[1:])
    by_y = jnp.concatenate([add_low(by_y[:half], top), by_y[half:]])
    by_x = jnp.concatenate([by_x[:half], add_low(by_x[half:], bottom)])
    by_x, by_y, join = lax.optimization_barrier((by_x, by_y, join))
    from_x = plane_send(by_x, 2)
    from_y = plane_send(by_y, 4)
    return wide(here) + wide(from_x) + wide(from_y), far, join


def sum_line(values):
    size = lax.axis_size("tp")
    if size & (size - 1):
        return lax.psum(values, "tp")
    distance = 1
    while distance < size:
        pairs = [(i, i ^ distance) for i in range(size)]
        values = values + lax.ppermute(values, "tp", pairs)
        distance *= 2
    return values


def sum_plane(values):
    for distance in (1, 2, 4):
        values = values + plane_send(values, distance)
    return values


def after(token, *values):
    if token is None:
        return values
    return lax.optimization_barrier((token, *values))[1:]


def line_gather(own, axis=0):
    return lax.all_gather(own, "tp", axis=axis, tiled=True)


def line_reduce(terms, axis=0):
    return lax.psum_scatter(terms, "tp", scatter_dimension=axis, tiled=True)


def assemble(sets, block_shape, axis, places):
    size = sum(len(held) for _, held in sets)
    block = block_shape[axis]
    shape = list(block_shape)
    shape[axis] = size * block

    def kernel(place_ref, *refs):
        out, d = refs[len(sets)], 0
        for (_, held), ref in zip(sets, refs):
            for i in held:
                start = pl.multiple_of(place_ref[d] * block, block)
                where = tuple([slice(None)] * axis + [pl.ds(start, block)])
                out[where] = ref[...] if i is None else ref[i]
                d += 1

    return pl.pallas_call(
        kernel,
        out_shape=jax.ShapeDtypeStruct(tuple(shape), sets[0][0].dtype),
        in_specs=[pl.BlockSpec(memory_space=pltpu.SMEM)]
        + [pl.BlockSpec(memory_space=pltpu.VMEM)] * len(sets),
        out_specs=pl.BlockSpec(memory_space=pltpu.VMEM),
        compiler_params=kernel_params(12),
        cost_estimate=kernel_cost(),
        name="assemble",
    )(places, *(array for array, _ in sets))


def block_at(array, index, block, axis):
    return lax.dynamic_slice_in_dim(array, index * block, block, axis)


def swap(array, axis, into, start=None, done=None, first=None):
    size = lax.axis_size("fsdp")
    places = lax.axis_index("fsdp").astype(jnp.int32) ^ jnp.arange(size, dtype=jnp.int32)
    block = array.shape[axis] // size
    (array,) = after(start, array)
    pieces = [block_at(array, places[d], block, axis) for d in range(size)]
    other = plane_send(jnp.stack(pieces[1::2]), 1)
    chips = [plane_send(jnp.stack([pieces[d], other[d // 2]]), d) for d in (6, 4, 2)]
    if first is not None:
        first.extend(chips)
    other, *chips = after(done, other[0], *chips)
    sets = [(pieces[0], (None,)), (other, (None,))] + [(v, (0, 1)) for v in reversed(chips)]
    return assemble(sets, pieces[0].shape, into, places)


def line_swap(array, start=None, done=None):
    size = lax.axis_size("tp")
    place = lax.axis_index("tp").astype(jnp.int32)
    block = array.shape[0] // size
    sources = (place - jnp.arange(size, dtype=jnp.int32)) % size
    (array,) = after(start, array)
    moved = []
    for step in range(1, size):
        piece = block_at(array, (place + step) % size, block, 0)
        pairs = [(i, (i + step) % size) for i in range(size)]
        moved.append(lax.ppermute(piece, "tp", pairs))
    moved = after(done, *moved)
    own = block_at(array, place, block, 0)
    return assemble([(v, (None,)) for v in (own, *moved)], own.shape, 0, sources)


def line_rows(rows, start=None, done=None):
    size, line = lax.axis_size("fsdp"), lax.axis_size("tp")
    count, width = rows.shape
    blocks = line_swap(rows, start, done).reshape(line, size // line, count // size, width)
    return blocks.transpose(1, 0, 2, 3).reshape(count, width)


def line_rows_back(rows, start=None, done=None):
    size, line = lax.axis_size("fsdp"), lax.axis_size("tp")
    count, width = rows.shape
    blocks = rows.reshape(size // line, line, count // size, width).transpose(1, 0, 2, 3)
    return line_swap(blocks.reshape(count, width), start, done)


def plane_segments(segment_ids):
    size, line = lax.axis_size("fsdp"), lax.axis_size("tp")
    rows = segment_ids
    for distance in (1, 2, 4):
        rows = jnp.concatenate([rows, plane_send(rows, distance)])
    local = size // line
    wanted = lax.axis_index("tp") * local + jnp.arange(local)
    return rows[wanted ^ lax.axis_index("fsdp")]


def attention_weights(query_shard, key_shard, value_shard, out_shard):
    size, line = lax.axis_size("fsdp"), lax.axis_size("tp")
    per, depth = size // line, query_shard.shape[0]
    pack = jnp.concatenate(
        [
            query_shard.T.reshape(per, -1, depth),
            key_shard.T.reshape(per, -1, depth),
            value_shard.T.reshape(per, -1, depth),
            out_shard.reshape(per, -1, depth),
        ],
        axis=1,
    )
    return line_gather(pack)


def turn(values, cosine, sine):
    return values * cosine + pltpu.roll(values, values.shape[1] // 2, 1) * sine


def turn_back(values, cosine, sine):
    return values * cosine - pltpu.roll(values, values.shape[1] // 2, 1) * sine


def inverse_rms(values):
    return lax.rsqrt(jnp.mean(values * values, axis=-1, keepdims=True) + EPSILON)


def rows_in_order(place, groups, target, pick):
    shards = [(ref, e) for ref in groups for e in range(ref.shape[0])]
    for d, (ref, e) in enumerate(shards):
        blocks, block = ref.shape[2], ref.shape[3]
        for i in range(blocks):
            start = pl.multiple_of((i * len(shards) + (place ^ d)) * block, block)
            target[pl.ds(start, block), :] = pick(ref[e, 0, i])


def rows_from_order(place, source, groups):
    shards = [(ref, e) for ref in groups for e in range(ref.shape[0])]
    for d, (ref, e) in enumerate(shards):
        blocks, block = ref.shape[2], ref.shape[3]
        for i in range(blocks):
            start = pl.multiple_of((i * len(shards) + (place ^ d)) * block, block)
            ref[e, 0, i] = source[pl.ds(start, block), :].astype(ref.dtype)


def head_columns(index, head):
    return slice(index * head, (index + 1) * head)


def heads_from_raw(nat, cos_ref, sin_ref, gains, heads, low_ref, rows):
    head = cos_ref.shape[-1]
    for start in range(0, nat.shape[0], rows):
        here = slice(start, start + rows)
        cosine, sine = cos_ref[0, here, :], sin_ref[0, here, :]
        for h in range(heads + 2):
            raw = nat[here, head_columns(h, head)]
            if h <= heads:
                gain = gains[0] if h < heads else gains[1]
                raw = turn(raw * inverse_rms(raw) * gain[...], cosine, sine)
            low_ref[here, head_columns(h, head)] = raw.astype(low_ref.dtype)


def block_operands(low_ref, start, rows, heads, head):
    query = jnp.concatenate(
        [low_ref[start : start + rows, head_columns(h, head)] for h in range(heads)], axis=0
    )
    key = low_ref[: start + rows, head_columns(heads, head)]
    value = low_ref[: start + rows, head_columns(heads + 1, head)]
    return query, key, value


def masked_scores(key, query, first_ref, start, rows, heads, scale):
    scores = lax.dot_general(
        key, query, (((1,), (1,)), ((), ())), preferred_element_type=jnp.float32
    )
    shape = (key.shape[0], rows)
    index = lax.broadcasted_iota(jnp.int32, shape, 0)
    mine = lax.broadcasted_iota(jnp.int32, shape, 1) + start
    first = first_ref[0, :, start : start + rows]
    allowed = (index <= mine) & (index >= first)
    allowed = jnp.concatenate([allowed] * heads, axis=1)
    return jnp.where(allowed, scores * scale, -1e30)


def attend_kernel(groups, heads, rows, *refs):
    place = refs[0][0]
    raw_refs = refs[1 : 1 + groups]
    cos_ref, sin_ref, first_ref, query_gain, key_gain = refs[1 + groups : 6 + groups]
    out_refs = refs[6 + groups : 6 + 2 * groups]
    total_ref, nat, low_ref, mixed = refs[6 + 2 * groups :]
    head = cos_ref.shape[-1]
    rows_in_order(place, raw_refs, nat, lambda v: v)
    heads_from_raw(nat, cos_ref, sin_ref, (query_gain, key_gain), heads, low_ref, rows)
    for i in range(nat.shape[0] // rows):
        start = i * rows
        query, key, value = block_operands(low_ref, start, rows, heads, head)
        scores = masked_scores(key, query, first_ref, start, rows, heads, head ** (-0.5))
        top = jnp.max(scores, axis=0, keepdims=True)
        weights = jnp.exp(scores - top)
        total = jnp.sum(weights, axis=0, keepdims=True)
        total_ref[0, i : i + 1, :] = top + jnp.log(total)
        prob = (weights * (1.0 / total)).astype(jnp.bfloat16)
        out = lax.dot_general(
            prob, value, (((0,), (0,)), ((), ())), preferred_element_type=jnp.float32
        ).astype(jnp.bfloat16)
        for h in range(heads):
            mixed[start : start + rows, head_columns(h, head)] = out[h * rows : (h + 1) * rows]
    rows_from_order(place, mixed, out_refs)


def attend_back_kernel(groups, heads, rows, *refs):
    place = refs[0][0]
    raw_refs = refs[1 : 1 + groups]
    grad_refs = refs[1 + groups : 1 + 2 * groups]
    rest = refs[1 + 2 * groups :]
    total_ref, cos_ref, sin_ref, first_ref, query_gain, key_gain = rest[:6]
    out_refs = rest[6 : 6 + groups]
    gain_ref, nat, low_ref, mixed, grads, key_sum, value_sum, done = rest[6 + groups :]
    head = cos_ref.shape[-1]
    scale = head ** (-0.5)
    rows_in_order(place, raw_refs, nat, lambda v: v)
    rows_in_order(place, grad_refs, mixed, lambda v: v)
    heads_from_raw(nat, cos_ref, sin_ref, (query_gain, key_gain), heads, low_ref, rows)
    key_sum[...] = jnp.zeros_like(key_sum)
    value_sum[...] = jnp.zeros_like(value_sum)
    for i in range(nat.shape[0] // rows):
        start = i * rows
        stop = start + rows
        query, key, value = block_operands(low_ref, start, rows, heads, head)
        out_grad = jnp.concatenate(
            [mixed[start:stop, head_columns(h, head)] for h in range(heads)], axis=0
        )
        scores = masked_scores(key, query, first_ref, start, rows, heads, scale)
        prob = jnp.exp(scores - total_ref[0, i : i + 1, :])
        prob_grad = lax.dot_general(
            value, out_grad, (((1,), (1,)), ((), ())), preferred_element_type=jnp.float32
        )
        inner = jnp.sum(prob * prob_grad, axis=0, keepdims=True)
        score_grad = (prob * (prob_grad - inner)).astype(jnp.bfloat16)
        value_sum[:stop, :] += jnp.dot(
            prob.astype(jnp.bfloat16), out_grad, preferred_element_type=jnp.float32
        )
        key_sum[:stop, :] += jnp.dot(score_grad, query, preferred_element_type=jnp.float32)
        query_grad = lax.dot_general(
            score_grad, key, (((0,), (0,)), ((), ())), preferred_element_type=jnp.float32
        )
        for h in range(heads):
            grads[start:stop, head_columns(h, head)] = query_grad[h * rows : (h + 1) * rows] * scale
    sums = [jnp.zeros((1, head), jnp.float32)] * 2
    for start in range(0, nat.shape[0], rows):
        here = slice(start, start + rows)
        cosine, sine = cos_ref[0, here, :], sin_ref[0, here, :]
        for h in range(heads + 1):
            kind = 0 if h < heads else 1
            gain = (query_gain, key_gain)[kind][...]
            grad = grads[here, head_columns(h, head)] if h < heads else key_sum[here, :] * scale
            raw = nat[here, head_columns(h, head)]
            inverse = inverse_rms(raw)
            grad = turn_back(grad, cosine, sine)
            sums[kind] += jnp.sum(grad * raw * inverse, axis=0, keepdims=True)
            grad = grad * gain
            middle = jnp.mean(grad * raw, axis=-1, keepdims=True)
            done[here, head_columns(h, head)] = (
                inverse * grad - raw * (inverse * inverse * inverse) * middle
            ).astype(done.dtype)
        done[here, head_columns(heads + 1, head)] = value_sum[here, :].astype(done.dtype)
    gain_ref[0] = jnp.concatenate(sums, axis=0)
    rows_from_order(place, done, out_refs)


def kernel_cost(flops=1024):
    return pl.CostEstimate(flops=flops // 2, bytes_accessed=1024, transcendentals=0)


def kernel_params(mib=48):
    return pltpu.CompilerParams(vmem_limit_bytes=mib * 1024 * 1024)


def group_specs(arrays):
    def spec(array):
        return pl.BlockSpec((array.shape[0], 1) + array.shape[2:], lambda s: (0, s, 0, 0, 0))

    return [spec(array) for array in arrays]


def table_specs(length, head):
    table = pl.BlockSpec((1, length, head), lambda s: (s, 0, 0))
    gain = pl.BlockSpec((1, head), lambda s: (0, 0))
    return [table, table, pl.BlockSpec((1, 1, length), lambda s: (s, 0, 0)), gain, gain]


def grouped(rows, shards, local, blocks):
    count, width = rows.shape
    return rows.reshape(shards, local, blocks, count // (shards * local * blocks), width)


def plane_attend(raw, tables, first, gains, rows=256):
    local, length, head = tables[0].shape
    width = raw[0].shape[-1]
    heads = width // head - 2
    groups = len(raw)
    outs = [jax.ShapeDtypeStruct(v.shape[:-1] + (heads * head,), jnp.bfloat16) for v in raw]
    totals = jax.ShapeDtypeStruct((local, length // rows, heads * rows), jnp.float32)
    out = pl.pallas_call(
        functools.partial(attend_kernel, groups, heads, rows),
        grid=(local,),
        out_shape=outs + [totals],
        in_specs=[pl.BlockSpec(memory_space=pltpu.SMEM)]
        + group_specs(raw)
        + table_specs(length, head),
        out_specs=group_specs(outs)
        + [pl.BlockSpec((1,) + totals.shape[1:], lambda s: (s, 0, 0))],
        scratch_shapes=[
            pltpu.VMEM((length, width), jnp.float32),
            pltpu.VMEM((length, width), jnp.bfloat16),
            pltpu.VMEM((length, heads * head), jnp.bfloat16),
        ],
        compiler_params=kernel_params(24),
        cost_estimate=kernel_cost(local * heads * length * length * head * 8),
        name="attend",
    )(plane_place(), *raw, *tables, first, *gains)
    return out[:groups], out[groups]


def plane_attend_back(raw, out_grad, totals, tables, first, gains, rows=256):
    local, length, head = tables[0].shape
    width = raw[0].shape[-1]
    heads = width // head - 2
    groups = len(raw)
    out = pl.pallas_call(
        functools.partial(attend_back_kernel, groups, heads, rows),
        grid=(local,),
        out_shape=[jax.ShapeDtypeStruct(v.shape, jnp.bfloat16) for v in raw]
        + [jax.ShapeDtypeStruct((local, 2, head), jnp.float32)],
        in_specs=[pl.BlockSpec(memory_space=pltpu.SMEM)]
        + group_specs(raw)
        + group_specs(out_grad)
        + [pl.BlockSpec((1,) + totals.shape[1:], lambda s: (s, 0, 0))]
        + table_specs(length, head),
        out_specs=group_specs(raw) + [pl.BlockSpec((1, 2, head), lambda s: (s, 0, 0))],
        scratch_shapes=[
            pltpu.VMEM((length, width), jnp.float32),
            pltpu.VMEM((length, width), jnp.bfloat16),
            pltpu.VMEM((length, heads * head), jnp.bfloat16),
            pltpu.VMEM((length, heads * head), jnp.float32),
            pltpu.VMEM((length, head), jnp.float32),
            pltpu.VMEM((length, head), jnp.float32),
            pltpu.VMEM((length, width), jnp.bfloat16),
        ],
        compiler_params=kernel_params(32),
        cost_estimate=kernel_cost(local * heads * length * length * head * 16),
        name="attend_back",
    )(plane_place(), *raw, *out_grad, totals, *tables, first, *gains)
    return out[:groups], jnp.sum(out[groups], axis=0)


def whole_spec(array):
    return pl.BlockSpec(
        array.shape, lambda n: (0,) * array.ndim, pipeline_mode=pl.Buffered(buffer_count=1)
    )


def dot_cols(left, right):
    return lax.dot_general(
        left, right, (((1,), (1,)), ((), ())), preferred_element_type=jnp.float32
    )


def joined(refs, rows_ref):
    @pl.when(pl.program_id(0) == 0)
    def _():
        start = 0
        for ref in refs:
            rows_ref[start : start + ref.shape[0], :] = ref[...]
            start += ref.shape[0]

    return rows_ref[...]


def joined_scratch(pieces):
    count = sum(v.shape[0] for v in pieces)
    return [pltpu.VMEM((count, pieces[0].shape[1]), pieces[0].dtype)]


def project_kernel(count, *refs):
    weight, out, rows_ref = refs[count:]
    out[...] = dot_cols(joined(refs[:count], rows_ref), weight[...]).astype(out.dtype)


def project(pieces, weight, first, width, dtype, tile=256):
    count = sum(v.shape[0] for v in pieces)
    return pl.pallas_call(
        functools.partial(project_kernel, len(pieces)),
        grid=(width // tile,),
        out_shape=jax.ShapeDtypeStruct((count, width), dtype),
        in_specs=[whole_spec(v) for v in pieces]
        + [pl.BlockSpec((tile, weight.shape[1]), lambda n: (first // tile + n, 0))],
        out_specs=pl.BlockSpec((count, tile), lambda n: (0, n)),
        scratch_shapes=joined_scratch(pieces),
        compiler_params=kernel_params(16),
        cost_estimate=kernel_cost(2 * count * width * weight.shape[1]),
        name="project",
    )(*pieces, weight)


def units_kernel(count, *refs):
    gate_rows, up_rows, hidden_ref, gate_ref, up_ref, rows_ref = refs[count:]
    rows = joined(refs[:count], rows_ref)
    gate = dot_cols(rows, gate_rows[0])
    up = dot_cols(rows, up_rows[0])
    hidden_ref[...] = (gate * up / (1.0 + jnp.exp(-gate))).astype(hidden_ref.dtype)
    gate_ref[...] = gate.astype(gate_ref.dtype)
    up_ref[...] = up.astype(up_ref.dtype)


def unit_spec(weights, kind, tile):
    return pl.BlockSpec((1, tile, weights.shape[2]), lambda n: (kind, n, 0))


def hidden_units(pieces, weights, tile=256):
    count = sum(v.shape[0] for v in pieces)
    shape = jax.ShapeDtypeStruct((count, weights.shape[1]), jnp.bfloat16)
    return pl.pallas_call(
        functools.partial(units_kernel, len(pieces)),
        grid=(weights.shape[1] // tile,),
        out_shape=[shape] * 3,
        in_specs=[whole_spec(v) for v in pieces]
        + [unit_spec(weights, kind, tile) for kind in (0, 1)],
        out_specs=[pl.BlockSpec((count, tile), lambda n: (0, n))] * 3,
        scratch_shapes=joined_scratch(pieces),
        compiler_params=kernel_params(20),
        cost_estimate=kernel_cost(4 * count * weights.shape[1] * weights.shape[2]),
        name="hidden_units",
    )(*pieces, weights, weights)


def units_back_kernel(count, *refs):
    down_rows, gate_ref, up_ref, gate_grad, up_grad, rows_ref = refs[count:]
    grad = dot_cols(joined(refs[:count], rows_ref), down_rows[0])
    gate, up = wide(gate_ref[...]), wide(up_ref[...])
    sigmoid = 1.0 / (1.0 + jnp.exp(-gate))
    gate_grad[...] = (grad * up * sigmoid * (1.0 + gate * (1.0 - sigmoid))).astype(gate_grad.dtype)
    up_grad[...] = (grad * gate * sigmoid).astype(up_grad.dtype)


def hidden_units_back(pieces, weights, gate, up, tile=256):
    count = gate.shape[0]
    side = pl.BlockSpec((count, tile), lambda n: (0, n))
    return pl.pallas_call(
        functools.partial(units_back_kernel, len(pieces)),
        grid=(weights.shape[1] // tile,),
        out_shape=[jax.ShapeDtypeStruct(gate.shape, jnp.bfloat16)] * 2,
        in_specs=[whole_spec(v) for v in pieces] + [unit_spec(weights, 2, tile), side, side],
        out_specs=[side, side],
        scratch_shapes=joined_scratch(pieces),
        compiler_params=kernel_params(20),
        cost_estimate=kernel_cost(2 * count * weights.shape[1] * weights.shape[2]),
        name="hidden_units_back",
    )(*pieces, weights, gate, up)


def parts_kernel(shards, terms, adding, *refs):
    lefts, weights = refs[: shards * terms], refs[shards * terms : (shards + 1) * terms]
    adds = refs[(shards + 1) * terms : -shards]
    outs = refs[-shards:]
    total = None
    for t in range(terms):
        weight = weights[t][...]
        left = jnp.concatenate([lefts[i * terms + t][...] for i in range(shards)], axis=0)
        term = jnp.dot(
            left, weight.reshape(weight.shape[-2:]), preferred_element_type=jnp.float32
        )
        total = term if total is None else total + term
    rows = outs[0].shape[0]
    for i in range(shards):
        mine = total[i * rows : (i + 1) * rows]
        if adding:
            mine = mine + wide(adds[i][...])
        outs[i][...] = mine.astype(outs[i].dtype)


def parts_of(terms, ds, adds, tile=512):
    lefts, specs = [], []
    for d in ds:
        for sets, _, _ in terms:
            array, place = shard_of(sets, d)
            rows = sets[0].shape[0] // 2
            lefts.append(array)
            specs.append(
                pl.BlockSpec(
                    (rows, array.shape[1]),
                    lambda n, p=place: (p, 0),
                    pipeline_mode=pl.Buffered(buffer_count=1),
                )
            )
    width = terms[0][1].shape[-1]
    side = pl.BlockSpec((rows, tile), lambda n: (0, n))
    return pl.pallas_call(
        functools.partial(parts_kernel, len(ds), len(terms), adds is not None),
        grid=(width // tile,),
        out_shape=[jax.ShapeDtypeStruct((rows, width), jnp.bfloat16)] * len(ds),
        in_specs=specs + [spec for _, _, spec in terms] + [side] * len(adds or ()),
        out_specs=[side] * len(ds),
        compiler_params=kernel_params(16),
        cost_estimate=kernel_cost(2 * len(ds) * rows * width * sum(v.shape[-1] for v in lefts[: len(terms)])),
        name="parts",
    )(*lefts, *(weights for _, weights, _ in terms), *(adds or ()))


def rows_spec(kind, weights, tile=512):
    return pl.BlockSpec((1, weights.shape[1], tile), lambda n: (kind, 0, n))


def pack_spec(block, height, tile=512):
    return pl.BlockSpec((height, tile), lambda n: (block, n))


def outer_kernel(plan, *refs):
    for lefts, rights, place in plan:
        total = None
        for left, pieces in zip(lefts, rights):
            right = jnp.concatenate([refs[p][...] for p in pieces], axis=0)
            term = lax.dot_general(
                refs[left][...], right, (((0,), (0,)), ((), ())), preferred_element_type=jnp.float32
            )
            total = term if total is None else total + term
        refs[-1][place] = total.astype(refs[-1].dtype)


def outer(products, shape, tile=512):
    operands, specs, plan, seen = [], [], [], {}

    def operand(array, split):
        if id(array) not in seen:
            seen[id(array)] = len(operands)
            operands.append(array)
            specs.append(
                pl.BlockSpec((array.shape[0], tile), lambda n: (0, n))
                if split
                else pl.BlockSpec(
                    array.shape, lambda n: (0, 0), pipeline_mode=pl.Buffered(buffer_count=1)
                )
            )
        return seen[id(array)]

    for lefts, rights, place in products:
        plan.append(
            (
                [operand(v, False) for v in lefts],
                [[operand(v, True) for v in pieces] for pieces in rights],
                place,
            )
        )
    block = shape[:-1] + (tile,)
    return pl.pallas_call(
        functools.partial(outer_kernel, plan),
        grid=(shape[-1] // tile,),
        out_shape=jax.ShapeDtypeStruct(shape, jnp.bfloat16),
        in_specs=specs,
        out_specs=pl.BlockSpec(block, lambda n: (0,) * (len(shape) - 1) + (n,)),
        compiler_params=kernel_params(56),
        cost_estimate=kernel_cost(2 * shape[-1] * sum(v.size for lefts, _, _ in products for v in lefts)),
        name="outer",
    )(*operands)


def plane_plan(
    tokens,
    segment_ids,
    attn_gain,
    query_gain,
    key_gain,
    query_weight,
    key_matrix,
    value_matrix,
    out_weight,
    mlp_gain,
    gate_weight,
    up_weight,
    down_weight,
    cotangent,
):
    layers = attn_gain.shape[0]
    head = query_gain.shape[-1]
    size, line = lax.axis_size("fsdp"), lax.axis_size("tp")
    local = size // line
    segments = plane_segments(segment_ids)
    length = segments.shape[1]
    positions = jax.vmap(positions_of)(segments)
    first = (jnp.arange(length, dtype=jnp.int32)[None] - positions).reshape(local, 1, length)
    cosine_table, sine_table = rope_tables(positions.reshape(-1), head)
    turned_sign = jnp.where(jnp.arange(head) < head // 2, -1.0, 1.0)
    tables = (
        cosine_table.reshape(local, length, head),
        (sine_table * turned_sign).reshape(local, length, head),
    )
    query_count = query_weight.shape[2] * line // size
    key_count = key_matrix.shape[2] * line // size
    split = query_count + 2 * key_count

    def group(sets):
        counts = [v.shape[0] * size // sum(u.shape[0] for u in sets) for v in sets]
        return [grouped(v, count, local, line) for v, count in zip(sets, counts)]

    def flat(sets):
        return [v.reshape(-1, v.shape[-1]) for v in sets]

    def hold(token, sets):
        return [list(after(token, *v)) for v in sets]

    def reduce_down(hidden, weights):
        term = (hidden, weights, rows_spec(2, weights))
        return reduce_plane(lambda ds, adds: parts_of([term], ds, adds))[0]

    attn_sets, attn_gathered, hidden_sets = ([None] * layers for _ in range(3))

    def fetch_attn(index, token):
        shards = (query_weight[index], key_matrix[index], value_matrix[index], out_weight[index])
        attn_gathered[index] = attention_weights(*after(token, *shards))

    fetch_attn(0, None)
    exchanged = []
    both = jnp.concatenate([tokens, cotangent], axis=1)
    both = swap(both, 0, 0, None, None, exchanged)
    gate_weight, up_weight, down_weight = after(
        tuple(exchanged), gate_weight, up_weight, down_weight
    )
    hidden_shards = jnp.stack(
        [gate_weight.swapaxes(1, 2), up_weight.swapaxes(1, 2), down_weight], axis=1
    ).reshape(-1, *down_weight.shape[1:])
    both = line_rows(both)
    both, attn_gathered[0] = lax.optimization_barrier((both, attn_gathered[0]))
    hidden_shards, first = lax.optimization_barrier((hidden_shards, first))
    hidden_shards = swap(hidden_shards, 1, 2, None, both)
    hidden_shards = hidden_shards.reshape(layers, -1, *hidden_shards.shape[1:])
    residual, grad = wide(both[:, : tokens.shape[1]]), wide(both[:, tokens.shape[1] :])
    saved = []
    for index in range(layers):
        attn_sets[index] = pack = swap(attn_gathered[index], 0, 2)[0]
        gains = (query_gain[index][None], key_gain[index][None])
        normed, attn_back = jax.vjp(rms_scale, residual, attn_gain[index])
        rows = gather_plane(low(normed))
        if index == 0:
            hidden_sets[0] = line_gather(after(attn_gathered[0], hidden_shards[0])[0], 1)
        raw = group([project(v, pack, 0, split, jnp.float32) for v in rows])
        if index + 1 < layers:
            fetch_attn(index + 1, raw[0])
        mixed, totals = plane_attend(raw, tables, first, gains)
        mixed = flat(mixed)
        out_term = (mixed, pack, pack_spec(split // query_count, query_count))
        total, *_ = reduce_plane(lambda ds, adds: parts_of([out_term], ds, adds))
        middle = residual + total
        weights = hidden_sets[index]
        normed, mlp_back = jax.vjp(rms_scale, middle, mlp_gain[index])
        mlp_rows = gather_plane(low(normed))
        hidden, gates, ups = zip(*(hidden_units(v, weights) for v in mlp_rows))
        if index + 1 < layers:
            hidden_sets[index + 1] = line_gather(
                after(mlp_rows[2][0], hidden_shards[index + 1])[0], 1
            )
        if index + 1 < layers:
            residual = middle + reduce_down(hidden, weights)
        else:
            residual = middle
        saved.append(
            (attn_back, rows, raw, mixed, totals, mlp_back, mlp_rows, gates, ups, hidden)
        )
    pack_grads, pack_sums, gain_grads, hidden_sums, hidden_grads = (
        [None] * layers for _ in range(5)
    )
    for index in reversed(range(layers)):
        pack = attn_sets[index]
        gains = (query_gain[index][None], key_gain[index][None])
        weights = hidden_sets[index]
        attn_back, rows, raw, mixed, totals = saved[index][:5]
        mlp_back, mlp_rows, gates, ups, hidden = saved[index][5:]
        if index + 1 == layers:
            (grad,) = after(tuple(mlp_rows[2]), grad)
        grad_rows, unit_grads = gather_plane(
            low(grad), lambda v, i: hidden_units_back(v, weights, gates[i], ups[i])
        )
        gate_grads, up_grads = zip(*unit_grads)
        unit_terms = [
            (gate_grads, weights, rows_spec(0, weights)),
            (up_grads, weights, rows_spec(1, weights)),
        ]
        above = ()
        if index + 1 < layers:
            above = swap(pack_grads[index + 1][None], 2, 0, gate_grads[2])
        normed_grad, token, above = reduce_plane(
            lambda ds, adds: parts_of(unit_terms, ds, adds), above
        )
        (held,) = after(token, gate_grads[0])
        terms = outer(
            [
                ((held, *gate_grads[1:]), mlp_rows, 0),
                (up_grads, mlp_rows, 1),
                (hidden, grad_rows, 2),
            ],
            weights.shape,
        )
        normed_grad, terms = lax.optimization_barrier((normed_grad, terms))
        if index + 1 < layers:
            done = hidden_sums[index + 1]
            pack_sums[index + 1] = line_reduce(after(done, above)[0])
        hidden_sums[index] = line_reduce(terms, 1)
        grad_part, mlp_gain_grad = mlp_back(normed_grad)
        grad = grad + grad_part
        grad_rows, mixed_grad = gather_plane(
            low(grad), lambda v, i: project(v, pack, split, query_count, jnp.bfloat16)
        )
        mixed_grad = group(mixed_grad)
        raw_grad, head_gain_grads = plane_attend_back(raw, mixed_grad, totals, tables, first, gains)
        raw_grad = flat(raw_grad)
        if index + 1 == layers:
            result = residual + reduce_down(after(normed_grad, *hidden), weights)
            result, *raw_grad = lax.optimization_barrier((result, *raw_grad))
        if index + 1 < layers:
            hidden_grads[index + 1] = swap(hidden_sums[index + 1], 2, 1, mixed_grad[2])
            hidden_grads[index + 1], *raw_grad = lax.optimization_barrier(
                (hidden_grads[index + 1], *raw_grad)
            )
        raw_term = (raw_grad, pack, pack_spec(0, split))
        normed_grad, token, *_ = reduce_plane(
            lambda ds, adds: parts_of([raw_term], ds, adds)
        )
        (held,) = after(token, mixed[0])
        pack_grad = outer(
            [
                (raw_grad, rows, slice(0, split)),
                ((held, *mixed[1:]), grad_rows, slice(split, split + query_count)),
            ],
            pack.shape,
        )
        normed_grad, pack_grad = lax.optimization_barrier((normed_grad, pack_grad))
        pack_grads[index] = pack_grad
        grad_part, attn_gain_grad = attn_back(normed_grad)
        grad = grad + grad_part
        gain_grads[index] = jnp.concatenate(
            [attn_gain_grad, mlp_gain_grad, head_gain_grads[0], head_gain_grads[1]]
        )
    below = swap(pack_grads[0][None], 2, 0)
    pack_sums[0] = line_reduce(after((hidden_sums[0], pack_sums[1:]), below)[0])
    both = jnp.concatenate([low(result), low(grad)], axis=1)
    gain_stack = sum_line(jnp.stack(gain_grads).reshape(-1, head))
    both, gain_stack = lax.optimization_barrier((both, gain_stack))
    both = line_rows_back(both, below)
    gain_stack = sum_plane(gain_stack)
    hidden_grads[0] = swap(hidden_sums[0], 2, 1, below)
    both = swap(both, 0, 0)
    result, token_grad = both[:, : tokens.shape[1]], wide(both[:, tokens.shape[1] :])
    kinds = wide(jnp.stack(hidden_grads, 1))
    hidden_stacks = (kinds[0].swapaxes(1, 2), kinds[1].swapaxes(1, 2), kinds[2])
    marks = (0, query_count, query_count + key_count, split, pack_sums[0].shape[1])
    kinds = [
        jnp.stack(
            [wide(v[:, low_mark:high_mark]).reshape(-1, v.shape[-1]) for v in pack_sums]
        )
        for low_mark, high_mark in zip(marks, marks[1:])
    ]
    weight_stacks = [v.swapaxes(1, 2) for v in kinds[:3]] + kinds[3:]
    width = attn_gain.shape[1]
    gain_stack = gain_stack.reshape(layers, -1)
    attn_sum, mlp_sum, query_sum, key_sum = (
        gain_stack[:, :width],
        gain_stack[:, width : 2 * width],
        gain_stack[:, 2 * width : 2 * width + head],
        gain_stack[:, 2 * width + head :],
    )
    return (
        result,
        token_grad,
        attn_sum,
        query_sum,
        key_sum,
        *weight_stacks,
        mlp_sum,
        *hidden_stacks,
    )


def plane_fits(mesh, shapes):
    size, line = mesh.shape["fsdp"], mesh.shape["tp"]
    heads = shapes[6].shape[2] // shapes[4].shape[1]
    return size == 8 and heads == size and size % line == 0 and shapes[1].shape[0] == size


def solution(mesh):
    placed = (
        P(("fsdp", "tp"), None),
        P("fsdp", None),
        P(),
        P(),
        P(),
        P(None, "fsdp", "tp"),
        P(None, "fsdp", "tp"),
        P(None, "fsdp", "tp"),
        P(None, "tp", "fsdp"),
        P(),
        P(None, "fsdp", "tp"),
        P(None, "fsdp", "tp"),
        P(None, "tp", "fsdp"),
        P(("fsdp", "tp"), None),
    )
    def mapped(plan):
      return jax.shard_map(
        plan,
        mesh=mesh,
        in_specs=placed,
        out_specs=(
            P(("fsdp", "tp"), None),
            P(("fsdp", "tp"), None),
            P(),
            P(),
            P(),
            P(None, "fsdp", "tp"),
            P(None, "fsdp", "tp"),
            P(None, "fsdp", "tp"),
            P(None, "tp", "fsdp"),
            P(),
            P(None, "fsdp", "tp"),
            P(None, "fsdp", "tp"),
            P(None, "tp", "fsdp"),
        ),
        check_vma=False,
    )

    def whole(*args):
        return mapped(plane_plan if plane_fits(mesh, args) else general_plan)(*args)

    return whole
```

```python
import functools
import math

import jax
import jax.numpy as jnp
from jax import lax
from jax.experimental import pallas as pl
from jax.experimental.pallas import tpu as pltpu
from jax.sharding import PartitionSpec as P

EPSILON = 1e-06
ROPE_BASE = 1000000.0


def rms_scale(values, gain_row):
    return (
        values * lax.rsqrt(jnp.mean(values * values, axis=-1, keepdims=True) + EPSILON) * gain_row
    )


def positions_of(segment_row):
    sequence_length = segment_row.shape[0]
    position_index = jnp.arange(sequence_length, dtype=jnp.int32)
    starts = jnp.concatenate([jnp.ones((1,), dtype=jnp.bool_), segment_row[1:] != segment_row[:-1]])
    first_index = lax.cummax(
        jnp.where(starts, position_index, jnp.zeros_like(position_index)), axis=0
    )
    return position_index - first_index


def rope_tables(positions, head_size):
    half_size = head_size // 2
    steps_float = jnp.arange(half_size, dtype=jnp.float32)
    inverse = jnp.exp(steps_float * (-2.0 * math.log(ROPE_BASE) / head_size))
    angles = positions.astype(jnp.float32)[:, None] * inverse[None, :]
    angles = jnp.concatenate([angles, angles], axis=-1)
    return (jnp.cos(angles), jnp.sin(angles))


def rotate(values, cosine_table, sine_table):
    half_size = values.shape[-1] // 2
    turned = jnp.concatenate([-values[..., half_size:], values[..., :half_size]], axis=-1)
    return values * cosine_table[:, None, :] + turned * sine_table[:, None, :]


def head_norm(raw_rows, gain_row, cosine_table, sine_table):
    head_size = gain_row.shape[-1]
    shaped = raw_rows.reshape(raw_rows.shape[0], raw_rows.shape[1] // head_size, head_size)
    return rotate(rms_scale(shaped, gain_row), cosine_table, sine_table)


def swiglu(gate_proj, upward):
    return jax.nn.silu(gate_proj) * upward


def contract_rows(left_side, right_side):
    return lax.dot_general(
        left_side, right_side, (((0,), (0,)), ((), ())), preferred_element_type=jnp.float32
    )


def contract_cols(left_side, right_side):
    return lax.dot_general(
        left_side, right_side, (((1,), (1,)), ((), ())), preferred_element_type=jnp.float32
    )


def spread_rows(rows_low):
    return lax.all_gather(rows_low, "tp", axis=0, tiled=True)


def spread_grads(grad_low):
    return lax.all_gather(grad_low, "tp", axis=0, tiled=True)


def collect_rows(left_side, right_side):
    return lax.psum_scatter(
        jnp.dot(left_side, right_side, preferred_element_type=jnp.float32).astype(jnp.bfloat16),
        "tp",
        scatter_dimension=0,
        tiled=True,
    ).astype(jnp.float32)


def collect_grads(pairs_list):
    running = None
    for left_side, right_side in pairs_list:
        product = contract_cols(left_side, right_side)
        running = product if running is None else running + product
    return lax.psum_scatter(
        running.astype(jnp.bfloat16), "tp", scatter_dimension=0, tiled=True
    ).astype(jnp.float32)


def gather_layer(weight_set, layer_index):
    query_weight, key_matrix, value_matrix, out_weight, gate_weight, up_weight, down_weight = (
        weight_set
    )
    return (
        lax.all_gather(query_weight[layer_index], "fsdp", axis=0, tiled=True),
        lax.all_gather(key_matrix[layer_index], "fsdp", axis=0, tiled=True),
        lax.all_gather(value_matrix[layer_index], "fsdp", axis=0, tiled=True),
        lax.all_gather(out_weight[layer_index], "fsdp", axis=1, tiled=True),
        lax.all_gather(gate_weight[layer_index], "fsdp", axis=0, tiled=True),
        lax.all_gather(up_weight[layer_index], "fsdp", axis=0, tiled=True),
        lax.all_gather(down_weight[layer_index], "fsdp", axis=1, tiled=True),
    )


def score_block(
    query_block, heads_of_key, block_index, block_segment, position_index, segment_row, score_scale
):
    raw_dots = jnp.einsum(
        "qngd,knd->ngqk", query_block, heads_of_key, preferred_element_type=jnp.float32
    )
    allowed = (position_index[None, :] <= block_index[:, None]) & (
        segment_row[None, :] == block_segment[:, None]
    )
    return jnp.where(allowed[None, None], raw_dots * score_scale, -1e30)


def block_layout(heads_of_query, segment_row):
    sequence_length, kv_local, group_width, head_size = heads_of_query.shape
    rows_per_block = min(512, sequence_length)
    number_blocks = sequence_length // rows_per_block
    position_index = jnp.arange(sequence_length, dtype=jnp.int32)
    row_index = position_index.reshape(number_blocks, rows_per_block)
    row_segment = segment_row.reshape(number_blocks, rows_per_block)
    return (number_blocks, rows_per_block, position_index, row_index, row_segment)


def attend(heads_of_query, heads_of_key, heads_of_value, segment_row):
    sequence_length, kv_local, group_width, head_size = heads_of_query.shape
    score_scale = head_size ** (-0.5)
    number_blocks, rows_per_block, position_index, row_index, row_segment = block_layout(
        heads_of_query, segment_row
    )
    blocks_of_query = heads_of_query.reshape(
        number_blocks, rows_per_block, kv_local, group_width, head_size
    )

    def forward_block(inputs):
        query_block, block_index, block_segment = inputs
        scores = score_block(
            query_block,
            heads_of_key,
            block_index,
            block_segment,
            position_index,
            segment_row,
            score_scale,
        )
        top_score = jnp.max(scores, axis=-1, keepdims=True)
        weights = jnp.exp(scores - top_score)
        total_weight = jnp.sum(weights, axis=-1, keepdims=True)
        prob_low = (weights / total_weight).astype(jnp.bfloat16)
        block_out = jnp.einsum(
            "ngqk,knd->qngd", prob_low, heads_of_value, preferred_element_type=jnp.float32
        )
        return (block_out.astype(jnp.bfloat16), (top_score + jnp.log(total_weight))[..., 0])

    outputs, log_totals = lax.map(forward_block, (blocks_of_query, row_index, row_segment))
    return (outputs.reshape(sequence_length, kv_local * group_width * head_size), log_totals)


def attend_back(heads_of_query, heads_of_key, heads_of_value, segment_row, out_grad, log_totals):
    sequence_length, kv_local, group_width, head_size = heads_of_query.shape
    score_scale = head_size ** (-0.5)
    number_blocks, rows_per_block, position_index, row_index, row_segment = block_layout(
        heads_of_query, segment_row
    )
    blocks_of_query = heads_of_query.reshape(
        number_blocks, rows_per_block, kv_local, group_width, head_size
    )
    grad_blocks = out_grad.reshape(number_blocks, rows_per_block, kv_local, group_width, head_size)

    def backward_block(running_grads, inputs):
        key_grad, value_grad = running_grads
        query_block, grad_block, block_total, block_index, block_segment = inputs
        scores = score_block(
            query_block,
            heads_of_key,
            block_index,
            block_segment,
            position_index,
            segment_row,
            score_scale,
        )
        prob_block = jnp.exp(scores - block_total[..., None])
        prob_grad = jnp.einsum(
            "qngd,knd->ngqk", grad_block, heads_of_value, preferred_element_type=jnp.float32
        )
        inner_sum = jnp.sum(prob_block * prob_grad, axis=-1, keepdims=True)
        score_grad = (prob_block * (prob_grad - inner_sum)).astype(jnp.bfloat16)
        query_grad = (
            jnp.einsum(
                "ngqk,knd->qngd", score_grad, heads_of_key, preferred_element_type=jnp.float32
            )
            * score_scale
        )
        key_grad = (
            key_grad
            + jnp.einsum(
                "ngqk,qngd->knd", score_grad, query_block, preferred_element_type=jnp.float32
            )
            * score_scale
        )
        value_grad = value_grad + jnp.einsum(
            "ngqk,qngd->knd",
            prob_block.astype(jnp.bfloat16),
            grad_block,
            preferred_element_type=jnp.float32,
        )
        return ((key_grad, value_grad), query_grad)

    zero_keys = jnp.zeros(heads_of_key.shape, jnp.float32)
    (key_grad, value_grad), query_grad = lax.scan(
        backward_block,
        (zero_keys, zero_keys),
        (blocks_of_query, grad_blocks, log_totals, row_index, row_segment),
    )
    return (
        query_grad.reshape(sequence_length, kv_local * group_width, head_size),
        key_grad,
        value_grad,
    )


def general_plan(
    tokens,
    segment_ids,
    attn_gain,
    query_gain,
    key_gain,
    query_weight,
    key_matrix,
    value_matrix,
    out_weight,
    mlp_gain,
    gate_weight,
    up_weight,
    down_weight,
    cotangent,
):
    layer_count = attn_gain.shape[0]
    head_size = query_gain.shape[-1]
    segment_row = segment_ids[0]
    cosine_table, sine_table = rope_tables(positions_of(segment_row), head_size)
    weight_set = (
        query_weight,
        key_matrix,
        value_matrix,
        out_weight,
        gate_weight,
        up_weight,
        down_weight,
    )

    def turn_heads(raw_rows, gain_row):
        return head_norm(raw_rows, gain_row, cosine_table, sine_table)

    residual = tokens.astype(jnp.float32)
    saved_layers = []
    for layer_index in range(layer_count):
        gathered = gather_layer(weight_set, layer_index)
        wide_query, wide_key, wide_value, wide_out, wide_gate, wide_up, wide_down = gathered
        attn_normed, attn_back = jax.vjp(rms_scale, residual, attn_gain[layer_index])
        seq_rows = spread_rows(attn_normed.astype(jnp.bfloat16))
        sequence_length = seq_rows.shape[0]
        query_raw = jnp.dot(seq_rows, wide_query, preferred_element_type=jnp.float32)
        key_raw = jnp.dot(seq_rows, wide_key, preferred_element_type=jnp.float32)
        value_raw = jnp.dot(seq_rows, wide_value, preferred_element_type=jnp.float32)
        query_turned, query_back = jax.vjp(turn_heads, query_raw, query_gain[layer_index])
        key_turned, key_back = jax.vjp(turn_heads, key_raw, key_gain[layer_index])
        kv_local = key_raw.shape[1] // head_size
        heads_of_query = query_turned.astype(jnp.bfloat16).reshape(
            sequence_length, kv_local, -1, head_size
        )
        heads_of_key = key_turned.astype(jnp.bfloat16)
        heads_of_value = value_raw.astype(jnp.bfloat16).reshape(
            sequence_length, kv_local, head_size
        )
        attn_rows, log_totals = attend(heads_of_query, heads_of_key, heads_of_value, segment_row)
        residual_mid = residual + collect_rows(attn_rows, wide_out)
        mlp_normed, mlp_back = jax.vjp(rms_scale, residual_mid, mlp_gain[layer_index])
        mlp_rows = spread_rows(mlp_normed.astype(jnp.bfloat16))
        gate_proj = jnp.dot(mlp_rows, wide_gate, preferred_element_type=jnp.float32)
        upward = jnp.dot(mlp_rows, wide_up, preferred_element_type=jnp.float32)
        hidden_float, swiglu_back = jax.vjp(swiglu, gate_proj, upward)
        hidden = hidden_float.astype(jnp.bfloat16)
        residual = residual_mid + collect_rows(hidden, wide_down)
        saved_layers.append(
            (
                gathered,
                attn_back,
                seq_rows,
                query_back,
                key_back,
                heads_of_query,
                heads_of_key,
                heads_of_value,
                attn_rows,
                log_totals,
                mlp_back,
                mlp_rows,
                swiglu_back,
                hidden,
            )
        )
    result = residual.astype(jnp.bfloat16)
    residual_grad = cotangent.astype(jnp.float32)
    grad_weights = [None] * layer_count
    gain_grads = [None] * layer_count
    for layer_index in reversed(range(layer_count)):
        (
            gathered,
            attn_back,
            seq_rows,
            query_back,
            key_back,
            heads_of_query,
            heads_of_key,
            heads_of_value,
            attn_rows,
            log_totals,
            mlp_back,
            mlp_rows,
            swiglu_back,
            hidden,
        ) = saved_layers[layer_index]
        gathered = gather_layer(weight_set, layer_index)
        wide_query, wide_key, wide_value, wide_out, wide_gate, wide_up, wide_down = gathered
        grad_rows = spread_grads(residual_grad.astype(jnp.bfloat16))
        down_grad = contract_rows(hidden, grad_rows)
        hidden_grad = contract_cols(grad_rows, wide_down)
        gate_grad, upward_grad = swiglu_back(hidden_grad)
        gate_low = gate_grad.astype(jnp.bfloat16)
        upward_low = upward_grad.astype(jnp.bfloat16)
        gate_wgrad = contract_rows(mlp_rows, gate_low)
        upward_wgrad = contract_rows(mlp_rows, upward_low)
        normed_grad = collect_grads(((gate_low, wide_gate), (upward_low, wide_up)))
        residual_part, mlp_gain_grad = mlp_back(normed_grad)
        residual_grad = residual_grad + residual_part
        grad_rows = spread_grads(residual_grad.astype(jnp.bfloat16))
        sequence_length = grad_rows.shape[0]
        out_wgrad = contract_rows(attn_rows, grad_rows)
        mixed_grad = contract_cols(grad_rows, wide_out).astype(jnp.bfloat16)
        query_grad, key_grad, value_grad = attend_back(
            heads_of_query,
            heads_of_key,
            heads_of_value,
            segment_row,
            mixed_grad.reshape(heads_of_query.shape),
            log_totals,
        )
        query_raw_grad, query_gain_grad = query_back(query_grad)
        key_raw_grad, key_gain_grad = key_back(key_grad)
        query_low = query_raw_grad.astype(jnp.bfloat16)
        key_low = key_raw_grad.astype(jnp.bfloat16)
        value_low = value_grad.reshape(sequence_length, -1).astype(jnp.bfloat16)
        query_wgrad = contract_rows(seq_rows, query_low)
        key_wgrad = contract_rows(seq_rows, key_low)
        value_wgrad = contract_rows(seq_rows, value_low)
        normed_grad = collect_grads(
            ((query_low, wide_query), (key_low, wide_key), (value_low, wide_value))
        )
        residual_part, attn_gain_grad = attn_back(normed_grad)
        residual_grad = residual_grad + residual_part
        grad_weights[layer_index] = (
            lax.psum_scatter(
                query_wgrad.astype(jnp.bfloat16), "fsdp", scatter_dimension=0, tiled=True
            ).astype(jnp.float32),
            lax.psum_scatter(
                key_wgrad.astype(jnp.bfloat16), "fsdp", scatter_dimension=0, tiled=True
            ).astype(jnp.float32),
            lax.psum_scatter(
                value_wgrad.astype(jnp.bfloat16), "fsdp", scatter_dimension=0, tiled=True
            ).astype(jnp.float32),
            lax.psum_scatter(
                out_wgrad.astype(jnp.bfloat16), "fsdp", scatter_dimension=1, tiled=True
            ).astype(jnp.float32),
            lax.psum_scatter(
                gate_wgrad.astype(jnp.bfloat16), "fsdp", scatter_dimension=0, tiled=True
            ).astype(jnp.float32),
            lax.psum_scatter(
                upward_wgrad.astype(jnp.bfloat16), "fsdp", scatter_dimension=0, tiled=True
            ).astype(jnp.float32),
            lax.psum_scatter(
                down_grad.astype(jnp.bfloat16), "fsdp", scatter_dimension=1, tiled=True
            ).astype(jnp.float32),
        )
        gain_grads[layer_index] = (attn_gain_grad, query_gain_grad, key_gain_grad, mlp_gain_grad)
    local_stacks = tuple(
        (
            jnp.stack([grad_weights[layer_index][member] for layer_index in range(layer_count)])
            for member in range(7)
        )
    )
    gain_stacks = tuple(
        (
            jnp.stack([gain_grads[layer_index][member] for layer_index in range(layer_count)])
            for member in range(4)
        )
    )
    summed = lax.psum(
        (gain_stacks[0], gain_stacks[1], gain_stacks[2], gain_stacks[3]), ("fsdp", "tp")
    )
    return (
        result,
        residual_grad,
        summed[0],
        summed[1],
        summed[2],
        local_stacks[0],
        local_stacks[1],
        local_stacks[2],
        local_stacks[3],
        summed[3],
        local_stacks[4],
        local_stacks[5],
        local_stacks[6],
    )


def plane_send(values, distance):
    size = lax.axis_size("fsdp")
    return lax.ppermute(values, "fsdp", [(i, i ^ distance) for i in range(size)])


def plane_place():
    return lax.axis_index("fsdp").astype(jnp.int32).reshape(1)


def low(values):
    return values.astype(jnp.bfloat16)


def wide(values):
    return values.astype(jnp.float32)


def add_low(left, right):
    return low(wide(left) + wide(right))


def gather_plane(own, use=None):
    half = own.shape[0] // 2
    near = [own, plane_send(own, 1)]
    made = [use(near, 0)] if use else []
    across_x, across_y, made = lax.optimization_barrier(
        (plane_send(own, 2), plane_send(own, 4), made)
    )
    far = plane_send(across_y[:half], 2), plane_send(across_x[half:], 4)
    across = [across_x, plane_send(across_x, 1), across_y, plane_send(across_y, 1)]
    if use:
        made = made + [use(across, 1)]
    top, bottom, made = lax.optimization_barrier((*far, made))
    last = [top, bottom, plane_send(top, 1), plane_send(bottom, 1)]
    if use:
        return [near, across, last], made + [use(last, 2)]
    return [near, across, last]


def shard_of(sets, d):
    return (sets[0], d) if d < 2 else (sets[1], d - 2) if d < 6 else (sets[2], d - 6)


def reduce_plane(part, join=()):
    odd = part((7, 5, 3, 1), None)
    received = [plane_send(v, 1) for v in odd]
    (far,) = part((6,), received[:1])
    half = far.shape[0] // 2
    top, bottom = lax.optimization_barrier(
        (plane_send(far[:half], 2), plane_send(far[half:], 4))
    )
    by_y, by_x, here = part((4, 2, 0), received[1:])
    by_y = jnp.concatenate([add_low(by_y[:half], top), by_y[half:]])
    by_x = jnp.concatenate([by_x[:half], add_low(by_x[half:], bottom)])
    by_x, by_y, join = lax.optimization_barrier((by_x, by_y, join))
    from_x = plane_send(by_x, 2)
    from_y = plane_send(by_y, 4)
    return wide(here) + wide(from_x) + wide(from_y), far, join


def sum_line(values):
    size = lax.axis_size("tp")
    if size & (size - 1):
        return lax.psum(values, "tp")
    distance = 1
    while distance < size:
        pairs = [(i, i ^ distance) for i in range(size)]
        values = values + lax.ppermute(values, "tp", pairs)
        distance *= 2
    return values


def sum_plane(values):
    for distance in (1, 2, 4):
        values = values + plane_send(values, distance)
    return values


def after(token, *values):
    if token is None:
        return values
    return lax.optimization_barrier((token, *values))[1:]


def line_gather(own, axis=0):
    return lax.all_gather(own, "tp", axis=axis, tiled=True)


def line_reduce(terms, axis=0):
    return lax.psum_scatter(terms, "tp", scatter_dimension=axis, tiled=True)


def assemble(sets, block_shape, axis, places):
    size = sum(len(held) for _, held in sets)
    block = block_shape[axis]
    shape = list(block_shape)
    shape[axis] = size * block

    def kernel(place_ref, *refs):
        out, d = refs[len(sets)], 0
        for (_, held), ref in zip(sets, refs):
            for i in held:
                start = pl.multiple_of(place_ref[d] * block, block)
                where = tuple([slice(None)] * axis + [pl.ds(start, block)])
                out[where] = ref[...] if i is None else ref[i]
                d += 1

    return pl.pallas_call(
        kernel,
        out_shape=jax.ShapeDtypeStruct(tuple(shape), sets[0][0].dtype),
        in_specs=[pl.BlockSpec(memory_space=pltpu.SMEM)]
        + [pl.BlockSpec(memory_space=pltpu.VMEM)] * len(sets),
        out_specs=pl.BlockSpec(memory_space=pltpu.VMEM),
        compiler_params=kernel_params(12),
        cost_estimate=kernel_cost(),
        name="assemble",
    )(places, *(array for array, _ in sets))


def block_at(array, index, block, axis):
    return lax.dynamic_slice_in_dim(array, index * block, block, axis)


def swap(array, axis, into, start=None, done=None, first=None):
    size = lax.axis_size("fsdp")
    places = lax.axis_index("fsdp").astype(jnp.int32) ^ jnp.arange(size, dtype=jnp.int32)
    block = array.shape[axis] // size
    (array,) = after(start, array)
    pieces = [block_at(array, places[d], block, axis) for d in range(size)]
    other = plane_send(jnp.stack(pieces[1::2]), 1)
    chips = [plane_send(jnp.stack([pieces[d], other[d // 2]]), d) for d in (6, 4, 2)]
    if first is not None:
        first.extend(chips)
    other, *chips = after(done, other[0], *chips)
    sets = [(pieces[0], (None,)), (other, (None,))] + [(v, (0, 1)) for v in reversed(chips)]
    return assemble(sets, pieces[0].shape, into, places)


def line_swap(array, start=None, done=None):
    size = lax.axis_size("tp")
    place = lax.axis_index("tp").astype(jnp.int32)
    block = array.shape[0] // size
    sources = (place - jnp.arange(size, dtype=jnp.int32)) % size
    (array,) = after(start, array)
    moved = []
    for step in range(1, size):
        piece = block_at(array, (place + step) % size, block, 0)
        pairs = [(i, (i + step) % size) for i in range(size)]
        moved.append(lax.ppermute(piece, "tp", pairs))
    moved = after(done, *moved)
    own = block_at(array, place, block, 0)
    return assemble([(v, (None,)) for v in (own, *moved)], own.shape, 0, sources)


def line_rows(rows, start=None, done=None):
    size, line = lax.axis_size("fsdp"), lax.axis_size("tp")
    count, width = rows.shape
    blocks = line_swap(rows, start, done).reshape(line, size // line, count // size, width)
    return blocks.transpose(1, 0, 2, 3).reshape(count, width)


def line_rows_back(rows, start=None, done=None):
    size, line = lax.axis_size("fsdp"), lax.axis_size("tp")
    count, width = rows.shape
    blocks = rows.reshape(size // line, line, count // size, width).transpose(1, 0, 2, 3)
    return line_swap(blocks.reshape(count, width), start, done)


def plane_segments(segment_ids):
    size, line = lax.axis_size("fsdp"), lax.axis_size("tp")
    rows = segment_ids
    for distance in (1, 2, 4):
        rows = jnp.concatenate([rows, plane_send(rows, distance)])
    local = size // line
    wanted = lax.axis_index("tp") * local + jnp.arange(local)
    return rows[wanted ^ lax.axis_index("fsdp")]


def attention_weights(query_shard, key_shard, value_shard, out_shard):
    size, line = lax.axis_size("fsdp"), lax.axis_size("tp")
    per, depth = size // line, query_shard.shape[0]
    pack = jnp.concatenate(
        [
            query_shard.T.reshape(per, -1, depth),
            key_shard.T.reshape(per, -1, depth),
            value_shard.T.reshape(per, -1, depth),
            out_shard.reshape(per, -1, depth),
        ],
        axis=1,
    )
    return line_gather(pack)


def turn(values, cosine, sine):
    return values * cosine + pltpu.roll(values, values.shape[1] // 2, 1) * sine


def turn_back(values, cosine, sine):
    return values * cosine - pltpu.roll(values, values.shape[1] // 2, 1) * sine


def inverse_rms(values):
    return lax.rsqrt(jnp.mean(values * values, axis=-1, keepdims=True) + EPSILON)


def rows_in_order(place, groups, target, pick):
    shards = [(ref, e) for ref in groups for e in range(ref.shape[0])]
    for d, (ref, e) in enumerate(shards):
        blocks, block = ref.shape[2], ref.shape[3]
        for i in range(blocks):
            start = pl.multiple_of((i * len(shards) + (place ^ d)) * block, block)
            target[pl.ds(start, block), :] = pick(ref[e, 0, i])


def rows_from_order(place, source, groups):
    shards = [(ref, e) for ref in groups for e in range(ref.shape[0])]
    for d, (ref, e) in enumerate(shards):
        blocks, block = ref.shape[2], ref.shape[3]
        for i in range(blocks):
            start = pl.multiple_of((i * len(shards) + (place ^ d)) * block, block)
            ref[e, 0, i] = source[pl.ds(start, block), :].astype(ref.dtype)


def head_columns(index, head):
    return slice(index * head, (index + 1) * head)


def heads_from_raw(nat, cos_ref, sin_ref, gains, heads, low_ref, rows):
    head = cos_ref.shape[-1]
    for start in range(0, nat.shape[0], rows):
        here = slice(start, start + rows)
        cosine, sine = cos_ref[0, here, :], sin_ref[0, here, :]
        for h in range(heads + 2):
            raw = nat[here, head_columns(h, head)]
            if h <= heads:
                gain = gains[0] if h < heads else gains[1]
                raw = turn(raw * inverse_rms(raw) * gain[...], cosine, sine)
            low_ref[here, head_columns(h, head)] = raw.astype(low_ref.dtype)


def block_operands(low_ref, start, rows, heads, head):
    query = jnp.concatenate(
        [low_ref[start : start + rows, head_columns(h, head)] for h in range(heads)], axis=0
    )
    key = low_ref[: start + rows, head_columns(heads, head)]
    value = low_ref[: start + rows, head_columns(heads + 1, head)]
    return query, key, value


def masked_scores(key, query, first_ref, start, rows, heads, scale):
    scores = lax.dot_general(
        key, query, (((1,), (1,)), ((), ())), preferred_element_type=jnp.float32
    )
    shape = (key.shape[0], rows)
    index = lax.broadcasted_iota(jnp.int32, shape, 0)
    mine = lax.broadcasted_iota(jnp.int32, shape, 1) + start
    first = first_ref[0, :, start : start + rows]
    allowed = (index <= mine) & (index >= first)
    allowed = jnp.concatenate([allowed] * heads, axis=1)
    return jnp.where(allowed, scores * scale, -1e30)


def attend_kernel(groups, heads, rows, *refs):
    place = refs[0][0]
    raw_refs = refs[1 : 1 + groups]
    cos_ref, sin_ref, first_ref, query_gain, key_gain = refs[1 + groups : 6 + groups]
    out_refs = refs[6 + groups : 6 + 2 * groups]
    total_ref, nat, low_ref, mixed = refs[6 + 2 * groups :]
    head = cos_ref.shape[-1]
    rows_in_order(place, raw_refs, nat, lambda v: v)
    heads_from_raw(nat, cos_ref, sin_ref, (query_gain, key_gain), heads, low_ref, rows)
    for i in range(nat.shape[0] // rows):
        start = i * rows
        query, key, value = block_operands(low_ref, start, rows, heads, head)
        scores = masked_scores(key, query, first_ref, start, rows, heads, head ** (-0.5))
        top = jnp.max(scores, axis=0, keepdims=True)
        weights = jnp.exp(scores - top)
        total = jnp.sum(weights, axis=0, keepdims=True)
        total_ref[0, i : i + 1, :] = top + jnp.log(total)
        prob = (weights * (1.0 / total)).astype(jnp.bfloat16)
        out = lax.dot_general(
            prob, value, (((0,), (0,)), ((), ())), preferred_element_type=jnp.float32
        ).astype(jnp.bfloat16)
        for h in range(heads):
            mixed[start : start + rows, head_columns(h, head)] = out[h * rows : (h + 1) * rows]
    rows_from_order(place, mixed, out_refs)


def attend_back_kernel(groups, heads, rows, *refs):
    place = refs[0][0]
    raw_refs = refs[1 : 1 + groups]
    grad_refs = refs[1 + groups : 1 + 2 * groups]
    rest = refs[1 + 2 * groups :]
    total_ref, cos_ref, sin_ref, first_ref, query_gain, key_gain = rest[:6]
    out_refs = rest[6 : 6 + groups]
    gain_ref, nat, low_ref, mixed, grads, key_sum, value_sum, done = rest[6 + groups :]
    head = cos_ref.shape[-1]
    scale = head ** (-0.5)
    rows_in_order(place, raw_refs, nat, lambda v: v)
    rows_in_order(place, grad_refs, mixed, lambda v: v)
    heads_from_raw(nat, cos_ref, sin_ref, (query_gain, key_gain), heads, low_ref, rows)
    key_sum[...] = jnp.zeros_like(key_sum)
    value_sum[...] = jnp.zeros_like(value_sum)
    for i in range(nat.shape[0] // rows):
        start = i * rows
        stop = start + rows
        query, key, value = block_operands(low_ref, start, rows, heads, head)
        out_grad = jnp.concatenate(
            [mixed[start:stop, head_columns(h, head)] for h in range(heads)], axis=0
        )
        scores = masked_scores(key, query, first_ref, start, rows, heads, scale)
        prob = jnp.exp(scores - total_ref[0, i : i + 1, :])
        prob_grad = lax.dot_general(
            value, out_grad, (((1,), (1,)), ((), ())), preferred_element_type=jnp.float32
        )
        inner = jnp.sum(prob * prob_grad, axis=0, keepdims=True)
        score_grad = (prob * (prob_grad - inner)).astype(jnp.bfloat16)
        value_sum[:stop, :] += jnp.dot(
            prob.astype(jnp.bfloat16), out_grad, preferred_element_type=jnp.float32
        )
        key_sum[:stop, :] += jnp.dot(score_grad, query, preferred_element_type=jnp.float32)
        query_grad = lax.dot_general(
            score_grad, key, (((0,), (0,)), ((), ())), preferred_element_type=jnp.float32
        )
        for h in range(heads):
            grads[start:stop, head_columns(h, head)] = query_grad[h * rows : (h + 1) * rows] * scale
    sums = [jnp.zeros((1, head), jnp.float32)] * 2
    for start in range(0, nat.shape[0], rows):
        here = slice(start, start + rows)
        cosine, sine = cos_ref[0, here, :], sin_ref[0, here, :]
        for h in range(heads + 1):
            kind = 0 if h < heads else 1
            gain = (query_gain, key_gain)[kind][...]
            grad = grads[here, head_columns(h, head)] if h < heads else key_sum[here, :] * scale
            raw = nat[here, head_columns(h, head)]
            inverse = inverse_rms(raw)
            grad = turn_back(grad, cosine, sine)
            sums[kind] += jnp.sum(grad * raw * inverse, axis=0, keepdims=True)
            grad = grad * gain
            middle = jnp.mean(grad * raw, axis=-1, keepdims=True)
            done[here, head_columns(h, head)] = (
                inverse * grad - raw * (inverse * inverse * inverse) * middle
            ).astype(done.dtype)
        done[here, head_columns(heads + 1, head)] = value_sum[here, :].astype(done.dtype)
    gain_ref[0] = jnp.concatenate(sums, axis=0)
    rows_from_order(place, done, out_refs)


def kernel_cost(flops=1024):
    return pl.CostEstimate(flops=flops // 2, bytes_accessed=1024, transcendentals=0)


def kernel_params(mib=48):
    return pltpu.CompilerParams(vmem_limit_bytes=mib * 1024 * 1024)


def group_specs(arrays):
    def spec(array):
        return pl.BlockSpec((array.shape[0], 1) + array.shape[2:], lambda s: (0, s, 0, 0, 0))

    return [spec(array) for array in arrays]


def table_specs(length, head):
    table = pl.BlockSpec((1, length, head), lambda s: (s, 0, 0))
    gain = pl.BlockSpec((1, head), lambda s: (0, 0))
    return [table, table, pl.BlockSpec((1, 1, length), lambda s: (s, 0, 0)), gain, gain]


def grouped(rows, shards, local, blocks):
    count, width = rows.shape
    return rows.reshape(shards, local, blocks, count // (shards * local * blocks), width)


def plane_attend(raw, tables, first, gains, rows=256):
    local, length, head = tables[0].shape
    width = raw[0].shape[-1]
    heads = width // head - 2
    groups = len(raw)
    outs = [jax.ShapeDtypeStruct(v.shape[:-1] + (heads * head,), jnp.bfloat16) for v in raw]
    totals = jax.ShapeDtypeStruct((local, length // rows, heads * rows), jnp.float32)
    out = pl.pallas_call(
        functools.partial(attend_kernel, groups, heads, rows),
        grid=(local,),
        out_shape=outs + [totals],
        in_specs=[pl.BlockSpec(memory_space=pltpu.SMEM)]
        + group_specs(raw)
        + table_specs(length, head),
        out_specs=group_specs(outs)
        + [pl.BlockSpec((1,) + totals.shape[1:], lambda s: (s, 0, 0))],
        scratch_shapes=[
            pltpu.VMEM((length, width), jnp.float32),
            pltpu.VMEM((length, width), jnp.bfloat16),
            pltpu.VMEM((length, heads * head), jnp.bfloat16),
        ],
        compiler_params=kernel_params(24),
        cost_estimate=kernel_cost(local * heads * length * length * head * 8),
        name="attend",
    )(plane_place(), *raw, *tables, first, *gains)
    return out[:groups], out[groups]


def plane_attend_back(raw, out_grad, totals, tables, first, gains, rows=256):
    local, length, head = tables[0].shape
    width = raw[0].shape[-1]
    heads = width // head - 2
    groups = len(raw)
    out = pl.pallas_call(
        functools.partial(attend_back_kernel, groups, heads, rows),
        grid=(local,),
        out_shape=[jax.ShapeDtypeStruct(v.shape, jnp.bfloat16) for v in raw]
        + [jax.ShapeDtypeStruct((local, 2, head), jnp.float32)],
        in_specs=[pl.BlockSpec(memory_space=pltpu.SMEM)]
        + group_specs(raw)
        + group_specs(out_grad)
        + [pl.BlockSpec((1,) + totals.shape[1:], lambda s: (s, 0, 0))]
        + table_specs(length, head),
        out_specs=group_specs(raw) + [pl.BlockSpec((1, 2, head), lambda s: (s, 0, 0))],
        scratch_shapes=[
            pltpu.VMEM((length, width), jnp.float32),
            pltpu.VMEM((length, width), jnp.bfloat16),
            pltpu.VMEM((length, heads * head), jnp.bfloat16),
            pltpu.VMEM((length, heads * head), jnp.float32),
            pltpu.VMEM((length, head), jnp.float32),
            pltpu.VMEM((length, head), jnp.float32),
            pltpu.VMEM((length, width), jnp.bfloat16),
        ],
        compiler_params=kernel_params(32),
        cost_estimate=kernel_cost(local * heads * length * length * head * 16),
        name="attend_back",
    )(plane_place(), *raw, *out_grad, totals, *tables, first, *gains)
    return out[:groups], jnp.sum(out[groups], axis=0)


def whole_spec(array):
    return pl.BlockSpec(
        array.shape, lambda n: (0,) * array.ndim, pipeline_mode=pl.Buffered(buffer_count=1)
    )


def dot_cols(left, right):
    return lax.dot_general(
        left, right, (((1,), (1,)), ((), ())), preferred_element_type=jnp.float32
    )


def joined(refs, rows_ref):
    @pl.when(pl.program_id(0) == 0)
    def _():
        start = 0
        for ref in refs:
            rows_ref[start : start + ref.shape[0], :] = ref[...]
            start += ref.shape[0]

    return rows_ref[...]


def joined_scratch(pieces):
    count = sum(v.shape[0] for v in pieces)
    return [pltpu.VMEM((count, pieces[0].shape[1]), pieces[0].dtype)]


def project_kernel(count, *refs):
    weight, out, rows_ref = refs[count:]
    out[...] = dot_cols(joined(refs[:count], rows_ref), weight[...]).astype(out.dtype)


def project(pieces, weight, first, width, dtype, tile=256):
    count = sum(v.shape[0] for v in pieces)
    return pl.pallas_call(
        functools.partial(project_kernel, len(pieces)),
        grid=(width // tile,),
        out_shape=jax.ShapeDtypeStruct((count, width), dtype),
        in_specs=[whole_spec(v) for v in pieces]
        + [pl.BlockSpec((tile, weight.shape[1]), lambda n: (first // tile + n, 0))],
        out_specs=pl.BlockSpec((count, tile), lambda n: (0, n)),
        scratch_shapes=joined_scratch(pieces),
        compiler_params=kernel_params(16),
        cost_estimate=kernel_cost(2 * count * width * weight.shape[1]),
        name="project",
    )(*pieces, weight)


def units_kernel(count, *refs):
    gate_rows, up_rows, hidden_ref, gate_ref, up_ref, rows_ref = refs[count:]
    rows = joined(refs[:count], rows_ref)
    gate = dot_cols(rows, gate_rows[0])
    up = dot_cols(rows, up_rows[0])
    hidden_ref[...] = (gate * up / (1.0 + jnp.exp(-gate))).astype(hidden_ref.dtype)
    gate_ref[...] = gate.astype(gate_ref.dtype)
    up_ref[...] = up.astype(up_ref.dtype)


def unit_spec(weights, kind, tile):
    return pl.BlockSpec((1, tile, weights.shape[2]), lambda n: (kind, n, 0))


def hidden_units(pieces, weights, tile=256):
    count = sum(v.shape[0] for v in pieces)
    shape = jax.ShapeDtypeStruct((count, weights.shape[1]), jnp.bfloat16)
    return pl.pallas_call(
        functools.partial(units_kernel, len(pieces)),
        grid=(weights.shape[1] // tile,),
        out_shape=[shape] * 3,
        in_specs=[whole_spec(v) for v in pieces]
        + [unit_spec(weights, kind, tile) for kind in (0, 1)],
        out_specs=[pl.BlockSpec((count, tile), lambda n: (0, n))] * 3,
        scratch_shapes=joined_scratch(pieces),
        compiler_params=kernel_params(20),
        cost_estimate=kernel_cost(4 * count * weights.shape[1] * weights.shape[2]),
        name="hidden_units",
    )(*pieces, weights, weights)


def units_back_kernel(count, *refs):
    down_rows, gate_ref, up_ref, gate_grad, up_grad, rows_ref = refs[count:]
    grad = dot_cols(joined(refs[:count], rows_ref), down_rows[0])
    gate, up = wide(gate_ref[...]), wide(up_ref[...])
    sigmoid = 1.0 / (1.0 + jnp.exp(-gate))
    gate_grad[...] = (grad * up * sigmoid * (1.0 + gate * (1.0 - sigmoid))).astype(gate_grad.dtype)
    up_grad[...] = (grad * gate * sigmoid).astype(up_grad.dtype)


def hidden_units_back(pieces, weights, gate, up, tile=256):
    count = gate.shape[0]
    side = pl.BlockSpec((count, tile), lambda n: (0, n))
    return pl.pallas_call(
        functools.partial(units_back_kernel, len(pieces)),
        grid=(weights.shape[1] // tile,),
        out_shape=[jax.ShapeDtypeStruct(gate.shape, jnp.bfloat16)] * 2,
        in_specs=[whole_spec(v) for v in pieces] + [unit_spec(weights, 2, tile), side, side],
        out_specs=[side, side],
        scratch_shapes=joined_scratch(pieces),
        compiler_params=kernel_params(20),
        cost_estimate=kernel_cost(2 * count * weights.shape[1] * weights.shape[2]),
        name="hidden_units_back",
    )(*pieces, weights, gate, up)


def parts_kernel(shards, terms, adding, *refs):
    lefts, weights = refs[: shards * terms], refs[shards * terms : (shards + 1) * terms]
    adds = refs[(shards + 1) * terms : -shards]
    outs = refs[-shards:]
    total = None
    for t in range(terms):
        weight = weights[t][...]
        left = jnp.concatenate([lefts[i * terms + t][...] for i in range(shards)], axis=0)
        term = jnp.dot(
            left, weight.reshape(weight.shape[-2:]), preferred_element_type=jnp.float32
        )
        total = term if total is None else total + term
    rows = outs[0].shape[0]
    for i in range(shards):
        mine = total[i * rows : (i + 1) * rows]
        if adding:
            mine = mine + wide(adds[i][...])
        outs[i][...] = mine.astype(outs[i].dtype)


def parts_of(terms, ds, adds, tile=512):
    lefts, specs = [], []
    for d in ds:
        for sets, _, _ in terms:
            array, place = shard_of(sets, d)
            rows = sets[0].shape[0] // 2
            lefts.append(array)
            specs.append(
                pl.BlockSpec(
                    (rows, array.shape[1]),
                    lambda n, p=place: (p, 0),
                    pipeline_mode=pl.Buffered(buffer_count=1),
                )
            )
    width = terms[0][1].shape[-1]
    side = pl.BlockSpec((rows, tile), lambda n: (0, n))
    return pl.pallas_call(
        functools.partial(parts_kernel, len(ds), len(terms), adds is not None),
        grid=(width // tile,),
        out_shape=[jax.ShapeDtypeStruct((rows, width), jnp.bfloat16)] * len(ds),
        in_specs=specs + [spec for _, _, spec in terms] + [side] * len(adds or ()),
        out_specs=[side] * len(ds),
        compiler_params=kernel_params(16),
        cost_estimate=kernel_cost(2 * len(ds) * rows * width * sum(v.shape[-1] for v in lefts[: len(terms)])),
        name="parts",
    )(*lefts, *(weights for _, weights, _ in terms), *(adds or ()))


def rows_spec(kind, weights, tile=512):
    return pl.BlockSpec((1, weights.shape[1], tile), lambda n: (kind, 0, n))


def pack_spec(block, height, tile=512):
    return pl.BlockSpec((height, tile), lambda n: (block, n))


def outer_kernel(plan, *refs):
    for lefts, rights, place in plan:
        total = None
        for left, pieces in zip(lefts, rights):
            right = jnp.concatenate([refs[p][...] for p in pieces], axis=0)
            term = lax.dot_general(
                refs[left][...], right, (((0,), (0,)), ((), ())), preferred_element_type=jnp.float32
            )
            total = term if total is None else total + term
        refs[-1][place] = total.astype(refs[-1].dtype)


def outer(products, shape, tile=512):
    operands, specs, plan, seen = [], [], [], {}

    def operand(array, split):
        if id(array) not in seen:
            seen[id(array)] = len(operands)
            operands.append(array)
            specs.append(
                pl.BlockSpec((array.shape[0], tile), lambda n: (0, n))
                if split
                else pl.BlockSpec(
                    array.shape, lambda n: (0, 0), pipeline_mode=pl.Buffered(buffer_count=1)
                )
            )
        return seen[id(array)]

    for lefts, rights, place in products:
        plan.append(
            (
                [operand(v, False) for v in lefts],
                [[operand(v, True) for v in pieces] for pieces in rights],
                place,
            )
        )
    block = shape[:-1] + (tile,)
    return pl.pallas_call(
        functools.partial(outer_kernel, plan),
        grid=(shape[-1] // tile,),
        out_shape=jax.ShapeDtypeStruct(shape, jnp.bfloat16),
        in_specs=specs,
        out_specs=pl.BlockSpec(block, lambda n: (0,) * (len(shape) - 1) + (n,)),
        compiler_params=kernel_params(56),
        cost_estimate=kernel_cost(2 * shape[-1] * sum(v.size for lefts, _, _ in products for v in lefts)),
        name="outer",
    )(*operands)


def plane_plan(
    tokens,
    segment_ids,
    attn_gain,
    query_gain,
    key_gain,
    query_weight,
    key_matrix,
    value_matrix,
    out_weight,
    mlp_gain,
    gate_weight,
    up_weight,
    down_weight,
    cotangent,
):
    layers = attn_gain.shape[0]
    head = query_gain.shape[-1]
    size, line = lax.axis_size("fsdp"), lax.axis_size("tp")
    local = size // line
    segments = plane_segments(segment_ids)
    length = segments.shape[1]
    positions = jax.vmap(positions_of)(segments)
    first = (jnp.arange(length, dtype=jnp.int32)[None] - positions).reshape(local, 1, length)
    cosine_table, sine_table = rope_tables(positions.reshape(-1), head)
    turned_sign = jnp.where(jnp.arange(head) < head // 2, -1.0, 1.0)
    tables = (
        cosine_table.reshape(local, length, head),
        (sine_table * turned_sign).reshape(local, length, head),
    )
    query_count = query_weight.shape[2] * line // size
    key_count = key_matrix.shape[2] * line // size
    split = query_count + 2 * key_count

    def group(sets):
        counts = [v.shape[0] * size // sum(u.shape[0] for u in sets) for v in sets]
        return [grouped(v, count, local, line) for v, count in zip(sets, counts)]

    def flat(sets):
        return [v.reshape(-1, v.shape[-1]) for v in sets]

    def hold(token, sets):
        return [list(after(token, *v)) for v in sets]

    def reduce_down(hidden, weights):
        term = (hidden, weights, rows_spec(2, weights))
        return reduce_plane(lambda ds, adds: parts_of([term], ds, adds))[0]

    attn_sets, attn_gathered, hidden_sets = ([None] * layers for _ in range(3))

    def fetch_attn(index, token):
        shards = (query_weight[index], key_matrix[index], value_matrix[index], out_weight[index])
        attn_gathered[index] = attention_weights(*after(token, *shards))

    fetch_attn(0, None)
    exchanged = []
    both = jnp.concatenate([tokens, cotangent], axis=1)
    both = swap(both, 0, 0, None, None, exchanged)
    gate_weight, up_weight, down_weight = after(
        tuple(exchanged), gate_weight, up_weight, down_weight
    )
    hidden_shards = jnp.stack(
        [gate_weight.swapaxes(1, 2), up_weight.swapaxes(1, 2), down_weight], axis=1
    ).reshape(-1, *down_weight.shape[1:])
    both = line_rows(both)
    both, attn_gathered[0] = lax.optimization_barrier((both, attn_gathered[0]))
    hidden_shards, first = lax.optimization_barrier((hidden_shards, first))
    hidden_shards = swap(hidden_shards, 1, 2, None, both)
    hidden_shards = hidden_shards.reshape(layers, -1, *hidden_shards.shape[1:])
    residual, grad = wide(both[:, : tokens.shape[1]]), wide(both[:, tokens.shape[1] :])
    saved = []
    for index in range(layers):
        attn_sets[index] = pack = swap(attn_gathered[index], 0, 2)[0]
        gains = (query_gain[index][None], key_gain[index][None])
        normed, attn_back = jax.vjp(rms_scale, residual, attn_gain[index])
        rows = gather_plane(low(normed))
        if index == 0:
            hidden_sets[0] = line_gather(after(attn_gathered[0], hidden_shards[0])[0], 1)
        raw = group([project(v, pack, 0, split, jnp.float32) for v in rows])
        if index + 1 < layers:
            fetch_attn(index + 1, raw[0])
        mixed, totals = plane_attend(raw, tables, first, gains)
        mixed = flat(mixed)
        out_term = (mixed, pack, pack_spec(split // query_count, query_count))
        total, *_ = reduce_plane(lambda ds, adds: parts_of([out_term], ds, adds))
        middle = residual + total
        weights = hidden_sets[index]
        normed, mlp_back = jax.vjp(rms_scale, middle, mlp_gain[index])
        mlp_rows = gather_plane(low(normed))
        hidden, gates, ups = zip(*(hidden_units(v, weights) for v in mlp_rows))
        if index + 1 < layers:
            hidden_sets[index + 1] = line_gather(
                after(mlp_rows[2][0], hidden_shards[index + 1])[0], 1
            )
        if index + 1 < layers:
            residual = middle + reduce_down(hidden, weights)
        else:
            residual = middle
        saved.append(
            (attn_back, rows, raw, mixed, totals, mlp_back, mlp_rows, gates, ups, hidden)
        )
    pack_grads, pack_sums, gain_grads, hidden_sums, hidden_grads = (
        [None] * layers for _ in range(5)
    )
    for index in reversed(range(layers)):
        pack = attn_sets[index]
        gains = (query_gain[index][None], key_gain[index][None])
        weights = hidden_sets[index]
        attn_back, rows, raw, mixed, totals = saved[index][:5]
        mlp_back, mlp_rows, gates, ups, hidden = saved[index][5:]
        if index + 1 == layers:
            (grad,) = after(tuple(mlp_rows[2]), grad)
        grad_rows, unit_grads = gather_plane(
            low(grad), lambda v, i: hidden_units_back(v, weights, gates[i], ups[i])
        )
        gate_grads, up_grads = zip(*unit_grads)
        unit_terms = [
            (gate_grads, weights, rows_spec(0, weights)),
            (up_grads, weights, rows_spec(1, weights)),
        ]
        above = ()
        if index + 1 < layers:
            above = swap(pack_grads[index + 1][None], 2, 0, gate_grads[2])
        normed_grad, token, above = reduce_plane(
            lambda ds, adds: parts_of(unit_terms, ds, adds), above
        )
        (held,) = after(token, gate_grads[0])
        terms = outer(
            [
                ((held, *gate_grads[1:]), mlp_rows, 0),
                (up_grads, mlp_rows, 1),
                (hidden, grad_rows, 2),
            ],
            weights.shape,
        )
        normed_grad, terms = lax.optimization_barrier((normed_grad, terms))
        if index + 1 < layers:
            done = hidden_sums[index + 1]
            pack_sums[index + 1] = line_reduce(after(done, above)[0])
        hidden_sums[index] = line_reduce(terms, 1)
        grad_part, mlp_gain_grad = mlp_back(normed_grad)
        grad = grad + grad_part
        grad_rows, mixed_grad = gather_plane(
            low(grad), lambda v, i: project(v, pack, split, query_count, jnp.bfloat16)
        )
        mixed_grad = group(mixed_grad)
        raw_grad, head_gain_grads = plane_attend_back(raw, mixed_grad, totals, tables, first, gains)
        raw_grad = flat(raw_grad)
        if index + 1 == layers:
            result = residual + reduce_down(after(normed_grad, *hidden), weights)
            result, *raw_grad = lax.optimization_barrier((result, *raw_grad))
        if index + 1 < layers:
            hidden_grads[index + 1] = swap(hidden_sums[index + 1], 2, 1, mixed_grad[2])
            hidden_grads[index + 1], *raw_grad = lax.optimization_barrier(
                (hidden_grads[index + 1], *raw_grad)
            )
        raw_term = (raw_grad, pack, pack_spec(0, split))
        normed_grad, token, *_ = reduce_plane(
            lambda ds, adds: parts_of([raw_term], ds, adds)
        )
        (held,) = after(token, mixed[0])
        pack_grad = outer(
            [
                (raw_grad, rows, slice(0, split)),
                ((held, *mixed[1:]), grad_rows, slice(split, split + query_count)),
            ],
            pack.shape,
        )
        normed_grad, pack_grad = lax.optimization_barrier((normed_grad, pack_grad))
        pack_grads[index] = pack_grad
        grad_part, attn_gain_grad = attn_back(normed_grad)
        grad = grad + grad_part
        gain_grads[index] = jnp.concatenate(
            [attn_gain_grad, mlp_gain_grad, head_gain_grads[0], head_gain_grads[1]]
        )
    below = swap(pack_grads[0][None], 2, 0)
    pack_sums[0] = line_reduce(after((hidden_sums[0], pack_sums[1:]), below)[0])
    both = jnp.concatenate([low(result), low(grad)], axis=1)
    gain_stack = sum_line(jnp.stack(gain_grads).reshape(-1, head))
    both, gain_stack = lax.optimization_barrier((both, gain_stack))
    both = line_rows_back(both, below)
    gain_stack = sum_plane(gain_stack)
    hidden_grads[0] = swap(hidden_sums[0], 2, 1, below)
    both, hidden_grads[0] = lax.optimization_barrier((both, hidden_grads[0]))
    both = swap(both, 0, 0)
    result, token_grad = both[:, : tokens.shape[1]], wide(both[:, tokens.shape[1] :])
    kinds = wide(jnp.stack(hidden_grads, 1))
    hidden_stacks = (kinds[0].swapaxes(1, 2), kinds[1].swapaxes(1, 2), kinds[2])
    marks = (0, query_count, query_count + key_count, split, pack_sums[0].shape[1])
    kinds = [
        jnp.stack(
            [wide(v[:, low_mark:high_mark]).reshape(-1, v.shape[-1]) for v in pack_sums]
        )
        for low_mark, high_mark in zip(marks, marks[1:])
    ]
    weight_stacks = [v.swapaxes(1, 2) for v in kinds[:3]] + kinds[3:]
    width = attn_gain.shape[1]
    gain_stack = gain_stack.reshape(layers, -1)
    attn_sum, mlp_sum, query_sum, key_sum = (
        gain_stack[:, :width],
        gain_stack[:, width : 2 * width],
        gain_stack[:, 2 * width : 2 * width + head],
        gain_stack[:, 2 * width + head :],
    )
    return (
        result,
        token_grad,
        attn_sum,
        query_sum,
        key_sum,
        *weight_stacks,
        mlp_sum,
        *hidden_stacks,
    )


def plane_fits(mesh, shapes):
    size, line = mesh.shape["fsdp"], mesh.shape["tp"]
    heads = shapes[6].shape[2] // shapes[4].shape[1]
    return size == 8 and heads == size and size % line == 0 and shapes[1].shape[0] == size


def solution(mesh):
    placed = (
        P(("fsdp", "tp"), None),
        P("fsdp", None),
        P(),
        P(),
        P(),
        P(None, "fsdp", "tp"),
        P(None, "fsdp", "tp"),
        P(None, "fsdp", "tp"),
        P(None, "tp", "fsdp"),
        P(),
        P(None, "fsdp", "tp"),
        P(None, "fsdp", "tp"),
        P(None, "tp", "fsdp"),
        P(("fsdp", "tp"), None),
    )
    def mapped(plan):
      return jax.shard_map(
        plan,
        mesh=mesh,
        in_specs=placed,
        out_specs=(
            P(("fsdp", "tp"), None),
            P(("fsdp", "tp"), None),
            P(),
            P(),
            P(),
            P(None, "fsdp", "tp"),
            P(None, "fsdp", "tp"),
            P(None, "fsdp", "tp"),
            P(None, "tp", "fsdp"),
            P(),
            P(None, "fsdp", "tp"),
            P(None, "fsdp", "tp"),
            P(None, "tp", "fsdp"),
        ),
        check_vma=False,
    )

    def whole(*args):
        return mapped(plane_plan if plane_fits(mesh, args) else general_plan)(*args)

    return whole
```
